32 devices in a mesh: dp: 16 (over z, y, core), chan: 2 (over x).
Axes of the slice: x: 2, y: 2, z: 4, core: 2. Of those that a mesh axis runs over, the one named last changes fastest.
Arguments:
- features: bfloat16 [64, 384, 1024], P('dp', 'chan'), may hold values from -6 to 6
- pixel_masks: int32 [64, 1024], P('dp'), may hold values 0 or 1
- timesteps: int32 [64], P('dp'), may hold values from 0 to 999
- first_filter: float32 [9, 384, 384], P(None, 'dp', 'chan'), may hold values from -0.109375 to 0.109375
- second_filter: float32 [9, 384, 384], P(None, 'dp', 'chan'), may hold values from -0.109375 to 0.109375
- project_weight: float32 [384, 3, 384], P('dp', None, 'chan'), may hold values from -0.3125 to 0.3125
- output_weight: float32 [384, 384], P('chan', 'dp'), may hold values from -6 to 6
- embed_weight: float32 [2, 768, 384], P(None, 'dp', 'chan'), may hold values from -0.21875 to 0.21875
- norm_gains: float32 [3, 384], P(None, 'chan'), may hold values from 0.1 to 1.9
- norm_biases: float32 [3, 384], P(None, 'chan'), may hold values from -3 to 3
- cotangent: bfloat16 [64, 384, 1024], P('dp', 'chan'), may hold values from -6 to 6
Outputs:
- block_output: bfloat16 [64, 384, 1024], P('dp', 'chan')
- input_grad: float32 [64, 384, 1024], P('dp', 'chan')
- grad_first: float32 [9, 384, 384], P(None, 'dp', 'chan')
- grad_second: float32 [9, 384, 384], P(None, 'dp', 'chan')
- grad_project: float32 [384, 3, 384], P('dp', None, 'chan')
- grad_output: float32 [384, 384], P('chan', 'dp')
- grad_embed: float32 [2, 768, 384], P(None, 'dp', 'chan')
- grad_gains: float32 [3, 384], P(None, 'chan')
- grad_biases: float32 [3, 384], P(None, 'chan')
The draws below stay inside these ranges and needn't reach their ends.
All inputs are finite; a program needn't handle non-finite values. No bound on the sum of `pixel_masks` on one device may be relied on, other than what follows from the above.
Results may differ from the reference program's by a relative error of at most 0.017.
Values may be sent and summed in bfloat16 or wider, within the bound.
No kernel may reach another device: no remote copies, remote signals or barrier semaphores. Data moves between devices by JAX's collectives and lax.ppermute only.
A program may use at most 128 MiB of HBM per device.

```python
import math
import jax
import jax.numpy as jnp
from jax import lax

C = 384
HEAD = 64
HEADS = 6
GROUPS = 32
EMBED = 768
SIDE = 32
PIX = 1024
TIMES = 1000
IMAGES = 64


def plant(entries, rng, least, high):
    spot = [jax.random.randint(jax.random.fold_in(rng, axis), (), 0, length) for axis, length in enumerate(entries.shape)]
    longest = entries.shape.index(max(entries.shape))
    neighbour = spot[:longest] + [(spot[longest] + 1) % entries.shape[longest]] + spot[longest + 1:]
    return entries.at[tuple(spot)].set(least).at[tuple(neighbour)].set(high)


def raised(array, stream_key, source, target, blocks, factor):
    owner, partner = [(jnp.arange(array.shape[axis_at]) // (array.shape[axis_at] // blocks)).reshape([-1 if axis == axis_at else 1 for axis in range(array.ndim)]) for axis_at in (source, target)]
    chosen = jax.random.permutation(stream_key, blocks)[partner]
    strong = (owner == chosen) | (owner == (partner + blocks // 2) % blocks)
    return jnp.where(strong, factor * array, array)


def level_of(stream_key, shape, split, least, high):
    level, own = 1.0, jax.random.fold_in(stream_key, 6)
    for dim, parts in split:
        draws = jnp.exp(jax.random.uniform(jax.random.fold_in(own, dim), (parts,), jnp.float32, least / len(split), high / len(split)))
        level = level * jnp.repeat(draws, shape[dim] // parts).reshape([-1 if axis == dim else 1 for axis in range(len(shape))])
    return level


def bell_draw(own_key, dims, deviation, most, split=(), dtype=jnp.bfloat16):
    level = level_of(own_key, dims, split, -0.22, 0.18) if split else 1.0
    values = jax.random.normal(own_key, dims, jnp.float32) * deviation * level
    return jnp.minimum(jnp.maximum(values, -most), most).astype(dtype)


def gaussian_with(stream_key, dims, width, limit, split, heavy, dtype=jnp.bfloat16):
    entries = width * jax.random.normal(stream_key, dims, jnp.float32)
    if split:
        entries = entries * level_of(stream_key, dims, split, -0.22, 0.18)
    return jnp.clip(raised(entries, jax.random.fold_in(stream_key, 3), *heavy), -limit, limit).astype(dtype)


def setup_inputs(seed: int = 0) -> dict:
    key_list = jax.random.split(jax.random.key(seed), 12)
    features = gaussian_with(key_list[0], (IMAGES, C, PIX), 1.0, 6.0, ((0, 16), (1, 2)), (0, 1, 16, 2.0))
    pixel_masks = plant((jax.random.randint(key_list[1], (IMAGES, PIX), 0, 8) < 7).astype(jnp.int32), jax.random.fold_in(key_list[1], 1), 0, 1)
    timesteps = plant(jax.random.randint(key_list[2], (IMAGES,), 0, TIMES), jax.random.fold_in(key_list[2], 1), 0, TIMES - 1).astype(jnp.int32)
    first_filter = bell_draw(key_list[3], (9, C, C), (9 * C) ** -0.5, 0.109375, ((1, 16), (2, 2)), jnp.float32)
    second_filter = bell_draw(key_list[4], (9, C, C), (9 * C) ** -0.5, 0.109375, ((1, 16), (2, 2)), jnp.float32)
    project_weight = bell_draw(key_list[5], (C, 3, C), C ** -0.5, 0.3125, ((0, 16), (2, 2)), jnp.float32)
    output_weight = bell_draw(key_list[6], (C, C), 1 ** -0.5, 6.0, ((0, 2), (1, 16)), jnp.float32)
    embed_weight = bell_draw(key_list[7], (2, EMBED, C), EMBED ** -0.5, 0.21875, ((1, 16), (2, 2)), jnp.float32)
    norm_gains = jnp.clip(1.0 + 0.18 * jax.random.normal(key_list[8], (3, C), jnp.float32), 0.1, 1.9)
    norm_biases = bell_draw(key_list[9], (3, C), 0.5, 3.0, ((1, 2),), jnp.float32)
    cotangent = bell_draw(key_list[10], (IMAGES, C, PIX), 1.0, 6.0, ((0, 16), (1, 2)))
    return dict(features=features, pixel_masks=pixel_masks, timesteps=timesteps, first_filter=first_filter, second_filter=second_filter, project_weight=project_weight, output_weight=output_weight, embed_weight=embed_weight, norm_gains=norm_gains, norm_biases=norm_biases, cotangent=cotangent)


@jax.custom_vjp
def low(v):
    return lax.optimization_barrier(v.astype(jnp.bfloat16)).astype(jnp.float32)

@jax.custom_vjp
def low_back(v):
    return v

def low_keep(v):
    return (low(v), None)

def low_pass(kept, grad):
    return (grad,)

def back_keep(v):
    return (v, None)

def back_low(kept, grad):
    return (low(grad),)
low.defvjp(low_keep, low_pass)
low_back.defvjp(back_keep, back_low)
highest = lax.Precision.HIGHEST
epsilon = 1e-05
masked_penalty = 10000.0

def group_norm(feature, validity, gain, offset):
    pixels, channel_width = feature.shape
    grouped = feature.reshape(pixels, GROUPS, channel_width // GROUPS)
    weight = validity[:, None, None]
    divisor = jnp.maximum(jnp.sum(validity), 1.0) * (channel_width // GROUPS)
    group_mean = lax.optimization_barrier(jnp.sum(grouped * weight, axis=(0, 2))) / divisor
    centred = grouped - group_mean[None, :, None]
    variance = lax.optimization_barrier(jnp.sum(centred * centred * weight, axis=(0, 2))) / divisor
    normed = centred * lax.rsqrt(variance + epsilon)[None, :, None]
    return normed.reshape(pixels, channel_width) * gain + offset

def filter_image(feature, weight):
    grid_view = feature.reshape(SIDE, SIDE, feature.shape[1])
    padded = jnp.pad(grid_view, ((1, 1), (1, 1), (0, 0)))
    result = jnp.zeros((SIDE, SIDE, weight.shape[2]), jnp.float32)
    for down in range(3):
        for across in range(3):
            window = padded[down:down + SIDE, across:across + SIDE]
            result = result + jnp.einsum('hwc,cd->hwd', window, weight[3 * down + across], precision=highest)
    return result.reshape(SIDE * SIDE, weight.shape[2])

def time_features(timestep):
    half_width = EMBED // 2
    frequency = jnp.exp(-math.log(10000.0) * jnp.arange(half_width).astype(jnp.float32) / half_width)
    angles = timestep.astype(jnp.float32) * frequency
    return jax.nn.silu(jnp.concatenate([jnp.cos(angles), jnp.sin(angles)]))

def one_image(entry, filters, gains, offsets):
    image_in, validity, timestep = entry
    first_filter, second_filter, project_weight, output_weight, embed_weight = filters
    keep = validity[:, None]
    first_input = low(jax.nn.silu(group_norm(image_in, validity, gains[0], offsets[0])) * keep)
    first_conv = low_back(filter_image(first_input, first_filter))
    time_embed = time_features(timestep)
    modulation = jnp.einsum('e,ked->kd', time_embed, embed_weight, precision=highest)
    second_hidden = group_norm(first_conv, validity, gains[1], offsets[1]) * (1.0 + modulation[0]) + modulation[1]
    second_input = low(jax.nn.silu(second_hidden) * keep)
    residual = image_in + low_back(filter_image(second_input, second_filter))
    attend_input = low(group_norm(residual, validity, gains[2], offsets[2]))
    projected = low(low_back(jnp.einsum('pc,cjd->jpd', attend_input, project_weight, precision=highest)))
    split_heads = projected.reshape(3, SIDE * SIDE, HEADS, HEAD)
    score_scale = HEAD ** (-0.5)
    key_bias = (validity - 1.0) * masked_penalty
    products = jnp.einsum('qhd,khd->hqk', split_heads[0], split_heads[1], precision=highest)
    scores = low_back(products * score_scale + key_bias[None, None, :])
    probabilities = low(jax.nn.softmax(scores, axis=2))
    attended = low(low_back(jnp.einsum('hqk,khd->qhd', probabilities, split_heads[2], precision=highest)))
    mixed_heads = low_back(jnp.dot(attended.reshape(SIDE * SIDE, HEADS * HEAD), output_weight, precision=highest))
    return (residual + mixed_heads) * keep

def reference(features, pixel_masks, timesteps, first_filter, second_filter, project_weight, output_weight, embed_weight, norm_gains, norm_biases, cotangent):
    validity = pixel_masks.astype(jnp.float32)

    def forward(inputs, filter_one, filter_two, project, output, embedding, gains, offsets):
        filters = (low(filter_one), low(filter_two), low(project), low(output), low(embedding))

        def per_image(entry):
            return one_image(entry, filters, gains, offsets)
        pixel_major = jnp.transpose(inputs, (0, 2, 1))
        result = lax.map(jax.checkpoint(per_image), (pixel_major, validity, timesteps))
        return jnp.transpose(result, (0, 2, 1))
    result, pullback = jax.vjp(forward, features.astype(jnp.float32), first_filter, second_filter, project_weight, output_weight, embed_weight, norm_gains, norm_biases)
    gradients = pullback(cotangent.astype(jnp.float32))
    return (result.astype(jnp.bfloat16), gradients[0], gradients[1], gradients[2], gradients[3], gradients[4], gradients[5], gradients[6], gradients[7])
```

```python
import functools
import math

import jax
import jax.numpy as jnp
from jax import lax
from jax.experimental import pallas as pl
from jax.experimental.pallas import tpu as pltpu
from jax.sharding import PartitionSpec as P

C = 384
HALF = 192
HEAD = 64
GROUPS = 32
WIDTH = C // GROUPS
SIDE = 32
PIX = SIDE * SIDE
BLOCKS = 16
ROWS = C // BLOCKS
TAPS = 3 * C
EPSILON = 1e-05
QUERIES = 256
KEYDIM = 80
LOW = jnp.bfloat16
WIDE = jnp.float32
ORDER = (0, 8, 4, 12, 2, 10, 6, 14, 1, 9, 5, 13, 3, 11, 7, 15)

NN = (((1,), (0,)), ((), ()))
NT = (((1,), (1,)), ((), ()))
TN = (((0,), (0,)), ((), ()))


def dot(left, right, dims):
    return lax.dot_general(left, right, dims, preferred_element_type=WIDE)


def column_index(rows):
    return lax.broadcasted_iota(jnp.int32, (rows, PIX), 1)


def lane_pair(first, second):
    lane = lax.broadcasted_iota(jnp.int32, (C, 128), 1)
    return jnp.where(lane == 0, first, jnp.where(lane == 1, second, 0.0))


def group_sums(member, values):
    high = values.astype(LOW)
    rest = values - high.astype(WIDE)
    middle = rest.astype(LOW)
    low = (rest - middle.astype(WIDE)).astype(LOW)
    return dot(member, high, NN) + dot(member, middle, NN) + dot(member, low, NN)


def group_sum(member, column):
    return group_sums(member, jnp.broadcast_to(column, (C, 128)))[:, 0:1]


def group_stats(value_ref, member, mask, count):
    mean = group_sum(member, jnp.sum(value_ref[...] * mask, axis=1, keepdims=True)) / count
    centred = value_ref[...] - mean
    variance = (
        group_sum(member, jnp.sum(centred * centred * mask, axis=1, keepdims=True)) / count
    )
    return mean, lax.rsqrt(variance + EPSILON)


def silu(value):
    return value / (1.0 + jnp.exp(-value))


def silu_slope(value):
    squashed = 1.0 / (1.0 + jnp.exp(-value))
    return squashed * (1.0 + value * (1.0 - squashed))


def side_shifts(piece):
    column = column_index(piece.shape[0]) & (SIDE - 1)
    before = jnp.where(column == 0, 0.0, pltpu.roll(piece, 1, 1))
    after = jnp.where(column == SIDE - 1, 0.0, pltpu.roll(piece, PIX - 1, 1))
    return before, piece, after


def stack_pair(first, second):
    return jnp.concatenate(side_shifts(first) + side_shifts(second), axis=0).astype(LOW)


def shift_down(piece):
    return jnp.where(
        column_index(piece.shape[0]) < SIDE, 0.0, pltpu.roll(piece, SIDE, 1)
    )


def shift_up(piece):
    return jnp.where(
        column_index(piece.shape[0]) >= PIX - SIDE, 0.0, pltpu.roll(piece, PIX - SIDE, 1)
    )


def conv_out(product_ref, chan):
    base = chan * 3 * HALF
    return (
        product_ref[base + HALF : base + 2 * HALF, :]
        + shift_down(product_ref[base : base + HALF, :])
        + shift_up(product_ref[base + 2 * HALF : base + 3 * HALF, :])
    )


def stack_gradient(grad_ref, image, out_ref):
    for chan in range(2):
        piece = grad_ref[image, chan * HALF : (chan + 1) * HALF, :].astype(WIDE)
        base = chan * 3 * HALF
        out_ref[base : base + HALF, :] = shift_up(piece).astype(LOW)
        out_ref[base + HALF : base + 2 * HALF, :] = piece.astype(LOW)
        out_ref[base + 2 * HALF : base + 3 * HALF, :] = shift_down(piece).astype(LOW)


def block_offset(place_ref, position):
    return pl.multiple_of(place_ref[position], 8)


def back_to_channels(place_ref, product_ref, out_ref):
    for position in range(BLOCKS):
        base = position * 3 * ROWS
        first = product_ref[base : base + ROWS, :]
        middle = product_ref[base + ROWS : base + 2 * ROWS, :]
        last = product_ref[base + 2 * ROWS : base + 3 * ROWS, :]
        column = column_index(ROWS) & (SIDE - 1)
        total = (
            middle
            + jnp.where(column == SIDE - 1, 0.0, pltpu.roll(first, PIX - 1, 1))
            + jnp.where(column == 0, 0.0, pltpu.roll(last, 1, 1))
        )
        out_ref[pl.ds(block_offset(place_ref, position), ROWS), :] = total


def count_of(mask):
    return jnp.maximum(jnp.sum(mask, axis=1, keepdims=True), 1.0) * float(WIDTH)


def small_columns(columns):
    lane = lax.broadcasted_iota(jnp.int32, (C, 128), 1)
    result = jnp.zeros((C, 128), WIDE)
    for index, column in enumerate(columns):
        result = jnp.where(lane == index, column, result)
    return result


def first_kernel(
    place,
    mine,
    theirs,
    mask_ref,
    params,
    member,
    weight_a,
    weight_b,
    whole_out,
    input_out,
    normed_out,
    stats_out,
    weight,
    value,
    stack,
    product,
):
    @pl.when(pl.program_id(0) == 0)
    def _():
        weight[: TAPS // 2, :] = weight_a[...]
        weight[TAPS // 2 :, :] = weight_b[...]

    own = pl.multiple_of(place[BLOCKS] * HALF, HALF)
    other = pl.multiple_of((1 - place[BLOCKS]) * HALF, HALF)
    value[pl.ds(own, HALF), :] = mine[0].astype(WIDE)
    value[pl.ds(other, HALF), :] = theirs[0].astype(WIDE)
    mask = mask_ref[0]
    count = count_of(mask)
    whole_out[0] = value[...].astype(LOW)
    mean, factor = group_stats(value, member[...], mask, count)
    stats_out[0] = small_columns((mean, factor))
    scale = factor * params[:, 0:1]
    value[...] = (value[...] - mean) * scale + params[:, 1:2]
    for pair in range(BLOCKS // 2):
        pieces = []
        for part in range(2):
            hidden = value[pl.ds(block_offset(place, 2 * pair + part), ROWS), :]
            pieces.append((silu(hidden) * mask).astype(LOW).astype(WIDE))
        base = 2 * pair * ROWS
        input_out[0, base : base + 2 * ROWS, :] = jnp.concatenate(pieces, axis=0).astype(LOW)
        stack[3 * base : 3 * base + 6 * ROWS, :] = stack_pair(*pieces)
    product[...] = dot(weight[...], stack[...], TN)
    for chan in range(2):
        value[chan * HALF : (chan + 1) * HALF, :] = conv_out(product, chan)
    mean, factor = group_stats(value, member[...], mask, count)
    normed_out[0] = (value[...] - mean) * factor
    stats_out[0] = jnp.where(
        lax.broadcasted_iota(jnp.int32, (C, 128), 1) == 2, factor, stats_out[0]
    )


def second_kernel(
    place,
    normed,
    whole,
    embed_in,
    mask_ref,
    params,
    member,
    weight_a,
    weight_b,
    bundle,
    input_out,
    residual_out,
    attend_out,
    stats_out,
    weight,
    value,
    stack,
    product,
):
    @pl.when(pl.program_id(0) == 0)
    def _():
        weight[: TAPS // 2, :] = weight_a[...]
        weight[TAPS // 2 :, :] = weight_b[...]

    mask = mask_ref[0]
    count = count_of(mask)
    scales, shifts = [], []
    for chan in range(2):
        base = chan * 4 * C + 2 * C
        sums = dot(bundle[:, base : base + C], embed_in[0, :C, :], TN) + dot(
            bundle[:, base + C : base + 2 * C], embed_in[0, C:, :], TN
        )
        column = sums[:, 0:1] + sums[:, 1:2] + sums[:, 2:3]
        scales.append(column[:HALF])
        shifts.append(column[HALF:])
    time_scale = jnp.concatenate(scales, axis=0)
    time_shift = jnp.concatenate(shifts, axis=0)
    affine = normed[0] * params[:, 2:3] + params[:, 3:4]
    value[...] = affine * (1.0 + time_scale) + time_shift
    for pair in range(BLOCKS // 2):
        pieces = []
        for part in range(2):
            hidden = value[pl.ds(block_offset(place, 2 * pair + part), ROWS), :]
            pieces.append((silu(hidden) * mask).astype(LOW).astype(WIDE))
        base = 2 * pair * ROWS
        input_out[0, base : base + 2 * ROWS, :] = jnp.concatenate(pieces, axis=0).astype(LOW)
        stack[3 * base : 3 * base + 6 * ROWS, :] = stack_pair(*pieces)
    product[...] = dot(weight[...], stack[...], TN)
    for chan in range(2):
        rows = slice(chan * HALF, (chan + 1) * HALF)
        value[rows, :] = whole[0, rows, :].astype(WIDE) + conv_out(product, chan)
    residual_out[0] = value[...]
    mean, factor = group_stats(value, member[...], mask, count)
    scale = factor * params[:, 4:5]
    attend_out[0] = ((value[...] - mean) * scale + params[:, 5:6]).astype(LOW)
    stats_out[0] = small_columns((mean, factor, time_scale, time_shift))


def attend_kernel(
    place,
    attend_in,
    residual,
    stats,
    mine,
    theirs,
    mask_ref,
    params,
    member,
    bundle,
    block_out,
    send_out,
    residual_grad_out,
    second_grad_out,
    keep_grads,
    send_grads,
    small_out,
    weight_f,
    project,
    output,
    gradient,
    projected,
    attend_grad,
    attended,
    projected_grad,
    keys_t,
    values_t,
    query_aug,
    probs,
    score_grads,
    accumulated,
    value,
):
    image = pl.program_id(0)

    @pl.when(image == 0)
    def _():
        for chan in range(2):
            for pair in range(BLOCKS // 2):
                block = bundle[
                    2 * pair * ROWS : 2 * (pair + 1) * ROWS, chan * 4 * C : chan * 4 * C + 2 * C
                ].astype(WIDE)
                for part in range(2):
                    weight_f[chan, pl.ds(block_offset(place, 2 * pair + part), ROWS), :] = block[
                        part * ROWS : (part + 1) * ROWS
                    ]
        project[...] = jnp.concatenate(
            [weight_f[0, :, : 3 * HALF], weight_f[1, :, : 3 * HALF]], axis=1
        ).astype(LOW)
        output[...] = jnp.concatenate(
            [weight_f[0, :, 3 * HALF :], weight_f[1, :, 3 * HALF :]], axis=1
        ).astype(LOW)
        accumulated[...] = jnp.zeros_like(accumulated)

    own = pl.multiple_of(place[BLOCKS] * HALF, HALF)
    other = pl.multiple_of((1 - place[BLOCKS]) * HALF, HALF)
    mask = mask_ref[0]
    count = count_of(mask)
    gradient[pl.ds(own, HALF), :] = (mine[0].astype(WIDE) * mask).astype(LOW)
    gradient[pl.ds(other, HALF), :] = (theirs[0].astype(WIDE) * mask).astype(LOW)
    projected[...] = dot(project[...], attend_in[0], TN).astype(LOW)
    attend_grad[...] = dot(output[...], gradient[...], TN).astype(LOW)

    row = lax.broadcasted_iota(jnp.int32, (KEYDIM - HEAD, PIX), 0)
    penalty = mask - 1.0
    bias_rows = jnp.where(
        row == 0, penalty * 9984.0, jnp.where(row == 1, penalty * 16.0, 0.0)
    ).astype(LOW)
    ones_rows = jnp.where(row < 2, 1.0, 0.0).astype(LOW)
    query_aug[HEAD:, :] = ones_rows

    def one_head(head, carry):
        chan = head // 3
        row_q = pl.multiple_of(chan * (3 * HALF) + (head - 3 * chan) * HEAD, HEAD)
        row_k = pl.multiple_of(row_q + HALF, HEAD)
        row_v = pl.multiple_of(row_q + 2 * HALF, HEAD)
        row_o = pl.multiple_of(head * HEAD, HEAD)
        queries = projected[pl.ds(row_q, HEAD), :]
        keys = projected[pl.ds(row_k, HEAD), :]
        values = projected[pl.ds(row_v, HEAD), :]
        grads = attend_grad[pl.ds(row_o, HEAD), :]
        keys_t[...] = jnp.concatenate([keys, bias_rows], axis=0).T
        values_t[...] = values.T
        query_aug[:HEAD, :] = (queries.astype(WIDE) * HEAD**-0.5).astype(LOW)
        for step in range(PIX // QUERIES):
            span = slice(step * QUERIES, (step + 1) * QUERIES)
            scores = dot(keys_t[...], query_aug[:, span], NN)
            exponents = jnp.exp(scores - jnp.max(scores, axis=0, keepdims=True))
            chances = exponents * (1.0 / jnp.sum(exponents, axis=0, keepdims=True))
            low_chances = chances.astype(LOW)
            probs[:, span] = low_chances
            prob_grad = dot(values_t[...], grads[:, span], NN)
            result = dot(values, low_chances, NN)
            attended[pl.ds(row_o, HEAD), span] = result.astype(LOW)
            delta = jnp.sum(grads[:, span].astype(WIDE) * result, axis=0, keepdims=True)
            score_grad = (chances * (prob_grad - delta)).astype(LOW)
            score_grads[:, span] = score_grad
            projected_grad[pl.ds(row_q, HEAD), span] = (
                dot(keys, score_grad, NN) * HEAD**-0.5
            ).astype(LOW)
        projected_grad[pl.ds(row_k, HEAD), :] = (
            dot(queries, score_grads[...], NT) * HEAD**-0.5
        ).astype(LOW)
        projected_grad[pl.ds(row_v, HEAD), :] = dot(grads, probs[...], NT).astype(LOW)
        return carry

    lax.fori_loop(0, C // HEAD, one_head, 0)

    value[...] = (residual[0] + dot(output[...], attended[...], NN)) * mask
    block_out[0] = value[pl.ds(own, HALF), :].astype(LOW)
    send_out[0] = value[pl.ds(other, HALF), :].astype(LOW)
    accumulated[:, TAPS:] += dot(gradient[...], attended[...], NT)
    accumulated[:, :TAPS] += dot(attend_in[0], projected_grad[...], NT)
    third = dot(project[...], projected_grad[...], NN)
    mean, factor = stats[0, :, 0:1], stats[0, :, 1:2]
    normed = (residual[0] - mean) * factor
    bias_third = jnp.sum(third, axis=1, keepdims=True)
    gain_third = jnp.sum(third * normed, axis=1, keepdims=True)
    gain = params[:, 4:5]
    sums = group_sums(member[...], lane_pair(gain * bias_third, gain * gain_third))
    first_sum, second_sum = sums[:, 0:1] / count, sums[:, 1:2] / count
    total = gradient[...].astype(WIDE) + factor * (
        third * gain - mask * (first_sum + normed * second_sum)
    )
    residual_grad_out[0] = total
    second_grad_out[0] = total.astype(LOW)
    small_out[0] = small_columns((gain_third, bias_third))

    @pl.when(image == pl.num_programs(0) - 1)
    def _():
        for position in range(BLOCKS // 2):
            base = position * ROWS
            keep_grads[base : base + ROWS, :] = accumulated[
                pl.ds(block_offset(place, position), ROWS), :
            ]
        for pair in range(BLOCKS // 4):
            base = 2 * pair * ROWS
            send_grads[base : base + 2 * ROWS, :] = jnp.concatenate(
                [
                    accumulated[
                        pl.ds(block_offset(place, BLOCKS // 2 + 2 * pair + part), ROWS), :
                    ]
                    for part in range(2)
                ],
                axis=0,
            ).astype(LOW)


def filter_kernel(inputs, grads, keep_out, send_out, stack, grad_stack):
    images = inputs.shape[0]
    for image in range(images):
        span = slice(image * PIX, (image + 1) * PIX)
        for pair in range(BLOCKS // 2):
            base = 2 * pair * ROWS
            both = inputs[image, base : base + 2 * ROWS, :].astype(WIDE)
            stack[3 * base : 3 * base + 6 * ROWS, span] = stack_pair(both[:ROWS], both[ROWS:])
        stack_gradient(grads, image, grad_stack.at[:, span])
    middle = TAPS // 2
    send_out[...] = dot(stack[middle:, :], grad_stack[...], NT).astype(LOW)
    keep_out[...] = dot(stack[:middle, :], grad_stack[...], NT)


def conv_back(place, grads, weight_a, weight_b, grad_stack, product, value):
    stack_gradient(grads, 0, grad_stack)
    middle = TAPS // 2
    product[:middle, :] = dot(weight_a[...], grad_stack[...], NN)
    product[middle:, :] = dot(weight_b[...], grad_stack[...], NN)
    back_to_channels(place, product, value)


def second_back_kernel(
    place,
    grads,
    weight_a,
    weight_b,
    normed_ref,
    stats_first,
    stats,
    mask_ref,
    params,
    member,
    first_grad_out,
    small_out,
    grad_stack,
    product,
    value,
):
    conv_back(place, grads, weight_a, weight_b, grad_stack, product, value)
    mask = mask_ref[0]
    count = count_of(mask)
    gain, bias = params[:, 2:3], params[:, 3:4]
    factor = stats_first[0, :, 2:3]
    time_scale, time_shift = 1.0 + stats[0, :, 2:3], stats[0, :, 3:4]
    normed = normed_ref[0]
    hidden = (normed * gain + bias) * time_scale + time_shift
    delta = value[...] * mask * silu_slope(hidden)
    value[...] = delta
    plain = jnp.sum(delta, axis=1, keepdims=True)
    weighted = jnp.sum(delta * normed, axis=1, keepdims=True)
    scaled = gain * time_scale
    sums = group_sums(member[...], lane_pair(scaled * plain, scaled * weighted))
    first_sum, second_sum = sums[:, 0:1] / count, sums[:, 1:2] / count
    first_grad_out[0] = (
        factor * (value[...] * scaled - mask * (first_sum + normed * second_sum))
    ).astype(LOW)
    small_out[0] = small_columns(
        (
            gain * weighted + bias * plain,
            plain,
            time_scale * weighted,
            time_scale * plain,
        )
    )


def first_back_kernel(
    place,
    grads,
    weight_a,
    weight_b,
    whole,
    stats_first,
    residual_grad,
    mask_ref,
    params,
    member,
    keep_out,
    send_out,
    small_out,
    grad_stack,
    product,
    value,
):
    conv_back(place, grads, weight_a, weight_b, grad_stack, product, value)
    own = pl.multiple_of(place[BLOCKS] * HALF, HALF)
    other = pl.multiple_of((1 - place[BLOCKS]) * HALF, HALF)
    mask = mask_ref[0]
    count = count_of(mask)
    gain, bias = params[:, 0:1], params[:, 1:2]
    mean, factor = stats_first[0, :, 0:1], stats_first[0, :, 1:2]
    normed = (whole[0].astype(WIDE) - mean) * factor
    hidden = normed * gain + bias
    delta = value[...] * mask * silu_slope(hidden)
    value[...] = delta
    plain = jnp.sum(delta, axis=1, keepdims=True)
    weighted = jnp.sum(delta * normed, axis=1, keepdims=True)
    sums = group_sums(member[...], lane_pair(gain * plain, gain * weighted))
    first_sum, second_sum = sums[:, 0:1] / count, sums[:, 1:2] / count
    value[...] = residual_grad[0] + factor * (
        value[...] * gain - mask * (first_sum + normed * second_sum)
    )
    keep_out[0] = value[pl.ds(own, HALF), :]
    send_out[0] = value[pl.ds(other, HALF), :].astype(LOW)
    small_out[0] = small_columns((weighted, plain))


def shape(*sizes, dtype=WIDE):
    return jax.ShapeDtypeStruct(sizes, dtype)


def per_image(*sizes):
    return pl.BlockSpec((1,) + sizes, lambda g, place: (g,) + (0,) * len(sizes))


def own_image(*sizes):
    return pl.BlockSpec(
        (1,) + sizes, lambda g, place: (place[BLOCKS + 1] + g,) + (0,) * len(sizes)
    )


def fixed(*sizes):
    return pl.BlockSpec(sizes, lambda g, place: (0,) * len(sizes))


def run(kernel, place, images, ins, outs, scratch, flops, moved):
    return pl.pallas_call(
        kernel,
        grid_spec=pltpu.PrefetchScalarGridSpec(
            num_scalar_prefetch=1,
            grid=(images,),
            in_specs=[spec for _, spec in ins],
            out_specs=[spec for _, spec in outs],
            scratch_shapes=scratch,
        ),
        out_shape=[out for out, _ in outs],
        compiler_params=pltpu.CompilerParams(
            dimension_semantics=("arbitrary",), vmem_limit_bytes=60 * 2**20
        ),
        cost_estimate=pl.CostEstimate(flops=flops, bytes_accessed=moved, transcendentals=0),
    )(place, *[array for array, _ in ins])


def filter_gradient(inputs, grads):
    images = inputs.shape[0]
    return pl.pallas_call(
        filter_kernel,
        out_shape=[shape(TAPS // 2, TAPS), shape(TAPS // 2, TAPS, dtype=LOW)],
        scratch_shapes=[
            pltpu.VMEM((TAPS, images * PIX), LOW),
            pltpu.VMEM((TAPS, images * PIX), LOW),
        ],
        compiler_params=pltpu.CompilerParams(vmem_limit_bytes=60 * 2**20),
        cost_estimate=pl.CostEstimate(
            flops=2 * images * PIX * TAPS * TAPS, bytes_accessed=8 * 2**20, transcendentals=0
        ),
    )(inputs, grads)


def on_device(
    dp,
    features,
    pixel_masks,
    timesteps,
    first_filter,
    second_filter,
    project_weight,
    output_weight,
    embed_weight,
    norm_gains,
    norm_biases,
    cotangent,
):
    chan = lax.axis_index("chan")
    left = chan == 0
    span = dp // BLOCKS
    groups = [list(range(k * span, (k + 1) * span)) for k in range(BLOCKS)]
    block = lax.axis_index("dp") // span
    images = features.shape[0] // 2

    def swap(value, mask, flip):
        pairs = [
            (2 * d + x, 2 * (d ^ (mask * span)) + (x ^ flip)) for d in range(dp) for x in range(2)
        ]
        return lax.ppermute(value, ("dp", "chan"), pairs)

    def near(value, axis):
        if span == 1:
            return value
        return lax.all_gather(value, "dp", axis=axis, tiled=True, axis_index_groups=groups)

    def halves(mine, theirs, axis):
        return jnp.concatenate(
            [jnp.where(left, mine, theirs), jnp.where(left, theirs, mine)], axis=axis
        )

    def gather(shard):
        side = swap(shard, 0, 1)
        far = swap(shard, 8, 0)
        both = swap(shard, 8, 1)
        rows = jnp.concatenate([halves(shard, side, 1), halves(far, both, 1)], axis=0)
        rows = jnp.concatenate(
            [rows, swap(rows, 4, 0), swap(rows, 2, 0), swap(rows, 6, 0)], axis=0
        )
        return rows, swap(rows, 1, 0)

    def scatter(keep, send, pick):
        total = keep + swap(send, 1, 0).astype(WIDE)
        rows = total.shape[0] // 4
        parts = [total[k * rows : (k + 1) * rows] for k in range(4)]
        sent = [swap(parts[k].astype(LOW), m, 0) for k, m in ((1, 4), (2, 2), (3, 6))]
        total = parts[0] + sent[0].astype(WIDE) + sent[1].astype(WIDE) + sent[2].astype(WIDE)
        rows = rows // 2
        near_rows, far_rows = total[:rows], total[rows:]

        def both(value):
            one, two = pick(value, 0), pick(value, 1)
            return jnp.where(left, one, two), jnp.where(left, two, one)

        mine, side = both(near_rows)
        far, corner = both(far_rows)
        side = swap(side.astype(LOW), 0, 1)
        far = swap(far.astype(LOW), 8, 0)
        corner = swap(corner.astype(LOW), 8, 1)
        return mine + side.astype(WIDE) + far.astype(WIDE) + corner.astype(WIDE)

    def share(value, dimension):
        if span == 1:
            return value
        return lax.psum_scatter(
            value, "dp", scatter_dimension=dimension, tiled=True, axis_index_groups=groups
        )

    def filter_rows(weight):
        rows = near(weight.astype(LOW), 1).reshape(3, 3, ROWS, HALF)
        return jnp.transpose(rows, (1, 2, 0, 3)).reshape(3 * ROWS, 3 * HALF)

    embed_rows = jnp.transpose(near(embed_weight.astype(LOW), 1), (1, 0, 2))
    embed_rows = embed_rows.reshape(2, ROWS, 2 * HALF)
    bundle_rows = jnp.concatenate(
        [
            near(project_weight.astype(LOW), 0).reshape(ROWS, 3 * HALF),
            near(output_weight.astype(LOW), 1).T,
            embed_rows[0],
            embed_rows[1],
        ],
        axis=1,
    )

    own_start, other_start = chan * images, (1 - chan) * images
    theirs = swap(lax.dynamic_slice_in_dim(features, other_start, images, 0), 0, 1)
    first_a, first_b = gather(filter_rows(first_filter))
    norms = jnp.concatenate([norm_gains, norm_biases], axis=0)
    norms = halves(norms, swap(norms, 0, 1), 1)
    params = jnp.stack([norms[0], norms[3], norms[1], norms[4], norms[2], norms[5]], axis=1)
    params = jnp.pad(params, ((0, 0), (0, 2)))
    second_a, second_b = gather(filter_rows(second_filter))
    bundle_a, bundle_b = gather(bundle_rows)
    their_cots = swap(lax.dynamic_slice_in_dim(cotangent, other_start, images, 0), 0, 1)

    validity = lax.dynamic_slice_in_dim(pixel_masks, own_start, images, 0).astype(WIDE)
    validity = validity.reshape(images, 1, PIX)
    member = (jnp.arange(C)[:, None] // WIDTH == jnp.arange(C)[None, :] // WIDTH).astype(LOW)
    order = jnp.array(ORDER, jnp.int32)
    place = jnp.concatenate(
        [
            jnp.bitwise_xor(block, order) * ROWS,
            jnp.stack([chan, own_start]).astype(jnp.int32),
        ]
    )

    def time_features(steps, index, embed_width):
        half_width = embed_width // 2
        power = jnp.where(index < half_width, index, index - half_width).astype(WIDE)
        frequency = jnp.exp(-math.log(10000.0) * power / half_width)
        angles = steps[:, None] * frequency[None, :]
        return jax.nn.silu(
            jnp.where(index[None, :] < half_width, jnp.cos(angles), jnp.sin(angles))
        )

    embed_width = embed_weight.shape[1] * dp
    own_steps = lax.dynamic_slice_in_dim(timesteps, own_start, images, 0).astype(WIDE)
    low_index = (jnp.bitwise_xor(block, order)[:, None] * (2 * ROWS) + jnp.arange(ROWS)).reshape(-1)
    embed_index = jnp.concatenate([low_index, low_index + ROWS])
    embed_values = time_features(own_steps, embed_index, embed_width)
    embed_high = embed_values.astype(LOW)
    embed_rest = embed_values - embed_high.astype(WIDE)
    embed_middle = embed_rest.astype(LOW)
    embed_low = (embed_rest - embed_middle.astype(WIDE)).astype(LOW)
    embed_parts = jnp.pad(
        jnp.stack([embed_high, embed_middle, embed_low], axis=2), ((0, 0), (0, 0), (0, 125))
    )

    conv_flops = 2 * images * PIX * TAPS * TAPS
    conv_weights = [pltpu.VMEM((TAPS, TAPS), LOW)]
    conv_scratch = [
        pltpu.VMEM((C, PIX), WIDE),
        pltpu.VMEM((TAPS, PIX), LOW),
        pltpu.VMEM((TAPS, PIX), WIDE),
    ]
    back_scratch = [
        pltpu.VMEM((TAPS, PIX), LOW),
        pltpu.VMEM((TAPS, PIX), WIDE),
        pltpu.VMEM((C, PIX), WIDE),
    ]
    mask_in = (validity, per_image(1, PIX))
    params_in = (params, fixed(C, 8))
    member_in = (member, fixed(C, C))
    image_low = (shape(images, C, PIX, dtype=LOW), per_image(C, PIX))
    image_wide = (shape(images, C, PIX), per_image(C, PIX))
    image_small = (shape(images, C, 128), per_image(C, 128))
    half_filter = fixed(TAPS // 2, TAPS)

    whole, first_input, second_normed, stats_first = run(
        first_kernel,
        place,
        images,
        [
            (features, own_image(HALF, PIX)),
            (theirs, per_image(HALF, PIX)),
            mask_in,
            params_in,
            member_in,
            (first_a, half_filter),
            (first_b, half_filter),
        ],
        [image_low, image_low, image_wide, image_small],
        conv_weights + conv_scratch,
        conv_flops,
        12 * 2**20,
    )
    bundle = jnp.concatenate([bundle_a, bundle_b], axis=0)
    second_input, residual, attend_input, stats_second = run(
        second_kernel,
        place,
        images,
        [
            (second_normed, per_image(C, PIX)),
            (whole, per_image(C, PIX)),
            (embed_parts, per_image(2 * C, 128)),
            mask_in,
            params_in,
            member_in,
            (second_a, half_filter),
            (second_b, half_filter),
            (bundle, fixed(C, 8 * C)),
        ],
        [image_low, image_wide, image_low, image_small],
        conv_weights + conv_scratch,
        conv_flops,
        16 * 2**20,
    )
    width = 4 * C
    block_keep, block_send, residual_grad, second_grad, keep_grads, send_grads, small_third = run(
        attend_kernel,
        place,
        images,
        [
            (attend_input, per_image(C, PIX)),
            (residual, per_image(C, PIX)),
            (stats_second, per_image(C, 128)),
            (cotangent, own_image(HALF, PIX)),
            (their_cots, per_image(HALF, PIX)),
            mask_in,
            params_in,
            member_in,
            (bundle, fixed(C, 8 * C)),
        ],
        [
            (shape(2 * images, HALF, PIX, dtype=LOW), own_image(HALF, PIX)),
            (shape(images, HALF, PIX, dtype=LOW), per_image(HALF, PIX)),
            image_wide,
            image_low,
            (shape(C // 2, width), fixed(C // 2, width)),
            (shape(C // 2, width, dtype=LOW), fixed(C // 2, width)),
            image_small,
        ],
        [
            pltpu.VMEM((2, C, 2 * C), WIDE),
            pltpu.VMEM((C, TAPS), LOW),
            pltpu.VMEM((C, C), LOW),
            pltpu.VMEM((C, PIX), LOW),
            pltpu.VMEM((TAPS, PIX), LOW),
            pltpu.VMEM((C, PIX), LOW),
            pltpu.VMEM((C, PIX), LOW),
            pltpu.VMEM((TAPS, PIX), LOW),
            pltpu.VMEM((PIX, KEYDIM), LOW),
            pltpu.VMEM((PIX, HEAD), LOW),
            pltpu.VMEM((KEYDIM, PIX), LOW),
            pltpu.VMEM((PIX, PIX), LOW),
            pltpu.VMEM((PIX, PIX), LOW),
            pltpu.VMEM((C, width), WIDE),
            pltpu.VMEM((C, PIX), WIDE),
        ],
        8 * conv_flops,
        24 * 2**20,
    )
    block_theirs = swap(block_send, 0, 1)
    keep_second, send_second = filter_gradient(second_input, second_grad)
    first_grad, small_second = run(
        second_back_kernel,
        place,
        images,
        [
            (second_grad, per_image(C, PIX)),
            (second_a, half_filter),
            (second_b, half_filter),
            (second_normed, per_image(C, PIX)),
            (stats_first, per_image(C, 128)),
            (stats_second, per_image(C, 128)),
            mask_in,
            params_in,
            member_in,
        ],
        [image_low, image_small],
        back_scratch,
        conv_flops,
        12 * 2**20,
    )
    keep_first, send_first = filter_gradient(first_input, first_grad)
    input_keep, input_send, small_first = run(
        first_back_kernel,
        place,
        images,
        [
            (first_grad, per_image(C, PIX)),
            (first_a, half_filter),
            (first_b, half_filter),
            (whole, per_image(C, PIX)),
            (stats_first, per_image(C, 128)),
            (residual_grad, per_image(C, PIX)),
            mask_in,
            params_in,
            member_in,
        ],
        [
            (shape(2 * images, HALF, PIX), own_image(HALF, PIX)),
            (shape(images, HALF, PIX, dtype=LOW), per_image(HALF, PIX)),
            image_small,
        ],
        back_scratch,
        conv_flops,
        16 * 2**20,
    )
    input_theirs = swap(input_send, 0, 1)

    masked_out = lax.dynamic_update_slice_in_dim(block_keep, block_theirs, other_start, 0)
    input_grad = lax.dynamic_update_slice_in_dim(
        input_keep, input_theirs.astype(WIDE), other_start, 0
    )

    def pick_mixed(value, half):
        return jnp.concatenate(
            [
                value[:, half * 3 * HALF : (half + 1) * 3 * HALF],
                value[:, TAPS + half * HALF : TAPS + (half + 1) * HALF],
            ],
            axis=1,
        )

    def pick_filter(value, half):
        return value[:, half * 3 * HALF : (half + 1) * 3 * HALF]

    def filter_shape(rows):
        rows = jnp.transpose(rows.reshape(3, ROWS, 3, HALF), (2, 0, 1, 3))
        return share(rows.reshape(9, ROWS, HALF), 1)

    mixed = scatter(keep_grads, send_grads, pick_mixed)
    grad_project = share(mixed[:, : 3 * HALF].reshape(ROWS, 3, HALF), 0)
    grad_output = share(mixed[:, 3 * HALF :].T, 1)
    grad_second = filter_shape(scatter(keep_second, send_second, pick_filter))
    grad_first = filter_shape(scatter(keep_first, send_first, pick_filter))

    sums = jnp.stack(
        [
            jnp.sum(small[:, :, lane], axis=0)
            for small, lane in (
                (small_first, 0),
                (small_second, 2),
                (small_third, 0),
                (small_first, 1),
                (small_second, 3),
                (small_third, 1),
            )
        ],
        axis=0,
    )
    steps = jnp.pad(own_steps, (0, HALF - images))
    entry = jnp.concatenate(
        [
            jnp.transpose(small_second[:, :, :2], (2, 0, 1)).reshape(2 * images, C),
            jnp.concatenate([steps, steps])[None, :],
        ],
        axis=0,
    )

    def merge(values):
        return sum(v[:6] for v in values), [v[6:] for v in values]

    def spread(total, entries, masks, cut):
        message = jnp.concatenate([total] + entries, axis=0)
        if cut:
            one, two = message[:, :HALF], message[:, HALF:]
            own, away = jnp.where(left, one, two), jnp.where(left, two, one)
        else:
            own = away = message
        arrived = [own] + [swap(away if flip else own, m, flip) for m, flip in masks]
        return merge(arrived)

    total, entries = spread(sums, [entry], ((1, 0),), False)
    total, entries = spread(total, entries, ((4, 0), (2, 0), (6, 0)), False)
    total, entries = spread(total, entries, ((0, 1), (8, 0), (8, 1)), True)
    entries = jnp.concatenate(entries, axis=0)
    if span > 1:
        total = lax.psum(total, "dp", axis_index_groups=groups)
        entries = lax.all_gather(entries, "dp", axis=0, tiled=True, axis_index_groups=groups)
    entries = entries.reshape(-1, 2 * images + 1, HALF)
    all_steps = entries[:, 2 * images, :images].reshape(-1)
    scale_grads = entries[:, :images].reshape(-1, HALF)
    shift_grads = entries[:, images : 2 * images].reshape(-1, HALF)
    rows = embed_weight.shape[1]
    row_index = lax.axis_index("dp") * rows + jnp.arange(rows)
    all_embed = time_features(all_steps, row_index, embed_width)
    grad_embed = jnp.einsum(
        "be,kbd->ked",
        all_embed,
        jnp.stack([scale_grads, shift_grads]),
        precision=lax.Precision.HIGHEST,
    )
    return (
        masked_out,
        input_grad,
        grad_first,
        grad_second,
        grad_project,
        grad_output,
        grad_embed,
        total[:3],
        total[3:],
    )


def solution(mesh):
    in_specs = (
        P("dp", "chan", None),
        P("dp", None),
        P("dp"),
        P(None, "dp", "chan"),
        P(None, "dp", "chan"),
        P("dp", None, "chan"),
        P("chan", "dp"),
        P(None, "dp", "chan"),
        P(None, "chan"),
        P(None, "chan"),
        P("dp", "chan", None),
    )
    out_specs = (
        P("dp", "chan", None),
        P("dp", "chan", None),
        P(None, "dp", "chan"),
        P(None, "dp", "chan"),
        P("dp", None, "chan"),
        P("chan", "dp"),
        P(None, "dp", "chan"),
        P(None, "chan"),
        P(None, "chan"),
    )
    return jax.shard_map(
        functools.partial(on_device, mesh.shape["dp"]),
        mesh=mesh,
        in_specs=in_specs,
        out_specs=out_specs,
        check_vma=False,
    )
```

```python
import functools
import math

import jax
import jax.numpy as jnp
from jax import lax
from jax.experimental import pallas as pl
from jax.experimental.pallas import tpu as pltpu
from jax.sharding import PartitionSpec as P

C = 384
HALF = 192
HEAD = 64
GROUPS = 32
WIDTH = C // GROUPS
SIDE = 32
PIX = SIDE * SIDE
BLOCKS = 16
ROWS = C // BLOCKS
TAPS = 3 * C
EPSILON = 1e-05
MIXED = 8 * HALF
PAIR = 2 * ROWS
PIECE = 3 * PAIR
JOINT = PIECE + PAIR + PAIR // 3
PAIRS = BLOCKS // 2
KEYS = 128
CHUNK = 256
LOW = jnp.bfloat16
WIDE = jnp.float32
ORDER = (0, 8, 4, 12, 2, 10, 6, 14, 1, 9, 5, 13, 3, 11, 7, 15)

NN = (((1,), (0,)), ((), ()))
NT = (((1,), (1,)), ((), ()))
TN = (((0,), (0,)), ((), ()))


def dot(left, right, dims):
    return lax.dot_general(left, right, dims, preferred_element_type=WIDE)


def pixel_row(keep):
    pixel = lax.broadcasted_iota(jnp.int32, (1, PIX), 1)
    return jnp.where(keep(pixel), 1.0, 0.0).astype(LOW)


def lane_pair(first, second):
    lane = lax.broadcasted_iota(jnp.int32, (C, 128), 1)
    return jnp.where(lane == 0, first, jnp.where(lane == 1, second, 0.0))


def group_sums(member, values):
    high = values.astype(LOW)
    rest = values - high.astype(WIDE)
    middle = rest.astype(LOW)
    low = (rest - middle.astype(WIDE)).astype(LOW)
    return dot(member, high, NN) + dot(member, middle, NN) + dot(member, low, NN)


def group_sum(member, column):
    return group_sums(member, jnp.broadcast_to(column, (C, 128)))[:, 0:1]


def group_stats(value_ref, member, mask, count):
    mean = group_sum(member, jnp.sum(value_ref[...] * mask, axis=1, keepdims=True)) / count
    centred = value_ref[...] - mean
    variance = (
        group_sum(member, jnp.sum(centred * centred * mask, axis=1, keepdims=True)) / count
    )
    return mean, lax.rsqrt(variance + EPSILON)


def silu(value):
    return value / (1.0 + jnp.exp(-value))


def silu_slope(value):
    squashed = 1.0 / (1.0 + jnp.exp(-value))
    return squashed * (1.0 + value * (1.0 - squashed))


def shift_down(piece):
    pixel = lax.broadcasted_iota(jnp.int32, piece.shape, 1)
    return jnp.where(pixel < SIDE, 0.0, pltpu.roll(piece, SIDE, 1))


def shift_up(piece):
    pixel = lax.broadcasted_iota(jnp.int32, piece.shape, 1)
    return jnp.where(pixel >= PIX - SIDE, 0.0, pltpu.roll(piece, PIX - SIDE, 1))


def conv_out(product_ref, chan):
    base = chan * 3 * HALF
    return (
        product_ref[base + HALF : base + 2 * HALF, :]
        + shift_down(product_ref[base : base + HALF, :])
        + shift_up(product_ref[base + 2 * HALF : base + 3 * HALF, :])
    )


def stack_gradient(grad_ref, out_ref):
    not_top = pixel_row(lambda pixel: pixel >= SIDE)
    not_bottom = pixel_row(lambda pixel: pixel < PIX - SIDE)
    for chan in range(2):
        piece = grad_ref[chan * HALF : (chan + 1) * HALF, :]
        base = chan * 3 * HALF
        out_ref[base : base + HALF, :] = pltpu.roll(piece, PIX - SIDE, 1) * not_bottom
        out_ref[base + HALF : base + 2 * HALF, :] = piece
        out_ref[base + 2 * HALF : base + 3 * HALF, :] = pltpu.roll(piece, SIDE, 1) * not_top


def stack_gradients(grads, out_ref):
    at = 0
    for ref in grads:
        for image in range(ref.shape[0]):
            stack_gradient(ref.at[image], out_ref.at[:, at * PIX : (at + 1) * PIX])
            at += 1


def block_offset(place_ref, position):
    return pl.multiple_of(place_ref[position], 8)


def pair_rows(place, ref, pair):
    return jnp.concatenate(
        [ref[pl.ds(block_offset(place, 2 * pair + part), ROWS), :] for part in range(2)], axis=0
    )


def build_stack(place, value, mask, stacks):
    not_left = pixel_row(lambda pixel: pixel % SIDE != 0)
    not_right = pixel_row(lambda pixel: pixel % SIDE != SIDE - 1)
    for pair in range(PAIRS):
        piece = (silu(pair_rows(place, value, pair)) * mask).astype(LOW)
        stack = stacks[pair // (PAIRS // 2)]
        base = pair % (PAIRS // 2) * PIECE
        stack[base : base + PAIR, :] = pltpu.roll(piece, 1, 1) * not_left
        stack[base + PAIR : base + 2 * PAIR, :] = piece
        stack[base + 2 * PAIR : base + 3 * PAIR, :] = pltpu.roll(piece, PIX - 1, 1) * not_right


def back_to_channels(place_ref, product_ref, out_ref):
    column = lax.broadcasted_iota(jnp.int32, (PAIR, PIX), 1) & (SIDE - 1)
    for pair in range(PAIRS):
        base = pair * PIECE
        first = product_ref[base : base + PAIR, :]
        middle = product_ref[base + PAIR : base + 2 * PAIR, :]
        last = product_ref[base + 2 * PAIR : base + 3 * PAIR, :]
        total = (
            middle
            + jnp.where(column == SIDE - 1, 0.0, pltpu.roll(first, PIX - 1, 1))
            + jnp.where(column == 0, 0.0, pltpu.roll(last, 1, 1))
        )
        for part in range(2):
            out_ref[pl.ds(block_offset(place_ref, 2 * pair + part), ROWS), :] = total[
                part * ROWS : (part + 1) * ROWS
            ]


def count_of(mask):
    return jnp.maximum(jnp.sum(mask, axis=1, keepdims=True), 1.0) * float(WIDTH)


def small_columns(columns):
    lane = lax.broadcasted_iota(jnp.int32, (C, 128), 1)
    result = jnp.zeros((C, 128), WIDE)
    for index, column in enumerate(columns):
        result = jnp.where(lane == index, column, result)
    return result


def small_rows(columns):
    return small_columns(columns).T[:8]


def set_rows(rows, count):
    index = lax.broadcasted_iota(jnp.int32, (count, rows[0].shape[1]), 0)
    result = jnp.zeros((count, rows[0].shape[1]), WIDE)
    for at, row in enumerate(rows):
        result = jnp.where(index == at, row, result)
    return result


def three_parts(value):
    high = value.astype(LOW).astype(WIDE)
    rest = value - high
    middle = rest.astype(LOW).astype(WIDE)
    return [high, middle, rest - middle]


def load_weight(weight, pieces):
    @pl.when(pl.program_id(0) == 0)
    def _():
        for index, source in enumerate(pieces):
            weight[index * PIECE : (index + 1) * PIECE, :] = source[...]


def both_rows(stacks):
    return jnp.concatenate([stack[...] for stack in stacks], axis=0)


def half_offsets(place):
    own = pl.multiple_of(place[BLOCKS] * HALF, HALF)
    other = pl.multiple_of((1 - place[BLOCKS]) * HALF, HALF)
    return own, other


def prepare_kernel(place, *refs):
    (
        mine,
        theirs,
        mask_ref,
        params,
        member,
        whole_out,
        low_out,
        high_out,
        stats_out,
        value,
    ) = refs[-10:]
    own, other = half_offsets(place)
    value[pl.ds(own, HALF), :] = mine[0].astype(WIDE)
    value[pl.ds(other, HALF), :] = theirs[0].astype(WIDE)
    mask = mask_ref[0]
    whole_out[0] = value[...].astype(LOW)
    mean, factor = group_stats(value, member[...], mask, count_of(mask))
    stats_out[0] = small_columns((mean, factor))
    scale = factor * params[:, 0:1]
    value[...] = (value[...] - mean) * scale + params[:, 1:2]
    build_stack(place, value, mask, (low_out, high_out))


def first_kernel(
    place,
    mask_ref,
    member,
    pieces,
    stacks,
    normed_out,
    stats_out,
    weight,
    value,
    product,
):
    load_weight(weight, pieces)
    mask = mask_ref[0]
    product[...] = dot(weight[...], both_rows(stacks), TN)
    for chan in range(2):
        value[chan * HALF : (chan + 1) * HALF, :] = conv_out(product, chan)
    mean, factor = group_stats(value, member[...], mask, count_of(mask))
    normed_out[0] = (value[...] - mean) * factor
    stats_out[0] = small_columns((factor,))


def second_kernel(
    place,
    normed,
    whole,
    embed_in,
    mask_ref,
    params,
    member,
    bundle,
    pieces,
    low_out,
    high_out,
    residual_out,
    attend_out,
    stats_out,
    weight,
    value,
    product,
):
    load_weight(weight, pieces)
    mask = mask_ref[0]
    count = count_of(mask)
    scales, shifts = [], []
    for chan in range(2):
        base = chan * MIXED + 4 * HALF
        sums = dot(bundle[:, base : base + C], embed_in[0, 0], TN) + dot(
            bundle[:, base + C : base + 2 * C], embed_in[0, 1], TN
        )
        column = sums[:, 0:1] + sums[:, 1:2] + sums[:, 2:3]
        scales.append(column[:HALF])
        shifts.append(column[HALF:])
    time_scale = jnp.concatenate(scales, axis=0)
    time_shift = jnp.concatenate(shifts, axis=0)
    affine = normed[0] * params[:, 2:3] + params[:, 3:4]
    value[...] = affine * (1.0 + time_scale) + time_shift
    stacks = (low_out, high_out)
    build_stack(place, value, mask, stacks)
    product[...] = dot(weight[...], both_rows(stacks), TN)
    for chan in range(2):
        rows = slice(chan * HALF, (chan + 1) * HALF)
        value[rows, :] = whole[0, rows, :].astype(WIDE) + conv_out(product, chan)
    residual_out[0] = value[...]
    mean, factor = group_stats(value, member[...], mask, count)
    scale = factor * params[:, 4:5]
    attend_out[0] = ((value[...] - mean) * scale + params[:, 5:6]).astype(LOW)
    stats_out[0] = small_columns((mean, factor, time_scale, time_shift))


def attend_kernel(
    place,
    attend_in,
    residual,
    stats,
    mine,
    theirs,
    mask_ref,
    params,
    member,
    bundle,
    block_out,
    send_out,
    residual_grad_out,
    second_grad_out,
    mixed_keep,
    mixed_send,
    small_out,
    project,
    output,
    gradient,
    projected,
    attend_grad,
    attended,
    projected_grad,
    key_side,
    value_side,
    value_rows,
    query_side,
    grad_side,
    scores,
    probs,
    score_grads,
    accumulated,
    value,
):
    image = pl.program_id(0)

    @pl.when(image == 0)
    def _():
        project[...] = jnp.concatenate(
            [bundle[:, : 3 * HALF], bundle[:, MIXED : MIXED + 3 * HALF]], axis=1
        )
        output[...] = jnp.concatenate(
            [
                bundle[:, 3 * HALF : 4 * HALF].astype(WIDE),
                bundle[:, MIXED + 3 * HALF : MIXED + 4 * HALF].astype(WIDE),
            ],
            axis=1,
        ).astype(LOW)
        accumulated[...] = jnp.zeros_like(accumulated)

    own, other = half_offsets(place)
    mask = mask_ref[0]
    count = count_of(mask)
    gradient[pl.ds(own, HALF), :] = (mine[0].astype(WIDE) * mask).astype(LOW)
    gradient[pl.ds(other, HALF), :] = (theirs[0].astype(WIDE) * mask).astype(LOW)
    projected[...] = dot(project[...], attend_in[0], TN).astype(LOW)
    attend_grad[...] = dot(output[...], gradient[...], TN).astype(LOW)

    penalty = mask - 1.0
    one = jnp.ones((1, PIX), WIDE)
    fill = jnp.zeros((KEYS - HEAD - 16, PIX), LOW)
    key_rows = jnp.concatenate(
        [set_rows([penalty * 9984.0, penalty * 16.0], 16).astype(LOW), fill], axis=0
    )
    one_rows = jnp.concatenate([set_rows([one, one, one], 16).astype(LOW), fill], axis=0)
    query_side[HEAD:, :] = one_rows
    grad_side[HEAD:, :] = jnp.zeros((KEYS - HEAD, PIX), LOW)

    def one_head(head, carry):
        chan = head // 3
        row_q = pl.multiple_of(chan * (3 * HALF) + (head - 3 * chan) * HEAD, HEAD)
        row_k = pl.multiple_of(row_q + HALF, HEAD)
        row_v = pl.multiple_of(row_q + 2 * HALF, HEAD)
        row_o = pl.multiple_of(head * HEAD, HEAD)
        queries = projected[pl.ds(row_q, HEAD), :]
        keys = projected[pl.ds(row_k, HEAD), :]
        values = jnp.concatenate([projected[pl.ds(row_v, HEAD), :], one_rows], axis=0)
        grads = attend_grad[pl.ds(row_o, HEAD), :].astype(WIDE)
        key_side[...] = jnp.concatenate([keys, key_rows], axis=0).T
        value_rows[...] = values[: HEAD + 16]
        value_side[...] = values.T
        query_side[:HEAD, :] = (queries.astype(WIDE) * HEAD**-0.5).astype(LOW)
        peak = None
        for start in range(0, PIX, CHUNK):
            part = dot(key_side[start : start + CHUNK, :], query_side[...], NN)
            scores[start : start + CHUNK, :] = part
            highest = jnp.max(part.reshape(CHUNK // 8, 8, PIX), axis=0)
            peak = highest if peak is None else jnp.maximum(peak, highest)
        peak = jnp.max(peak, axis=0, keepdims=True)
        for start in range(0, PIX, CHUNK):
            span = slice(start, start + CHUNK)
            probs[span, :] = jnp.exp(scores[span, :] - peak).astype(LOW)
        result = dot(value_rows[...], probs[...], NN)
        inverse = 1.0 / result[HEAD : HEAD + 1, :]
        result = result[:HEAD, :] * inverse
        attended[pl.ds(row_o, HEAD), :] = result.astype(LOW)
        scaled = grads * inverse
        delta = jnp.sum(scaled * result, axis=0, keepdims=True)
        grad_side[:HEAD, :] = scaled.astype(LOW)
        grad_side[HEAD : HEAD + 16, :] = set_rows(three_parts(-delta), 16).astype(LOW)
        for start in range(0, PIX, CHUNK):
            span = slice(start, start + CHUNK)
            part = dot(value_side[span, :], grad_side[...], NN)
            score_grads[span, :] = (probs[span, :].astype(WIDE) * part).astype(LOW)
        projected_grad[pl.ds(row_q, HEAD), :] = (
            dot(keys, score_grads[...], NN) * HEAD**-0.5
        ).astype(LOW)
        projected_grad[pl.ds(row_k, HEAD), :] = (
            dot(queries, score_grads[...], NT) * HEAD**-0.5
        ).astype(LOW)
        projected_grad[pl.ds(row_v, HEAD), :] = dot(grad_side[:HEAD, :], probs[...], NT).astype(
            LOW
        )
        return carry

    lax.fori_loop(0, C // HEAD, one_head, 0)

    value[...] = (residual[0] + dot(output[...], attended[...], NN)) * mask
    block_out[0] = value[pl.ds(own, HALF), :].astype(LOW)
    send_out[0] = value[pl.ds(other, HALF), :].astype(LOW)
    accumulated[:, TAPS:] += dot(gradient[...], attended[...], NT)
    accumulated[:, :TAPS] += dot(attend_in[0], projected_grad[...], NT)
    third = dot(project[...], projected_grad[...], NN)
    mean, factor = stats[0, :, 0:1], stats[0, :, 1:2]
    normed = (residual[0] - mean) * factor
    bias_third = jnp.sum(third, axis=1, keepdims=True)
    gain_third = jnp.sum(third * normed, axis=1, keepdims=True)
    gain = params[:, 4:5]
    sums = group_sums(member[...], lane_pair(gain * bias_third, gain * gain_third))
    first_sum, second_sum = sums[:, 0:1] / count, sums[:, 1:2] / count
    total = gradient[...].astype(WIDE) + factor * (
        third * gain - mask * (first_sum + normed * second_sum)
    )
    residual_grad_out[0] = total
    second_grad_out[0] = total.astype(LOW)
    small_out[0] = small_rows((gain_third, bias_third))

    @pl.when(image == pl.num_programs(0) - 1)
    def _():
        for pair in range(PAIRS):
            rows = pair_rows(place, accumulated, pair)
            out = mixed_keep if pair < PAIRS // 2 else mixed_send
            base = pair % (PAIRS // 2) * (JOINT - PIECE)
            third_rows = PAIR // 3
            out[base : base + PAIR, :] = rows[:, :TAPS].astype(out.dtype)
            out[base + PAIR : base + PAIR + third_rows, :] = jnp.concatenate(
                [rows[part * third_rows : (part + 1) * third_rows, TAPS:] for part in range(3)],
                axis=1,
            ).astype(out.dtype)


def filter_kernel(place, grads, stacks, mixed, *refs):
    outs, grad_stack = refs[:-1], refs[-1]
    stack_gradients(grads, grad_stack)
    both = jnp.concatenate([stack[...] for stack in stacks], axis=1)
    total = dot(both, grad_stack[...], NT)
    extra = JOINT - PIECE
    for part, out in enumerate(outs):
        rows = slice(part * extra, (part + 1) * extra)
        out[:PIECE, :] = total[part * PIECE : (part + 1) * PIECE].astype(out.dtype)
        out[PIECE:, :] = (mixed[0][rows, :] + mixed[1][rows, :].astype(WIDE)).astype(out.dtype)


def own_filter_kernel(place, grads, stacks, send_out, keep_out, grad_stack):
    stack_gradients([grads], grad_stack)
    send_out[...] = dot(stacks[1][...], grad_stack[...], NT).astype(LOW)
    keep_out[...] = dot(stacks[0][...], grad_stack[...], NT)


def split_kernel(place, keep, received, *outs):
    for part, out in enumerate(outs):
        rows = slice(part * PIECE, (part + 1) * PIECE)
        out[...] = (keep[rows, :] + received[rows, :].astype(WIDE)).astype(out.dtype)


def conv_back(place, grads, weight, grad_stack, product, value):
    stack_gradient(grads.at[0], grad_stack)
    product[...] = dot(weight[...], grad_stack[...], NN)
    back_to_channels(place, product, value)


def second_back_kernel(
    place,
    grads,
    weight,
    normed_ref,
    stats_first,
    stats,
    mask_ref,
    params,
    member,
    first_grad_out,
    small_out,
    grad_stack,
    product,
    value,
):
    conv_back(place, grads, weight, grad_stack, product, value)
    mask = mask_ref[0]
    count = count_of(mask)
    gain, bias = params[:, 2:3], params[:, 3:4]
    factor = stats_first[0, :, 0:1]
    time_scale, time_shift = 1.0 + stats[0, :, 2:3], stats[0, :, 3:4]
    normed = normed_ref[0]
    hidden = (normed * gain + bias) * time_scale + time_shift
    delta = value[...] * mask * silu_slope(hidden)
    value[...] = delta
    plain = jnp.sum(delta, axis=1, keepdims=True)
    weighted = jnp.sum(delta * normed, axis=1, keepdims=True)
    scaled = gain * time_scale
    sums = group_sums(member[...], lane_pair(scaled * plain, scaled * weighted))
    first_sum, second_sum = sums[:, 0:1] / count, sums[:, 1:2] / count
    first_grad_out[0] = (
        factor * (value[...] * scaled - mask * (first_sum + normed * second_sum))
    ).astype(LOW)
    small_out[0] = small_rows(
        (
            time_scale * weighted,
            time_scale * plain,
            gain * weighted + bias * plain,
            plain,
        )
    )


def first_back_kernel(place, *refs):
    (
        grads,
        weight,
        whole,
        stats_first,
        residual_grad,
        mask_ref,
        params,
        member,
        small_in,
        keep_out,
        send_out,
        small_out,
        grad_stack,
        product,
        value,
    ) = refs[-15:]
    conv_back(place, grads, weight, grad_stack, product, value)
    own, other = half_offsets(place)
    mask = mask_ref[0]
    count = count_of(mask)
    gain, bias = params[:, 0:1], params[:, 1:2]
    mean, factor = stats_first[0, :, 0:1], stats_first[0, :, 1:2]
    normed = (whole[0].astype(WIDE) - mean) * factor
    hidden = normed * gain + bias
    delta = value[...] * mask * silu_slope(hidden)
    value[...] = delta
    plain = jnp.sum(delta, axis=1, keepdims=True)
    weighted = jnp.sum(delta * normed, axis=1, keepdims=True)
    sums = group_sums(member[...], lane_pair(gain * plain, gain * weighted))
    first_sum, second_sum = sums[:, 0:1] / count, sums[:, 1:2] / count
    value[...] = residual_grad[0] + factor * (
        value[...] * gain - mask * (first_sum + normed * second_sum)
    )
    keep_out[0] = value[pl.ds(own, HALF), :]
    send_out[0] = value[pl.ds(other, HALF), :].astype(LOW)
    rows = small_rows((weighted, plain))
    if len(small_in) == 0:
        small_out[...] = rows
    else:
        earlier, second, third, steps = small_in
        for ref in earlier:
            rows = rows + ref[...]
        images = second.shape[0]
        second_sum, third_sum = second[0], third[0]
        for image in range(1, images):
            second_sum, third_sum = second_sum + second[image], third_sum + third[image]
        small_out[:8, :] = set_rows(
            [
                rows[0:1],
                second_sum[0:1],
                third_sum[0:1],
                rows[1:2],
                second_sum[1:2],
                third_sum[1:2],
            ],
            8,
        )
        small_out[8:, :] = set_rows(
            [second[image, 2 + kind : 3 + kind] for kind in range(2) for image in range(images)]
            + [steps[0:1]],
            8,
        )


def cut_kernel(place, own, one, two, three, mine_out, side_out, far_out, corner_out):
    total = own[...] + one[...].astype(WIDE) + two[...].astype(WIDE) + three[...].astype(WIDE)
    left = place[BLOCKS] == 0
    outs = ((mine_out, side_out), (far_out, corner_out))
    for part in range(2):
        pieces = [
            total[tap * PAIR + part * ROWS : tap * PAIR + (part + 1) * ROWS] for tap in range(3)
        ]
        joint = total.shape[0] > PIECE
        if joint:
            pieces.append(total[PIECE + part * ROWS : PIECE + (part + 1) * ROWS])
        rows = jnp.concatenate(pieces, axis=0)
        halves = [rows[:, : 3 * HALF], rows[:, 3 * HALF :]]
        if joint:
            third_rows = PAIR // 3
            packed = total[PIECE + PAIR :]
            rows = jnp.concatenate(
                [packed[:, third * C : (third + 1) * C] for third in range(3)], axis=0
            )[part * ROWS : (part + 1) * ROWS]
            for half in range(2):
                columns = rows[:, half * HALF : (half + 1) * HALF]
                packed_half = jnp.concatenate(
                    [columns[third * 8 : (third + 1) * 8] for third in range(3)], axis=1
                )
                halves[half] = jnp.concatenate([halves[half], packed_half], axis=0)
        here, away = outs[part]
        here[...] = jnp.where(left, halves[0], halves[1]).astype(here.dtype)
        away[...] = jnp.where(left, halves[1], halves[0]).astype(away.dtype)


def shape(*sizes, dtype=WIDE):
    return jax.ShapeDtypeStruct(sizes, dtype)


def per_image(*sizes, first=0):
    return pl.BlockSpec((1,) + sizes, lambda g, place: (first + g,) + (0,) * len(sizes))


def own_image(*sizes, first=0):
    return pl.BlockSpec(
        (1,) + sizes, lambda g, place: (place[BLOCKS + 1] + first + g,) + (0,) * len(sizes)
    )


def per_columns(*sizes, first=0):
    return pl.BlockSpec(sizes, lambda g, place: (0, first + g))


def fixed(*sizes):
    return pl.BlockSpec(sizes, lambda g, place: (0,) * len(sizes))


def whole_array(entry):
    return fixed(*entry.shape)


def run(kernel, place, images, ins, outs, scratch, aliases=None, room=24, cost=8):
    arrays, structure = jax.tree.flatten([array for array, _ in ins])
    specs = jax.tree.leaves(
        [spec for _, spec in ins], is_leaf=lambda entry: isinstance(entry, pl.BlockSpec)
    )

    def body(place, *refs):
        given = jax.tree.unflatten(structure, refs[: len(arrays)])
        kernel(place, *given, *refs[len(arrays) :])

    return pl.pallas_call(
        body,
        grid_spec=pltpu.PrefetchScalarGridSpec(
            num_scalar_prefetch=1,
            grid=(images,),
            in_specs=specs,
            out_specs=[spec for _, spec in outs],
            scratch_shapes=scratch,
        ),
        out_shape=[out for out, _ in outs],
        input_output_aliases=aliases or {},
        compiler_params=pltpu.CompilerParams(
            dimension_semantics=("arbitrary",), vmem_limit_bytes=room * 2**20
        ),
        cost_estimate=pl.CostEstimate(flops=cost * 10**9, bytes_accessed=2**20, transcendentals=0),
    )(place, *arrays)


def filter_gradient(place, stacks, grads, mixed):
    images = sum(grad.shape[0] for grad in grads)
    ins = (grads, stacks, mixed)
    outs = [shape(JOINT, TAPS)] + [shape(JOINT, TAPS, dtype=LOW)] * 3
    return run(
        filter_kernel,
        place,
        1,
        [(entry, jax.tree.map(whole_array, entry)) for entry in ins],
        [(out, whole_array(out)) for out in outs],
        [pltpu.VMEM((TAPS, images * PIX), LOW)],
        room=40,
    )


def own_filter_gradient(place, stacks, grads):
    ins = (grads, stacks)
    outs = [shape(TAPS // 2, TAPS, dtype=LOW), shape(TAPS // 2, TAPS)]
    return run(
        own_filter_kernel,
        place,
        1,
        [(entry, jax.tree.map(whole_array, entry)) for entry in ins],
        [(out, whole_array(out)) for out in outs],
        [pltpu.VMEM((TAPS, grads.shape[0] * PIX), LOW)],
        room=32,
        cost=1,
    )


def simple(kernel, place, ins, outs, cost):
    return run(
        kernel,
        place,
        1,
        [(array, whole_array(array)) for array in ins],
        [(out, whole_array(out)) for out in outs],
        [],
        cost=cost,
    )


def on_device(
    dp,
    features,
    pixel_masks,
    timesteps,
    first_filter,
    second_filter,
    project_weight,
    output_weight,
    embed_weight,
    norm_gains,
    norm_biases,
    cotangent,
):
    chan = lax.axis_index("chan")
    left = chan == 0
    span = dp // BLOCKS
    groups = [list(range(k * span, (k + 1) * span)) for k in range(BLOCKS)]
    block = lax.axis_index("dp") // span
    images = features.shape[0] // 2

    def swap(value, mask, flip):
        pairs = [
            (2 * d + x, 2 * (d ^ (mask * span)) + (x ^ flip)) for d in range(dp) for x in range(2)
        ]
        return lax.ppermute(value, ("dp", "chan"), pairs)

    def near(value, axis):
        if span == 1:
            return value
        return lax.all_gather(value, "dp", axis=axis, tiled=True, axis_index_groups=groups)

    def halves(mine, theirs, axis):
        return jnp.concatenate(
            [jnp.where(left, mine, theirs), jnp.where(left, theirs, mine)], axis=axis
        )

    def after(value, *others):
        return lax.optimization_barrier((value, others))[0]

    def pair_up(one, two):
        taps = one.shape[0] // ROWS
        columns = one.shape[1]
        both = [v.reshape(taps, ROWS, columns) for v in (one, two)]
        return jnp.stack(both, axis=1).reshape(2 * taps * ROWS, columns)

    def gather_one(shard, extra=None):
        side = swap(shard if extra is None else jnp.concatenate([shard, extra], axis=0), 0, 1)
        far = swap(shard, 8, 0)
        both = swap(shard, 8, 1)
        count = shard.shape[0]
        rows = pair_up(halves(shard, side[:count], 1), halves(far, both, 1))
        return rows if extra is None else (rows, side[count:])

    def gather_two(rows):
        return [rows, swap(rows, 4, 0), swap(rows, 2, 0), swap(rows, 6, 0)]

    def gather_three(pieces):
        return [swap(rows, 1, 0) for rows in pieces]

    def scatter_one(send, keep):
        outs = [shape(PIECE, TAPS)] + [shape(PIECE, TAPS, dtype=LOW)] * 3
        return simple(split_kernel, place, [keep, swap(send, 1, 0)], outs, 1)

    def scatter_two(keep, *sends, late=()):
        keep = after(keep, late)
        arrived = [swap(send, mask, 0) for send, mask in zip(sends, (4, 2, 6))]
        rows = keep.shape[0] // 2
        outs = [shape(rows, 3 * HALF)] + [shape(rows, 3 * HALF, dtype=LOW)] * 3
        return simple(cut_kernel, place, [keep] + arrived, outs, 30)

    def scatter_three(keep, *sends):
        total = keep
        for send, (mask, flip) in zip(sends, ((0, 1), (8, 0), (8, 1))):
            total = total + swap(send, mask, flip).astype(WIDE)
        return total

    def share(value, dimension):
        if span == 1:
            return value
        return lax.psum_scatter(
            value, "dp", scatter_dimension=dimension, tiled=True, axis_index_groups=groups
        )

    def parts_of(value):
        high = value.astype(LOW)
        rest = value - high.astype(WIDE)
        middle = rest.astype(LOW)
        return [high, middle, (rest - middle.astype(WIDE)).astype(LOW)]

    own_start, other_start = chan * images, (1 - chan) * images

    def exchange(value, image):
        return swap(lax.dynamic_slice_in_dim(value, other_start + image, 1, 0), 0, 1)

    theirs = [exchange(features, image) for image in range(images)]

    def filter_rows(weight):
        rows = near(weight.astype(LOW), 1).reshape(3, 3, ROWS, HALF)
        return jnp.transpose(rows, (1, 2, 0, 3)).reshape(3 * ROWS, 3 * HALF)

    norms = jnp.concatenate([norm_gains, norm_biases], axis=0)
    norm_rows = jnp.pad(jnp.concatenate(parts_of(norms), axis=1), ((0, 2), (0, 0)))
    first_one, norm_rows = gather_one(filter_rows(first_filter), norm_rows)
    their_norms = norm_rows[:6].astype(WIDE).reshape(6, 3, HALF)
    their_norms = their_norms[:, 0] + their_norms[:, 1] + their_norms[:, 2]
    norms = halves(norms, their_norms, 1)
    params = jnp.stack([norms[0], norms[3], norms[1], norms[4], norms[2], norms[5]], axis=1)
    params = jnp.pad(params, ((0, 0), (0, 2)))
    first_pieces = gather_two(first_one)

    embed_rows = jnp.transpose(embed_weight.astype(LOW), (1, 0, 2))
    embed_rows = embed_rows.reshape(2, -1, 2 * HALF)
    rows = project_weight.shape[0]
    bundle_rows = jnp.concatenate(
        [
            project_weight.astype(LOW).reshape(rows, 3 * HALF),
            output_weight.astype(LOW).T,
            embed_rows[0],
            embed_rows[1],
        ],
        axis=1,
    )
    bundle_rows = halves(bundle_rows, swap(bundle_rows, 0, 1), 1)
    bundle = lax.all_gather(bundle_rows, "dp", axis=0, tiled=True)
    second_one = gather_one(after(filter_rows(second_filter), first_one, theirs[0]))
    first_pieces = first_pieces + gather_three(first_pieces)

    validity = lax.dynamic_slice_in_dim(pixel_masks, own_start, images, 0).astype(WIDE)
    validity = validity.reshape(images, 1, PIX)
    member = (jnp.arange(C)[:, None] // WIDTH == jnp.arange(C)[None, :] // WIDTH).astype(LOW)
    order = jnp.array(ORDER, jnp.int32)
    place = jnp.concatenate(
        [
            jnp.bitwise_xor(block, order) * ROWS,
            jnp.stack([chan, own_start]).astype(jnp.int32),
        ]
    )

    def time_features(steps, index, embed_width):
        half_width = embed_width // 2
        power = jnp.where(index < half_width, index, index - half_width).astype(WIDE)
        frequency = jnp.exp(-math.log(10000.0) * power / half_width)
        angles = steps[:, None] * frequency[None, :]
        return jax.nn.silu(
            jnp.where(index[None, :] < half_width, jnp.cos(angles), jnp.sin(angles))
        )

    embed_width = embed_weight.shape[1] * dp
    own_steps = lax.dynamic_slice_in_dim(timesteps, own_start, images, 0).astype(WIDE)
    half_rows = jnp.arange(2)[:, None, None] * rows + jnp.arange(rows)
    embed_index = (jnp.arange(dp)[:, None] * (2 * rows) + half_rows).reshape(-1)
    embed_values = time_features(own_steps, embed_index, embed_width)
    embed_parts = jnp.stack(parts_of(embed_values), axis=2).reshape(images, 2, C, 3)
    embed_parts = jnp.pad(embed_parts, ((0, 0), (0, 0), (0, 0), (0, 125)))
    steps_row = jnp.pad(own_steps, (0, HALF - images))
    steps_row = jnp.pad(jnp.concatenate([steps_row, steps_row])[None, :], ((0, 7), (0, 0)))

    value_scratch = pltpu.VMEM((C, PIX), WIDE)
    product_scratch = pltpu.VMEM((TAPS, PIX), WIDE)
    back_scratch = [pltpu.VMEM((TAPS, PIX), LOW), product_scratch, value_scratch]
    mask_in = (validity, per_image(1, PIX))
    params_in = (params, fixed(C, 8))
    member_in = (member, fixed(C, C))
    image_low = (shape(images, C, PIX, dtype=LOW), per_image(C, PIX))
    image_wide = (shape(images, C, PIX), per_image(C, PIX))
    image_small = (shape(images, C, 128), per_image(C, 128))
    image_rows = (shape(images, 8, C), per_image(8, C))
    weight_out = (shape(TAPS, TAPS, dtype=LOW), fixed(TAPS, TAPS))
    stack_out = (shape(TAPS // 2, images * PIX, dtype=LOW), per_columns(TAPS // 2, PIX))
    anywhere = pl.BlockSpec(memory_space=pl.ANY)

    prepared = ()
    for image in range(images):
        prepared = run(
            prepare_kernel,
            place,
            1,
            [(array, anywhere) for array in prepared]
            + [
                (features, own_image(HALF, PIX, first=image)),
                (theirs[image], per_image(HALF, PIX)),
                (validity, per_image(1, PIX, first=image)),
                params_in,
                member_in,
            ],
            [
                (image_low[0], per_image(C, PIX, first=image)),
                (stack_out[0], per_columns(TAPS // 2, PIX, first=image)),
                (stack_out[0], per_columns(TAPS // 2, PIX, first=image)),
                (image_small[0], per_image(C, 128, first=image)),
            ],
            [value_scratch],
            {1 + k: k for k in range(len(prepared))},
        )
    whole, first_low, first_high, stats_whole = prepared
    second_normed, stats_first, first_weight = run(
        first_kernel,
        place,
        images,
        [
            mask_in,
            member_in,
            (first_pieces, [fixed(PIECE, TAPS)] * 8),
            (after([first_low, first_high], second_one), [per_columns(TAPS // 2, PIX)] * 2),
        ],
        [image_wide, image_small, weight_out],
        [value_scratch, product_scratch],
    )
    second_pieces = gather_two(second_one)
    second_pieces = second_pieces + gather_three(after(second_pieces, second_normed))
    their_cots = swap(
        after(lax.dynamic_slice_in_dim(cotangent, other_start, images, 0), second_normed), 0, 1
    )
    second_low, second_high, residual, attend_input, stats_second, second_weight = run(
        second_kernel,
        place,
        images,
        [
            (second_normed, per_image(C, PIX)),
            (whole, per_image(C, PIX)),
            (embed_parts, per_image(2, C, 128)),
            mask_in,
            params_in,
            member_in,
            (bundle, fixed(C, 2 * MIXED)),
            (second_pieces, [fixed(PIECE, TAPS)] * 8),
        ],
        [stack_out, stack_out, image_wide, image_low, image_small, weight_out],
        [value_scratch, product_scratch],
        room=36,
    )
    second_theirs = swap(second_high, 1, 0)
    mixed_rows = PAIRS // 2 * (JOINT - PIECE)
    block_keep, block_send, residual_grad, second_grad, *mixed, small_third = run(
        attend_kernel,
        place,
        images,
        [
            (attend_input, per_image(C, PIX)),
            (residual, per_image(C, PIX)),
            (stats_second, per_image(C, 128)),
            (cotangent, own_image(HALF, PIX)),
            (their_cots, per_image(HALF, PIX)),
            mask_in,
            params_in,
            member_in,
            (bundle, fixed(C, 2 * MIXED)),
        ],
        [
            (shape(2 * images, HALF, PIX, dtype=LOW), own_image(HALF, PIX)),
            (shape(images, HALF, PIX, dtype=LOW), per_image(HALF, PIX)),
            image_wide,
            image_low,
            (shape(mixed_rows, TAPS), fixed(mixed_rows, TAPS)),
            (shape(mixed_rows, TAPS, dtype=LOW), fixed(mixed_rows, TAPS)),
            image_rows,
        ],
        [
            pltpu.VMEM((C, TAPS), LOW),
            pltpu.VMEM((C, C), LOW),
            pltpu.VMEM((C, PIX), LOW),
            pltpu.VMEM((TAPS, PIX), LOW),
            pltpu.VMEM((C, PIX), LOW),
            pltpu.VMEM((C, PIX), LOW),
            pltpu.VMEM((TAPS, PIX), LOW),
            pltpu.VMEM((PIX, KEYS), LOW),
            pltpu.VMEM((PIX, KEYS), LOW),
            pltpu.VMEM((HEAD + 16, PIX), LOW),
            pltpu.VMEM((KEYS, PIX), LOW),
            pltpu.VMEM((KEYS, PIX), LOW),
            pltpu.VMEM((PIX, PIX), WIDE),
            pltpu.VMEM((PIX, PIX), LOW),
            pltpu.VMEM((PIX, PIX), LOW),
            pltpu.VMEM((C, TAPS + C), WIDE),
            value_scratch,
        ],
        room=48,
        cost=60,
    )
    block_theirs = swap(block_send, 0, 1)
    mixed = [mixed[0], swap(mixed[1], 1, 0)]
    grads_theirs = swap(second_grad, 1, 0)
    joint = filter_gradient(
        place, [second_low, second_theirs], [second_grad, grads_theirs], mixed
    )
    first_grad, small_second = run(
        second_back_kernel,
        place,
        images,
        [
            (after(second_grad, joint), per_image(C, PIX)),
            (second_weight, fixed(TAPS, TAPS)),
            (second_normed, per_image(C, PIX)),
            (stats_first, per_image(C, 128)),
            (stats_second, per_image(C, 128)),
            mask_in,
            params_in,
            member_in,
        ],
        [image_low, image_rows],
        back_scratch,
    )
    masked_out = lax.dynamic_update_slice_in_dim(
        after(block_keep, joint), block_theirs, other_start, 0
    )
    send, keep = own_filter_gradient(
        place, [first_low, first_high], after(first_grad, masked_out)
    )
    first_part = scatter_one(send, keep)
    joint = scatter_two(*joint, late=send)
    input_grad, input_theirs, smalls = None, [], []
    back_grad = after(first_grad, first_part, joint)
    for image in range(images):
        last = image == images - 1
        small_in = (smalls, small_second, small_third, steps_row) if last else ()
        carried = [] if input_grad is None else [(input_grad, anywhere)]
        small_shape = shape(16 if last else 8, C)
        input_grad, input_send, small = run(
            first_back_kernel,
            place,
            1,
            carried
            + [
                (back_grad, per_image(C, PIX, first=image)),
                (first_weight, fixed(TAPS, TAPS)),
                (whole, per_image(C, PIX, first=image)),
                (stats_whole, per_image(C, 128, first=image)),
                (residual_grad, per_image(C, PIX, first=image)),
                (validity, per_image(1, PIX, first=image)),
                params_in,
                member_in,
                (small_in, jax.tree.map(whole_array, small_in)),
            ],
            [
                (shape(2 * images, HALF, PIX), own_image(HALF, PIX, first=image)),
                (shape(1, HALF, PIX, dtype=LOW), per_image(HALF, PIX)),
                (small_shape, whole_array(small_shape)),
            ],
            back_scratch,
            {1: 0} if carried else None,
        )
        smalls.append(small)
        input_theirs.append(swap(input_send, 0, 1))
    first_part = scatter_two(*first_part)
    joint = scatter_three(after(joint[0], smalls[0]), *joint[1:])
    message = after(smalls[-1], first_part, joint, input_theirs[:-1])
    first_part = scatter_three(*first_part)

    for image in range(images):
        input_grad = lax.dynamic_update_slice_in_dim(
            input_grad, input_theirs[image].astype(WIDE), other_start + image, 0
        )

    def filter_shape(rows):
        rows = jnp.transpose(rows.reshape(3, ROWS, 3, HALF), (2, 0, 1, 3))
        return share(rows.reshape(9, ROWS, HALF), 1)

    grad_second = filter_shape(joint[: 3 * ROWS])
    grad_project = share(joint[3 * ROWS : 4 * ROWS].reshape(ROWS, 3, HALF), 0)
    grad_output = jnp.transpose(joint[4 * ROWS :].reshape(8, 3, HALF), (2, 1, 0))
    grad_output = share(grad_output.reshape(HALF, ROWS), 1)
    grad_first = filter_shape(first_part)

    def merge(arrived):
        total = sum(message[:8] for message in arrived)
        return jnp.concatenate([total] + [message[8:] for message in arrived], axis=0)

    message = merge([message, swap(message, 1, 0)])
    message = merge([message] + [swap(message, m, 0) for m in (4, 2, 6)])
    one, two = after(message[:, :HALF], input_theirs[-1]), message[:, HALF:]
    own, away = jnp.where(left, one, two), jnp.where(left, two, one)
    message = merge([own, swap(away, 0, 1), swap(own, 8, 0), swap(away, 8, 1)])
    total, entries = message[:6], message[8:]
    if span > 1:
        total = lax.psum(total, "dp", axis_index_groups=groups)
        entries = lax.all_gather(entries, "dp", axis=0, tiled=True, axis_index_groups=groups)
    entries = entries.reshape(-1, 8, HALF)
    all_steps = entries[:, 2 * images, :images].reshape(-1)
    scale_grads = entries[:, :images].reshape(-1, HALF)
    shift_grads = entries[:, images : 2 * images].reshape(-1, HALF)
    rows = embed_weight.shape[1]
    row_index = lax.axis_index("dp") * rows + jnp.arange(rows)
    all_embed = time_features(all_steps, row_index, embed_width)
    grad_embed = jnp.einsum(
        "be,kbd->ked",
        all_embed,
        jnp.stack([scale_grads, shift_grads]),
        precision=lax.Precision.HIGHEST,
    )
    return (
        masked_out,
        input_grad,
        grad_first,
        grad_second,
        grad_project,
        grad_output,
        grad_embed,
        total[:3],
        total[3:],
    )


def solution(mesh):
    in_specs = (
        P("dp", "chan", None),
        P("dp", None),
        P("dp"),
        P(None, "dp", "chan"),
        P(None, "dp", "chan"),
        P("dp", None, "chan"),
        P("chan", "dp"),
        P(None, "dp", "chan"),
        P(None, "chan"),
        P(None, "chan"),
        P("dp", "chan", None),
    )
    out_specs = (
        P("dp", "chan", None),
        P("dp", "chan", None),
        P(None, "dp", "chan"),
        P(None, "dp", "chan"),
        P("dp", None, "chan"),
        P("chan", "dp"),
        P(None, "dp", "chan"),
        P(None, "chan"),
        P(None, "chan"),
    )
    return jax.shard_map(
        functools.partial(on_device, mesh.shape["dp"]),
        mesh=mesh,
        in_specs=in_specs,
        out_specs=out_specs,
        check_vma=False,
    )
```

```python
import functools
import math

import jax
import jax.numpy as jnp
from jax import lax
from jax.experimental import pallas as pl
from jax.experimental.pallas import tpu as pltpu
from jax.sharding import PartitionSpec as P

C = 384
HALF = 192
HEAD = 64
GROUPS = 32
WIDTH = C // GROUPS
SIDE = 32
PIX = SIDE * SIDE
BLOCKS = 16
ROWS = C // BLOCKS
TAPS = 3 * C
EPSILON = 1e-05
SECOND = 3 * HALF + 256
MIXED = 4 * HALF
PAIR = 2 * ROWS
PIECE = 3 * PAIR
JOINT = PIECE + PAIR + PAIR // 3
PAIRS = BLOCKS // 2
KEYS = 128
CHUNK = 256
LOW = jnp.bfloat16
WIDE = jnp.float32
ORDER = (0, 8, 4, 12, 2, 10, 6, 14, 1, 9, 5, 13, 3, 11, 7, 15)

NN = (((1,), (0,)), ((), ()))
NT = (((1,), (1,)), ((), ()))
TN = (((0,), (0,)), ((), ()))


def dot(left, right, dims):
    return lax.dot_general(left, right, dims, preferred_element_type=WIDE)


def pixel_row(keep):
    pixel = lax.broadcasted_iota(jnp.int32, (1, PIX), 1)
    return jnp.where(keep(pixel), 1.0, 0.0).astype(LOW)


def lane_pair(first, second):
    lane = lax.broadcasted_iota(jnp.int32, (C, 128), 1)
    return jnp.where(lane == 0, first, jnp.where(lane == 1, second, 0.0))


def group_sums(member, values):
    high = values.astype(LOW)
    rest = values - high.astype(WIDE)
    middle = rest.astype(LOW)
    low = (rest - middle.astype(WIDE)).astype(LOW)
    return dot(member, high, NN) + dot(member, middle, NN) + dot(member, low, NN)


def group_sum(member, column):
    return group_sums(member, jnp.broadcast_to(column, (C, 128)))[:, 0:1]


def group_stats(value_ref, member, mask, count):
    mean = group_sum(member, jnp.sum(value_ref[...] * mask, axis=1, keepdims=True)) / count
    centred = value_ref[...] - mean
    variance = (
        group_sum(member, jnp.sum(centred * centred * mask, axis=1, keepdims=True)) / count
    )
    return mean, lax.rsqrt(variance + EPSILON)


def silu(value):
    return value / (1.0 + jnp.exp(-value))


def silu_slope(value):
    squashed = 1.0 / (1.0 + jnp.exp(-value))
    return squashed * (1.0 + value * (1.0 - squashed))


def shift_down(piece):
    pixel = lax.broadcasted_iota(jnp.int32, piece.shape, 1)
    return jnp.where(pixel < SIDE, 0.0, pltpu.roll(piece, SIDE, 1))


def shift_up(piece):
    pixel = lax.broadcasted_iota(jnp.int32, piece.shape, 1)
    return jnp.where(pixel >= PIX - SIDE, 0.0, pltpu.roll(piece, PIX - SIDE, 1))


def conv_out(product_ref, chan):
    base = chan * 3 * HALF
    return (
        product_ref[base + HALF : base + 2 * HALF, :]
        + shift_down(product_ref[base : base + HALF, :])
        + shift_up(product_ref[base + 2 * HALF : base + 3 * HALF, :])
    )


def stack_gradient(grad_ref, out_ref):
    not_top = pixel_row(lambda pixel: pixel >= SIDE)
    not_bottom = pixel_row(lambda pixel: pixel < PIX - SIDE)
    for chan in range(2):
        piece = grad_ref[chan * HALF : (chan + 1) * HALF, :]
        base = chan * 3 * HALF
        out_ref[base : base + HALF, :] = pltpu.roll(piece, PIX - SIDE, 1) * not_bottom
        out_ref[base + HALF : base + 2 * HALF, :] = piece
        out_ref[base + 2 * HALF : base + 3 * HALF, :] = pltpu.roll(piece, SIDE, 1) * not_top


def stack_gradients(grads, out_ref):
    at = 0
    for ref in grads:
        for image in range(ref.shape[0]):
            stack_gradient(ref.at[image], out_ref.at[:, at * PIX : (at + 1) * PIX])
            at += 1


def block_offset(place_ref, position):
    return pl.multiple_of(place_ref[position], 8)


def pair_rows(place, ref, pair):
    return jnp.concatenate(
        [ref[pl.ds(block_offset(place, 2 * pair + part), ROWS), :] for part in range(2)], axis=0
    )


def build_stack(place, value, mask, stacks):
    not_left = pixel_row(lambda pixel: pixel % SIDE != 0)
    not_right = pixel_row(lambda pixel: pixel % SIDE != SIDE - 1)
    for pair in range(PAIRS):
        piece = (silu(pair_rows(place, value, pair)) * mask).astype(LOW)
        stack = stacks[pair // (PAIRS // 2)]
        base = pair % (PAIRS // 2) * PIECE
        stack[base : base + PAIR, :] = pltpu.roll(piece, 1, 1) * not_left
        stack[base + PAIR : base + 2 * PAIR, :] = piece
        stack[base + 2 * PAIR : base + 3 * PAIR, :] = pltpu.roll(piece, PIX - 1, 1) * not_right


def back_to_channels(place_ref, product_ref, out_ref):
    column = lax.broadcasted_iota(jnp.int32, (PAIR, PIX), 1) & (SIDE - 1)
    for pair in range(PAIRS):
        base = pair * PIECE
        first = product_ref[base : base + PAIR, :]
        middle = product_ref[base + PAIR : base + 2 * PAIR, :]
        last = product_ref[base + 2 * PAIR : base + 3 * PAIR, :]
        total = (
            middle
            + jnp.where(column == SIDE - 1, 0.0, pltpu.roll(first, PIX - 1, 1))
            + jnp.where(column == 0, 0.0, pltpu.roll(last, 1, 1))
        )
        for part in range(2):
            out_ref[pl.ds(block_offset(place_ref, 2 * pair + part), ROWS), :] = total[
                part * ROWS : (part + 1) * ROWS
            ]


def count_of(mask):
    return jnp.maximum(jnp.sum(mask, axis=1, keepdims=True), 1.0) * float(WIDTH)


def small_columns(columns):
    lane = lax.broadcasted_iota(jnp.int32, (C, 128), 1)
    result = jnp.zeros((C, 128), WIDE)
    for index, column in enumerate(columns):
        result = jnp.where(lane == index, column, result)
    return result


def small_rows(columns):
    return small_columns(columns).T[:8]


def set_rows(rows, count):
    index = lax.broadcasted_iota(jnp.int32, (count, rows[0].shape[1]), 0)
    result = jnp.zeros((count, rows[0].shape[1]), WIDE)
    for at, row in enumerate(rows):
        result = jnp.where(index == at, row, result)
    return result


def three_parts(value):
    high = value.astype(LOW).astype(WIDE)
    rest = value - high
    middle = rest.astype(LOW).astype(WIDE)
    return [high, middle, rest - middle]


def load_weight(weight, pieces):
    @pl.when(pl.program_id(0) == 0)
    def _():
        for index, source in enumerate(pieces):
            weight[index * PIECE : (index + 1) * PIECE, :] = source[...]


def load_second(weight, weight_e, pieces):
    @pl.when(pl.program_id(0) == 0)
    def _():
        for index, source in enumerate(pieces):
            rows = slice(index * PIECE, (index + 1) * PIECE)
            for chan in range(2):
                base = chan * SECOND
                weight[rows, chan * 3 * HALF : (chan + 1) * 3 * HALF] = source[
                    :, base : base + 3 * HALF
                ]
                for part in range(2):
                    lane = base + 3 * HALF + part * 128
                    weight_e[chan, part, rows, :] = source[:, lane : lane + 128]


def both_rows(stacks):
    return jnp.concatenate([stack[...] for stack in stacks], axis=0)


def half_offsets(place):
    own = pl.multiple_of(place[BLOCKS] * HALF, HALF)
    other = pl.multiple_of((1 - place[BLOCKS]) * HALF, HALF)
    return own, other


def prepare_kernel(
    place,
    mine,
    theirs,
    mask_ref,
    params,
    member,
    whole_out,
    low_out,
    high_out,
    stats_out,
    value,
):
    own, other = half_offsets(place)
    value[pl.ds(own, HALF), :] = mine[0].astype(WIDE)
    value[pl.ds(other, HALF), :] = theirs[0].astype(WIDE)
    mask = mask_ref[0]
    whole_out[0] = value[...].astype(LOW)
    mean, factor = group_stats(value, member[...], mask, count_of(mask))
    stats_out[0] = small_columns((mean, factor))
    scale = factor * params[:, 0:1]
    value[...] = (value[...] - mean) * scale + params[:, 1:2]
    build_stack(place, value, mask, (low_out, high_out))


def first_kernel(
    place,
    mask_ref,
    member,
    pieces,
    stacks,
    normed_out,
    stats_out,
    weight,
    value,
    product,
):
    load_weight(weight, pieces)
    mask = mask_ref[0]
    product[...] = dot(weight[...], both_rows(stacks), TN)
    for chan in range(2):
        value[chan * HALF : (chan + 1) * HALF, :] = conv_out(product, chan)
    mean, factor = group_stats(value, member[...], mask, count_of(mask))
    normed_out[0] = (value[...] - mean) * factor
    stats_out[0] = small_columns((factor,))


def second_kernel(
    place,
    normed,
    whole,
    embed_in,
    mask_ref,
    params,
    member,
    pieces,
    low_out,
    high_out,
    residual_out,
    attend_out,
    stats_out,
    weight,
    weight_e,
    value,
    product,
):
    load_second(weight, weight_e, pieces)
    mask = mask_ref[0]
    count = count_of(mask)
    scales, shifts = [], []
    for chan in range(2):
        low = dot(weight_e[chan, 0], embed_in[0, 0], TN)
        high = dot(weight_e[chan, 1], embed_in[0, 1], TN)
        column = jnp.concatenate(
            [
                low[:, 0:1] + low[:, 1:2] + low[:, 2:3],
                low[:, 3:4] + low[:, 4:5] + low[:, 5:6] + high[:, 0:1] + high[:, 1:2] + high[:, 2:3],
                high[:, 3:4] + high[:, 4:5] + high[:, 5:6],
            ],
            axis=0,
        )
        scales.append(column[:HALF])
        shifts.append(column[HALF:])
    time_scale = jnp.concatenate(scales, axis=0)
    time_shift = jnp.concatenate(shifts, axis=0)
    affine = normed[0] * params[:, 2:3] + params[:, 3:4]
    value[...] = affine * (1.0 + time_scale) + time_shift
    stacks = (low_out, high_out)
    build_stack(place, value, mask, stacks)
    product[...] = dot(weight[...], both_rows(stacks), TN)
    for chan in range(2):
        rows = slice(chan * HALF, (chan + 1) * HALF)
        value[rows, :] = whole[0, rows, :].astype(WIDE) + conv_out(product, chan)
    residual_out[0] = value[...]
    mean, factor = group_stats(value, member[...], mask, count)
    scale = factor * params[:, 4:5]
    attend_out[0] = ((value[...] - mean) * scale + params[:, 5:6]).astype(LOW)
    stats_out[0] = small_columns((mean, factor, time_scale, time_shift))


def attend_kernel(
    place,
    attend_in,
    residual,
    stats,
    mine,
    theirs,
    mask_ref,
    params,
    member,
    bundle,
    block_out,
    send_out,
    residual_grad_out,
    second_grad_out,
    mixed_keep,
    mixed_send,
    small_out,
    weight_f,
    project,
    output,
    gradient,
    projected,
    attend_grad,
    attended,
    projected_grad,
    key_side,
    value_side,
    value_rows,
    query_side,
    grad_side,
    scores,
    probs,
    score_grads,
    accumulated,
    value,
):
    image = pl.program_id(0)

    @pl.when(image == 0)
    def _():
        for chan in range(2):
            for pair in range(PAIRS):
                block = bundle[pair][:, chan * MIXED : (chan + 1) * MIXED].astype(WIDE)
                for part in range(2):
                    weight_f[chan, pl.ds(block_offset(place, 2 * pair + part), ROWS), :] = block[
                        part * ROWS : (part + 1) * ROWS
                    ]
        project[...] = jnp.concatenate(
            [weight_f[0, :, : 3 * HALF], weight_f[1, :, : 3 * HALF]], axis=1
        ).astype(LOW)
        output[...] = jnp.concatenate(
            [weight_f[0, :, 3 * HALF :], weight_f[1, :, 3 * HALF :]], axis=1
        ).astype(LOW)
        accumulated[...] = jnp.zeros_like(accumulated)

    own, other = half_offsets(place)
    mask = mask_ref[0]
    count = count_of(mask)
    gradient[pl.ds(own, HALF), :] = (mine[0].astype(WIDE) * mask).astype(LOW)
    gradient[pl.ds(other, HALF), :] = (theirs[0].astype(WIDE) * mask).astype(LOW)
    projected[...] = dot(project[...], attend_in[0], TN).astype(LOW)
    attend_grad[...] = dot(output[...], gradient[...], TN).astype(LOW)

    penalty = mask - 1.0
    one = jnp.ones((1, PIX), WIDE)
    fill = jnp.zeros((KEYS - HEAD - 16, PIX), LOW)
    key_rows = jnp.concatenate(
        [set_rows([penalty * 9984.0, penalty * 16.0], 16).astype(LOW), fill], axis=0
    )
    one_rows = jnp.concatenate([set_rows([one, one, one], 16).astype(LOW), fill], axis=0)
    query_side[HEAD:, :] = one_rows
    grad_side[HEAD:, :] = jnp.zeros((KEYS - HEAD, PIX), LOW)

    def one_head(head, carry):
        chan = head // 3
        row_q = pl.multiple_of(chan * (3 * HALF) + (head - 3 * chan) * HEAD, HEAD)
        row_k = pl.multiple_of(row_q + HALF, HEAD)
        row_v = pl.multiple_of(row_q + 2 * HALF, HEAD)
        row_o = pl.multiple_of(head * HEAD, HEAD)
        queries = projected[pl.ds(row_q, HEAD), :]
        keys = projected[pl.ds(row_k, HEAD), :]
        values = jnp.concatenate([projected[pl.ds(row_v, HEAD), :], one_rows], axis=0)
        grads = attend_grad[pl.ds(row_o, HEAD), :].astype(WIDE)
        key_side[...] = jnp.concatenate([keys, key_rows], axis=0).T
        value_rows[...] = values[: HEAD + 16]
        value_side[...] = values.T
        query_side[:HEAD, :] = (queries.astype(WIDE) * HEAD**-0.5).astype(LOW)
        peak = None
        for start in range(0, PIX, CHUNK):
            part = dot(key_side[start : start + CHUNK, :], query_side[...], NN)
            scores[start : start + CHUNK, :] = part
            highest = jnp.max(part.reshape(CHUNK // 8, 8, PIX), axis=0)
            peak = highest if peak is None else jnp.maximum(peak, highest)
        peak = jnp.max(peak, axis=0, keepdims=True)
        for start in range(0, PIX, CHUNK):
            span = slice(start, start + CHUNK)
            probs[span, :] = jnp.exp(scores[span, :] - peak).astype(LOW)
        result = dot(value_rows[...], probs[...], NN)
        inverse = 1.0 / result[HEAD : HEAD + 1, :]
        result = result[:HEAD, :] * inverse
        attended[pl.ds(row_o, HEAD), :] = result.astype(LOW)
        scaled = grads * inverse
        delta = jnp.sum(scaled * result, axis=0, keepdims=True)
        grad_side[:HEAD, :] = scaled.astype(LOW)
        grad_side[HEAD : HEAD + 16, :] = set_rows(three_parts(-delta), 16).astype(LOW)
        for start in range(0, PIX, CHUNK):
            span = slice(start, start + CHUNK)
            part = dot(value_side[span, :], grad_side[...], NN)
            score_grads[span, :] = (probs[span, :].astype(WIDE) * part).astype(LOW)
        projected_grad[pl.ds(row_q, HEAD), :] = (
            dot(keys, score_grads[...], NN) * HEAD**-0.5
        ).astype(LOW)
        projected_grad[pl.ds(row_k, HEAD), :] = (
            dot(queries, score_grads[...], NT) * HEAD**-0.5
        ).astype(LOW)
        projected_grad[pl.ds(row_v, HEAD), :] = dot(grad_side[:HEAD, :], probs[...], NT).astype(
            LOW
        )
        return carry

    lax.fori_loop(0, C // HEAD, one_head, 0)

    value[...] = (residual[0] + dot(output[...], attended[...], NN)) * mask
    block_out[0] = value[pl.ds(own, HALF), :].astype(LOW)
    send_out[0] = value[pl.ds(other, HALF), :].astype(LOW)
    accumulated[:, TAPS:] += dot(gradient[...], attended[...], NT)
    accumulated[:, :TAPS] += dot(attend_in[0], projected_grad[...], NT)
    third = dot(project[...], projected_grad[...], NN)
    mean, factor = stats[0, :, 0:1], stats[0, :, 1:2]
    normed = (residual[0] - mean) * factor
    bias_third = jnp.sum(third, axis=1, keepdims=True)
    gain_third = jnp.sum(third * normed, axis=1, keepdims=True)
    gain = params[:, 4:5]
    sums = group_sums(member[...], lane_pair(gain * bias_third, gain * gain_third))
    first_sum, second_sum = sums[:, 0:1] / count, sums[:, 1:2] / count
    total = gradient[...].astype(WIDE) + factor * (
        third * gain - mask * (first_sum + normed * second_sum)
    )
    residual_grad_out[0] = total
    second_grad_out[0] = total.astype(LOW)
    small_out[0] = small_rows((gain_third, bias_third))

    @pl.when(image == pl.num_programs(0) - 1)
    def _():
        for pair in range(PAIRS):
            rows = pair_rows(place, accumulated, pair)
            out = mixed_keep if pair < PAIRS // 2 else mixed_send
            base = pair % (PAIRS // 2) * (JOINT - PIECE)
            third_rows = PAIR // 3
            out[base : base + PAIR, :] = rows[:, :TAPS].astype(out.dtype)
            out[base + PAIR : base + PAIR + third_rows, :] = jnp.concatenate(
                [rows[part * third_rows : (part + 1) * third_rows, TAPS:] for part in range(3)],
                axis=1,
            ).astype(out.dtype)


def filter_kernel(place, grads, stacks, mixed, *refs):
    outs, grad_stack = refs[:-1], refs[-1]
    stack_gradients(grads, grad_stack)
    both = jnp.concatenate([stack[...] for stack in stacks], axis=1)
    total = dot(both, grad_stack[...], NT)
    extra = JOINT - PIECE
    for part, out in enumerate(outs):
        rows = slice(part * extra, (part + 1) * extra)
        out[:PIECE, :] = total[part * PIECE : (part + 1) * PIECE].astype(out.dtype)
        out[PIECE:, :] = (mixed[0][rows, :] + mixed[1][rows, :].astype(WIDE)).astype(out.dtype)


def own_filter_kernel(place, grads, stacks, send_out, keep_out, grad_stack):
    stack_gradients([grads], grad_stack)
    send_out[...] = dot(stacks[1][...], grad_stack[...], NT).astype(LOW)
    keep_out[...] = dot(stacks[0][...], grad_stack[...], NT)


def split_kernel(place, keep, received, *outs):
    for part, out in enumerate(outs):
        rows = slice(part * PIECE, (part + 1) * PIECE)
        out[...] = (keep[rows, :] + received[rows, :].astype(WIDE)).astype(out.dtype)


def conv_back(place, grads, weight, grad_stack, product, value):
    stack_gradient(grads.at[0], grad_stack)
    product[...] = dot(weight[...], grad_stack[...], NN)
    back_to_channels(place, product, value)


def second_back_kernel(
    place,
    grads,
    weight,
    normed_ref,
    stats_first,
    stats,
    mask_ref,
    params,
    member,
    first_grad_out,
    small_out,
    grad_stack,
    product,
    value,
):
    conv_back(place, grads, weight, grad_stack, product, value)
    mask = mask_ref[0]
    count = count_of(mask)
    gain, bias = params[:, 2:3], params[:, 3:4]
    factor = stats_first[0, :, 0:1]
    time_scale, time_shift = 1.0 + stats[0, :, 2:3], stats[0, :, 3:4]
    normed = normed_ref[0]
    hidden = (normed * gain + bias) * time_scale + time_shift
    delta = value[...] * mask * silu_slope(hidden)
    value[...] = delta
    plain = jnp.sum(delta, axis=1, keepdims=True)
    weighted = jnp.sum(delta * normed, axis=1, keepdims=True)
    scaled = gain * time_scale
    sums = group_sums(member[...], lane_pair(scaled * plain, scaled * weighted))
    first_sum, second_sum = sums[:, 0:1] / count, sums[:, 1:2] / count
    first_grad_out[0] = (
        factor * (value[...] * scaled - mask * (first_sum + normed * second_sum))
    ).astype(LOW)
    small_out[0] = small_rows(
        (
            time_scale * weighted,
            time_scale * plain,
            gain * weighted + bias * plain,
            plain,
        )
    )


def first_back_kernel(place, *refs):
    (
        grads,
        weight,
        whole,
        stats_first,
        residual_grad,
        mask_ref,
        params,
        member,
        small_in,
        keep_out,
        send_out,
        small_out,
        grad_stack,
        product,
        value,
    ) = refs[-15:]
    conv_back(place, grads, weight, grad_stack, product, value)
    own, other = half_offsets(place)
    mask = mask_ref[0]
    count = count_of(mask)
    gain, bias = params[:, 0:1], params[:, 1:2]
    mean, factor = stats_first[0, :, 0:1], stats_first[0, :, 1:2]
    normed = (whole[0].astype(WIDE) - mean) * factor
    hidden = normed * gain + bias
    delta = value[...] * mask * silu_slope(hidden)
    value[...] = delta
    plain = jnp.sum(delta, axis=1, keepdims=True)
    weighted = jnp.sum(delta * normed, axis=1, keepdims=True)
    sums = group_sums(member[...], lane_pair(gain * plain, gain * weighted))
    first_sum, second_sum = sums[:, 0:1] / count, sums[:, 1:2] / count
    value[...] = residual_grad[0] + factor * (
        value[...] * gain - mask * (first_sum + normed * second_sum)
    )
    keep_out[0] = value[pl.ds(own, HALF), :]
    send_out[0] = value[pl.ds(other, HALF), :].astype(LOW)
    rows = small_rows((weighted, plain))
    if len(small_in) == 0:
        small_out[...] = rows
    else:
        earlier, second, third, steps = small_in
        for ref in earlier:
            rows = rows + ref[...]
        images = second.shape[0]
        second_sum, third_sum = second[0], third[0]
        for image in range(1, images):
            second_sum, third_sum = second_sum + second[image], third_sum + third[image]
        small_out[:8, :] = set_rows(
            [
                rows[0:1],
                second_sum[0:1],
                third_sum[0:1],
                rows[1:2],
                second_sum[1:2],
                third_sum[1:2],
            ],
            8,
        )
        small_out[8:, :] = set_rows(
            [second[image, 2 + kind : 3 + kind] for kind in range(2) for image in range(images)]
            + [steps[0:1]],
            8,
        )


def cut_kernel(place, own, one, two, three, mine_out, side_out, far_out, corner_out):
    total = own[...] + one[...].astype(WIDE) + two[...].astype(WIDE) + three[...].astype(WIDE)
    left = place[BLOCKS] == 0
    outs = ((mine_out, side_out), (far_out, corner_out))
    for part in range(2):
        rows = jnp.concatenate(
            [total[tap * PAIR + part * ROWS : tap * PAIR + (part + 1) * ROWS] for tap in range(3)],
            axis=0,
        )
        halves = [rows[:, : 3 * HALF], rows[:, 3 * HALF :]]
        here, away = outs[part]
        here[...] = jnp.where(left, halves[0], halves[1]).astype(here.dtype)
        away[...] = jnp.where(left, halves[1], halves[0]).astype(away.dtype)


def unpack(rows, columns):
    return jnp.concatenate(
        [rows[:, third * columns : (third + 1) * columns] for third in range(3)], axis=0
    )


def pack(rows):
    count = rows.shape[0] // 3
    return jnp.concatenate(
        [rows[third * count : (third + 1) * count] for third in range(3)], axis=1
    )


def cut_columns_kernel(place, own, one, two, three, mine_out, side_out):
    total = own[...] + one[...].astype(WIDE) + two[...].astype(WIDE) + three[...].astype(WIDE)
    left = place[BLOCKS] == 0
    wide, output = total[: PIECE + PAIR], unpack(total[PIECE + PAIR :], C)
    halves = [
        jnp.concatenate(
            [
                wide[:, half * 3 * HALF : (half + 1) * 3 * HALF],
                pack(output[:, half * HALF : (half + 1) * HALF]),
            ],
            axis=0,
        )
        for half in range(2)
    ]
    mine_out[...] = jnp.where(left, halves[0], halves[1])
    side_out[...] = jnp.where(left, halves[1], halves[0]).astype(LOW)


def cut_rows_kernel(place, own, received, near_out, far_out):
    total = own[...] + received[...].astype(WIDE)
    output = unpack(total[PIECE + PAIR :], HALF)
    for part, out in enumerate((near_out, far_out)):
        rows = [
            total[tap * PAIR + part * ROWS : tap * PAIR + (part + 1) * ROWS] for tap in range(4)
        ]
        rows.append(pack(output[part * ROWS : (part + 1) * ROWS]))
        out[...] = jnp.concatenate(rows, axis=0).astype(out.dtype)


def finish_kernel(place, own, received, filter_out, *mixed_outs):
    total = own[...]
    for ref in received:
        total = total + ref[...].astype(WIDE)
    for down in range(3):
        for across in range(3):
            filter_out[3 * down + across] = total[
                across * ROWS : (across + 1) * ROWS, down * HALF : (down + 1) * HALF
            ]
    if mixed_outs:
        mixed_outs[0][...] = total[3 * ROWS : 4 * ROWS]
        mixed_outs[1][...] = unpack(total[4 * ROWS :], HALF)


def receive_kernel(place, carried, received, out):
    for image, ref in enumerate(received):

        @pl.when(pl.program_id(0) == image)
        def _(ref=ref):
            out[...] = ref[...].astype(out.dtype)


def shape(*sizes, dtype=WIDE):
    return jax.ShapeDtypeStruct(sizes, dtype)


def per_image(*sizes, first=0):
    return pl.BlockSpec((1,) + sizes, lambda g, place: (first + g,) + (0,) * len(sizes))


def own_image(*sizes, first=0):
    return pl.BlockSpec(
        (1,) + sizes, lambda g, place: (place[BLOCKS + 1] + first + g,) + (0,) * len(sizes)
    )


def other_image(*sizes):
    return pl.BlockSpec(
        (1,) + sizes, lambda g, place: (place[BLOCKS + 2] + g,) + (0,) * len(sizes)
    )


def per_columns(*sizes, first=0):
    return pl.BlockSpec(sizes, lambda g, place: (0, first + g))


def fixed(*sizes):
    return pl.BlockSpec(sizes, lambda g, place: (0,) * len(sizes))


def whole_array(entry):
    return fixed(*entry.shape)


def run(kernel, place, images, ins, outs, scratch, aliases=None, room=24, cost=8):
    arrays, structure = jax.tree.flatten([array for array, _ in ins])
    specs = jax.tree.leaves(
        [spec for _, spec in ins], is_leaf=lambda entry: isinstance(entry, pl.BlockSpec)
    )

    def body(place, *refs):
        given = jax.tree.unflatten(structure, refs[: len(arrays)])
        kernel(place, *given, *refs[len(arrays) :])

    return pl.pallas_call(
        body,
        grid_spec=pltpu.PrefetchScalarGridSpec(
            num_scalar_prefetch=1,
            grid=(images,),
            in_specs=specs,
            out_specs=[spec for _, spec in outs],
            scratch_shapes=scratch,
        ),
        out_shape=[out for out, _ in outs],
        input_output_aliases=aliases or {},
        compiler_params=pltpu.CompilerParams(
            dimension_semantics=("arbitrary",), vmem_limit_bytes=room * 2**20
        ),
        cost_estimate=pl.CostEstimate(flops=cost * 10**9, bytes_accessed=2**20, transcendentals=0),
    )(place, *arrays)


def filter_gradient(place, stacks, grads, mixed):
    images = sum(grad.shape[0] for grad in grads)
    ins = (grads, stacks, mixed)
    outs = [shape(JOINT, TAPS)] + [shape(JOINT, TAPS, dtype=LOW)] * 3
    return run(
        filter_kernel,
        place,
        1,
        [(entry, jax.tree.map(whole_array, entry)) for entry in ins],
        [(out, whole_array(out)) for out in outs],
        [pltpu.VMEM((TAPS, images * PIX), LOW)],
        room=40,
    )


def own_filter_gradient(place, stacks, grads):
    ins = (grads, stacks)
    outs = [shape(TAPS // 2, TAPS, dtype=LOW), shape(TAPS // 2, TAPS)]
    return run(
        own_filter_kernel,
        place,
        1,
        [(entry, jax.tree.map(whole_array, entry)) for entry in ins],
        [(out, whole_array(out)) for out in outs],
        [pltpu.VMEM((TAPS, grads.shape[0] * PIX), LOW)],
        room=32,
        cost=1,
    )


def simple(kernel, place, ins, outs, cost):
    return run(
        kernel,
        place,
        1,
        [(entry, jax.tree.map(whole_array, entry)) for entry in ins],
        [(out, whole_array(out)) for out in outs],
        [],
        cost=cost,
    )


def on_device(
    dp,
    features,
    pixel_masks,
    timesteps,
    first_filter,
    second_filter,
    project_weight,
    output_weight,
    embed_weight,
    norm_gains,
    norm_biases,
    cotangent,
):
    chan = lax.axis_index("chan")
    left = chan == 0
    span = dp // BLOCKS
    groups = [list(range(k * span, (k + 1) * span)) for k in range(BLOCKS)]
    block = lax.axis_index("dp") // span
    images = features.shape[0] // 2

    def swap(value, mask, flip):
        pairs = [
            (2 * d + x, 2 * (d ^ (mask * span)) + (x ^ flip)) for d in range(dp) for x in range(2)
        ]
        return lax.ppermute(value, ("dp", "chan"), pairs)

    def near(value, axis):
        if span == 1:
            return value
        return lax.all_gather(value, "dp", axis=axis, tiled=True, axis_index_groups=groups)

    def halves(mine, theirs, axis):
        return jnp.concatenate(
            [jnp.where(left, mine, theirs), jnp.where(left, theirs, mine)], axis=axis
        )

    def after(value, *others):
        return lax.optimization_barrier((value, others))[0]

    def pair_up(one, two):
        taps = one.shape[0] // ROWS
        columns = one.shape[1]
        both = [v.reshape(taps, ROWS, columns) for v in (one, two)]
        return jnp.stack(both, axis=1).reshape(2 * taps * ROWS, columns)

    def gather_one(shard, extra=None):
        side = swap(shard if extra is None else jnp.concatenate([shard, extra], axis=0), 0, 1)
        far = swap(shard, 8, 0)
        both = swap(shard, 8, 1)
        count = shard.shape[0]
        rows = pair_up(halves(shard, side[:count], 1), halves(far, both, 1))
        return rows if extra is None else (rows, side[count:])

    def gather_slow(shard, late):
        rows = after(pair_up(shard, swap(shard, 8, 0)), late)
        return halves(rows, swap(rows, 0, 1), 1)

    def gather_two(rows):
        return [rows, swap(rows, 4, 0), swap(rows, 2, 0), swap(rows, 6, 0)]

    def gather_three(pieces):
        return [swap(rows, 1, 0) for rows in pieces]

    def scatter_one(send, keep):
        outs = [shape(PIECE, TAPS)] + [shape(PIECE, TAPS, dtype=LOW)] * 3
        return simple(split_kernel, place, [keep, swap(send, 1, 0)], outs, 1)

    def scatter_two(keep, *sends):
        arrived = [swap(send, mask, 0) for send, mask in zip(sends, (4, 2, 6))]
        outs = [shape(3 * ROWS, 3 * HALF)] + [shape(3 * ROWS, 3 * HALF, dtype=LOW)] * 3
        return simple(cut_kernel, place, [keep] + arrived, outs, 30)

    def scatter_three(keep, *sends):
        arrived = [
            swap(send, mask, flip) for send, (mask, flip) in zip(sends, ((0, 1), (8, 0), (8, 1)))
        ]
        return simple(finish_kernel, place, [keep, arrived], [shape(9, ROWS, HALF)], 1)[0]

    def joint_two(keep, *sends, late):
        arrived = [swap(send, mask, 0) for send, mask in zip(sends, (4, 2, 6))]
        outs = [shape(JOINT, 3 * HALF), shape(JOINT, 3 * HALF, dtype=LOW)]
        return simple(cut_columns_kernel, place, [after(keep, late)] + arrived, outs, 30)

    def joint_three(keep, send, late):
        outs = [shape(JOINT // 2, 3 * HALF), shape(JOINT // 2, 3 * HALF, dtype=LOW)]
        ins = [after(keep, late), swap(send, 0, 1)]
        return simple(cut_rows_kernel, place, ins, outs, 1)

    def joint_four(keep, send, late):
        outs = [shape(9, ROWS, HALF), shape(ROWS, 3 * HALF), shape(ROWS, HALF)]
        ins = [after(keep, late), [swap(send, 8, 0)]]
        return simple(finish_kernel, place, ins, outs, 1)

    def share(value, dimension):
        if span == 1:
            return value
        return lax.psum_scatter(
            value, "dp", scatter_dimension=dimension, tiled=True, axis_index_groups=groups
        )

    def parts_of(value):
        high = value.astype(LOW)
        rest = value - high.astype(WIDE)
        middle = rest.astype(LOW)
        return [high, middle, (rest - middle.astype(WIDE)).astype(LOW)]

    own_start, other_start = chan * images, (1 - chan) * images

    def others(value):
        return lax.dynamic_slice_in_dim(value, other_start, images, 0)

    theirs = swap(others(features), 0, 1)

    def filter_rows(weight):
        rows = near(weight.astype(LOW), 1).reshape(3, 3, ROWS, HALF)
        return jnp.transpose(rows, (1, 2, 0, 3)).reshape(3 * ROWS, 3 * HALF)

    norms = jnp.concatenate([norm_gains, norm_biases], axis=0)
    norm_rows = jnp.pad(jnp.concatenate(parts_of(norms), axis=1), ((0, 2), (0, 0)))
    first_one, norm_rows = gather_one(filter_rows(first_filter), norm_rows)
    their_norms = norm_rows[:6].astype(WIDE).reshape(6, 3, HALF)
    their_norms = their_norms[:, 0] + their_norms[:, 1] + their_norms[:, 2]
    norms = halves(norms, their_norms, 1)
    params = jnp.stack([norms[0], norms[3], norms[1], norms[4], norms[2], norms[5]], axis=1)
    params = jnp.pad(params, ((0, 0), (0, 2)))
    first_pieces = gather_two(first_one)

    embed_rows = jnp.transpose(near(embed_weight.astype(LOW), 1), (1, 0, 2))
    embed_rows = jnp.transpose(embed_rows.reshape(PAIR, 3, 128), (1, 0, 2))
    embed_rows = embed_rows.reshape(2, 3 * ROWS, 128)
    second_rows = jnp.concatenate(
        [filter_rows(second_filter), embed_rows[0], embed_rows[1]], axis=1
    )
    bundle_rows = jnp.concatenate(
        [
            near(project_weight.astype(LOW), 0).reshape(ROWS, 3 * HALF),
            near(output_weight.astype(LOW), 1).T,
        ],
        axis=1,
    )
    second_one = gather_slow(second_rows, first_one)
    bundle_one = gather_slow(after(bundle_rows, theirs), second_one)
    first_pieces = first_pieces + gather_three(
        [after(first_pieces[0], theirs)] + first_pieces[1:]
    )

    validity = lax.dynamic_slice_in_dim(pixel_masks, own_start, images, 0).astype(WIDE)
    validity = validity.reshape(images, 1, PIX)
    member = (jnp.arange(C)[:, None] // WIDTH == jnp.arange(C)[None, :] // WIDTH).astype(LOW)
    order = jnp.array(ORDER, jnp.int32)
    place = jnp.concatenate(
        [
            jnp.bitwise_xor(block, order) * ROWS,
            jnp.stack([chan, own_start, other_start]).astype(jnp.int32),
        ]
    )

    def time_features(steps, index, embed_width):
        half_width = embed_width // 2
        power = jnp.where(index < half_width, index, index - half_width).astype(WIDE)
        frequency = jnp.exp(-math.log(10000.0) * power / half_width)
        angles = steps[:, None] * frequency[None, :]
        return jax.nn.silu(
            jnp.where(index[None, :] < half_width, jnp.cos(angles), jnp.sin(angles))
        )

    embed_width = embed_weight.shape[1] * dp
    own_steps = lax.dynamic_slice_in_dim(timesteps, own_start, images, 0).astype(WIDE)
    flat = jnp.arange(2 * 3 * ROWS)
    third, entry_row = flat // PAIR, flat % PAIR
    embed_index = (jnp.bitwise_xor(block, order)[:, None] * PAIR + entry_row).reshape(-1)
    embed_values = time_features(own_steps, embed_index, embed_width)
    embed_split = jnp.stack(parts_of(embed_values), axis=2)
    embed_split = embed_split.reshape(images, PAIRS, 2, 2, 3, ROWS, 3)
    embed_split = jnp.transpose(embed_split, (0, 3, 1, 4, 2, 5, 6))
    late = (third.reshape(2, 3, ROWS) == jnp.array([1, 2])[:, None, None])
    late = late[None, :, None, :, None, :, None]
    embed_parts = jnp.concatenate(
        [jnp.where(late, 0, embed_split), jnp.where(late, embed_split, 0)], axis=6
    ).reshape(images, 2, TAPS, 6)
    embed_parts = jnp.pad(embed_parts, ((0, 0), (0, 0), (0, 0), (0, 122)))
    steps_row = jnp.pad(own_steps, (0, HALF - images))
    steps_row = jnp.pad(jnp.concatenate([steps_row, steps_row])[None, :], ((0, 7), (0, 0)))

    value_scratch = pltpu.VMEM((C, PIX), WIDE)
    product_scratch = pltpu.VMEM((TAPS, PIX), WIDE)
    back_scratch = [pltpu.VMEM((TAPS, PIX), LOW), product_scratch, value_scratch]
    mask_in = (validity, per_image(1, PIX))
    params_in = (params, fixed(C, 8))
    member_in = (member, fixed(C, C))
    image_low = (shape(images, C, PIX, dtype=LOW), per_image(C, PIX))
    image_wide = (shape(images, C, PIX), per_image(C, PIX))
    image_small = (shape(images, C, 128), per_image(C, 128))
    image_rows = (shape(images, 8, C), per_image(8, C))
    weight_out = (shape(TAPS, TAPS, dtype=LOW), fixed(TAPS, TAPS))
    stack_out = (shape(TAPS // 2, images * PIX, dtype=LOW), per_columns(TAPS // 2, PIX))
    anywhere = pl.BlockSpec(memory_space=pl.ANY)

    prepared = run(
        prepare_kernel,
        place,
        images,
        [
            (features, own_image(HALF, PIX)),
            (theirs, per_image(HALF, PIX)),
            mask_in,
            params_in,
            member_in,
        ],
        [image_low, stack_out, stack_out, image_small],
        [value_scratch],
    )
    whole, first_low, first_high, stats_whole = prepared
    cots = others(cotangent)
    second_normed, stats_first, first_weight = run(
        first_kernel,
        place,
        images,
        [
            mask_in,
            member_in,
            (first_pieces, [fixed(PIECE, TAPS)] * 8),
            (after([first_low, first_high], second_one, cots), [per_columns(TAPS // 2, PIX)] * 2),
        ],
        [image_wide, image_small, weight_out],
        [value_scratch, product_scratch],
    )
    second_pieces = gather_two(second_one)
    second_pieces = second_pieces + gather_three(after(second_pieces, second_normed))
    bundle_pieces = gather_two(bundle_one)
    their_cots = swap(after(cots, second_normed), 0, 1)
    second_low, second_high, residual, attend_input, stats_second, second_weight = run(
        second_kernel,
        place,
        images,
        [
            (after(second_normed, bundle_one), per_image(C, PIX)),
            (whole, per_image(C, PIX)),
            (embed_parts, per_image(2, TAPS, 128)),
            mask_in,
            params_in,
            member_in,
            (second_pieces, [fixed(PIECE, 2 * SECOND)] * 8),
        ],
        [stack_out, stack_out, image_wide, image_low, image_small, weight_out],
        [pltpu.VMEM((2, 2, TAPS, 128), LOW), value_scratch, product_scratch],
        room=60,
    )
    bundle_pieces = bundle_pieces + gather_three(after(bundle_pieces, attend_input))
    second_theirs = swap(second_high, 1, 0)
    mixed_rows = PAIRS // 2 * (JOINT - PIECE)
    block_keep, block_send, residual_grad, second_grad, *mixed, small_third = run(
        attend_kernel,
        place,
        images,
        [
            (attend_input, per_image(C, PIX)),
            (residual, per_image(C, PIX)),
            (stats_second, per_image(C, 128)),
            (cotangent, own_image(HALF, PIX)),
            (their_cots, per_image(HALF, PIX)),
            mask_in,
            params_in,
            member_in,
            (bundle_pieces, [fixed(PAIR, 2 * MIXED)] * 8),
        ],
        [
            (shape(2 * images, HALF, PIX, dtype=LOW), own_image(HALF, PIX)),
            (shape(images, HALF, PIX, dtype=LOW), per_image(HALF, PIX)),
            image_wide,
            image_low,
            (shape(mixed_rows, TAPS), fixed(mixed_rows, TAPS)),
            (shape(mixed_rows, TAPS, dtype=LOW), fixed(mixed_rows, TAPS)),
            image_rows,
        ],
        [
            pltpu.VMEM((2, C, 2 * C), WIDE),
            pltpu.VMEM((C, TAPS), LOW),
            pltpu.VMEM((C, C), LOW),
            pltpu.VMEM((C, PIX), LOW),
            pltpu.VMEM((TAPS, PIX), LOW),
            pltpu.VMEM((C, PIX), LOW),
            pltpu.VMEM((C, PIX), LOW),
            pltpu.VMEM((TAPS, PIX), LOW),
            pltpu.VMEM((PIX, KEYS), LOW),
            pltpu.VMEM((PIX, KEYS), LOW),
            pltpu.VMEM((HEAD + 16, PIX), LOW),
            pltpu.VMEM((KEYS, PIX), LOW),
            pltpu.VMEM((KEYS, PIX), LOW),
            pltpu.VMEM((PIX, PIX), WIDE),
            pltpu.VMEM((PIX, PIX), LOW),
            pltpu.VMEM((PIX, PIX), LOW),
            pltpu.VMEM((C, TAPS + C), WIDE),
            value_scratch,
        ],
        room=62,
        cost=60,
    )
    block_theirs = swap(block_send, 0, 1)
    mixed = [mixed[0], swap(mixed[1], 1, 0)]
    grads_theirs = swap(second_grad, 1, 0)
    joint = filter_gradient(
        place, [second_low, second_theirs], [second_grad, grads_theirs], mixed
    )
    first_grad, small_second = run(
        second_back_kernel,
        place,
        images,
        [
            (after(second_grad, joint), per_image(C, PIX)),
            (second_weight, fixed(TAPS, TAPS)),
            (second_normed, per_image(C, PIX)),
            (stats_first, per_image(C, 128)),
            (stats_second, per_image(C, 128)),
            mask_in,
            params_in,
            member_in,
        ],
        [image_low, image_rows],
        back_scratch,
    )
    masked_out = lax.dynamic_update_slice_in_dim(
        after(block_keep, joint), block_theirs, other_start, 0
    )
    send, keep = own_filter_gradient(
        place, [first_low, first_high], after(first_grad, masked_out)
    )
    first_part = scatter_one(send, keep)
    joint = joint_two(*joint, late=send)
    input_grad, input_theirs, smalls = None, [], []
    back_grad = after(first_grad, first_part, joint)
    for image in range(images):
        last = image == images - 1
        small_in = (smalls, small_second, small_third, steps_row) if last else ()
        carried = [] if input_grad is None else [(input_grad, anywhere)]
        small_shape = shape(16 if last else 8, C)
        input_grad, input_send, small = run(
            first_back_kernel,
            place,
            1,
            carried
            + [
                (back_grad, per_image(C, PIX, first=image)),
                (first_weight, fixed(TAPS, TAPS)),
                (whole, per_image(C, PIX, first=image)),
                (stats_whole, per_image(C, 128, first=image)),
                (residual_grad, per_image(C, PIX, first=image)),
                (validity, per_image(1, PIX, first=image)),
                params_in,
                member_in,
                (small_in, jax.tree.map(whole_array, small_in)),
            ],
            [
                (shape(2 * images, HALF, PIX), own_image(HALF, PIX, first=image)),
                (shape(1, HALF, PIX, dtype=LOW), per_image(HALF, PIX)),
                (small_shape, whole_array(small_shape)),
            ],
            back_scratch,
            {1: 0} if carried else None,
        )
        smalls.append(small)
        input_theirs.append(swap(input_send, 0, 1))
        if image == 0:
            joint = joint_three(*joint, late=small)
            back_grad = after(back_grad, joint)
    first_part = scatter_two(*first_part)
    message = after(smalls[-1], input_theirs[:-1])

    def merge(arrived):
        total = sum(message[:8] for message in arrived)
        return jnp.concatenate([total] + [message[8:] for message in arrived], axis=0)

    message = after(merge([message, swap(message, 1, 0)]), first_part)
    joint = joint_four(*joint, late=first_part)
    grad_first = share(scatter_three(*first_part), 1)
    grad_second = share(joint[0], 1)
    grad_project = share(joint[1].reshape(ROWS, 3, HALF), 0)
    grad_output = share(joint[2].T, 1)
    (input_grad,) = run(
        receive_kernel,
        place,
        images,
        [(input_grad, anywhere), (input_theirs, [fixed(1, HALF, PIX)] * images)],
        [(shape(2 * images, HALF, PIX), other_image(HALF, PIX))],
        [],
        {1: 0},
        cost=1,
    )

    message = merge([message] + [swap(message, m, 0) for m in (4, 2, 6)])
    one, two = after(message[:, :HALF], input_theirs[-1]), message[:, HALF:]
    own, away = jnp.where(left, one, two), jnp.where(left, two, one)
    message = merge([own, swap(away, 0, 1), swap(own, 8, 0), swap(away, 8, 1)])
    total, entries = message[:6], message[8:]
    if span > 1:
        total = lax.psum(total, "dp", axis_index_groups=groups)
        entries = lax.all_gather(entries, "dp", axis=0, tiled=True, axis_index_groups=groups)
    entries = entries.reshape(-1, 8, HALF)
    all_steps = entries[:, 2 * images, :images].reshape(-1)
    scale_grads = entries[:, :images].reshape(-1, HALF)
    shift_grads = entries[:, images : 2 * images].reshape(-1, HALF)
    rows = embed_weight.shape[1]
    row_index = lax.axis_index("dp") * rows + jnp.arange(rows)
    all_embed = time_features(all_steps, row_index, embed_width)
    grad_embed = jnp.einsum(
        "be,kbd->ked",
        all_embed,
        jnp.stack([scale_grads, shift_grads]),
        precision=lax.Precision.HIGHEST,
    )
    return (
        masked_out,
        input_grad,
        grad_first,
        grad_second,
        grad_project,
        grad_output,
        grad_embed,
        total[:3],
        total[3:],
    )


def solution(mesh):
    in_specs = (
        P("dp", "chan", None),
        P("dp", None),
        P("dp"),
        P(None, "dp", "chan"),
        P(None, "dp", "chan"),
        P("dp", None, "chan"),
        P("chan", "dp"),
        P(None, "dp", "chan"),
        P(None, "chan"),
        P(None, "chan"),
        P("dp", "chan", None),
    )
    out_specs = (
        P("dp", "chan", None),
        P("dp", "chan", None),
        P(None, "dp", "chan"),
        P(None, "dp", "chan"),
        P("dp", None, "chan"),
        P("chan", "dp"),
        P(None, "dp", "chan"),
        P(None, "chan"),
        P(None, "chan"),
    )
    return jax.shard_map(
        functools.partial(on_device, mesh.shape["dp"]),
        mesh=mesh,
        in_specs=in_specs,
        out_specs=out_specs,
        check_vma=False,
    )
```

```python
import functools
import math

import jax
import jax.numpy as jnp
from jax import lax
from jax.experimental import pallas as pl
from jax.experimental.pallas import tpu as pltpu
from jax.sharding import PartitionSpec as P

C = 384
HALF = 192
HEAD = 64
GROUPS = 32
WIDTH = C // GROUPS
SIDE = 32
PIX = SIDE * SIDE
BLOCKS = 16
ROWS = C // BLOCKS
TAPS = 3 * C
EPSILON = 1e-05
SECOND = 3 * HALF + 256
MIXED = 4 * HALF
PACKED = MIXED // 3
PAIR = 2 * ROWS
PIECE = 3 * PAIR
JOINT = PIECE + PAIR + PAIR // 3
PAIRS = BLOCKS // 2
KEYS = 128
CHUNK = 256
LOW = jnp.bfloat16
WIDE = jnp.float32
ORDER = (0, 8, 4, 12, 2, 10, 6, 14, 1, 9, 5, 13, 3, 11, 7, 15)

NN = (((1,), (0,)), ((), ()))
NT = (((1,), (1,)), ((), ()))
TN = (((0,), (0,)), ((), ()))


def dot(left, right, dims):
    return lax.dot_general(left, right, dims, preferred_element_type=WIDE)


def pixel_row(keep):
    pixel = lax.broadcasted_iota(jnp.int32, (1, PIX), 1)
    return jnp.where(keep(pixel), 1.0, 0.0).astype(LOW)


def lane_pair(first, second):
    lane = lax.broadcasted_iota(jnp.int32, (C, 128), 1)
    return jnp.where(lane == 0, first, jnp.where(lane == 1, second, 0.0))


def group_sums(member, values):
    high = values.astype(LOW)
    rest = values - high.astype(WIDE)
    middle = rest.astype(LOW)
    low = (rest - middle.astype(WIDE)).astype(LOW)
    return dot(member, high, NN) + dot(member, middle, NN) + dot(member, low, NN)


def group_sum(member, column):
    return group_sums(member, jnp.broadcast_to(column, (C, 128)))[:, 0:1]


def group_stats(value_ref, member, mask, count):
    mean = group_sum(member, jnp.sum(value_ref[...] * mask, axis=1, keepdims=True)) / count
    centred = value_ref[...] - mean
    variance = (
        group_sum(member, jnp.sum(centred * centred * mask, axis=1, keepdims=True)) / count
    )
    return mean, lax.rsqrt(variance + EPSILON)


def silu(value):
    return value / (1.0 + jnp.exp(-value))


def silu_slope(value):
    squashed = 1.0 / (1.0 + jnp.exp(-value))
    return squashed * (1.0 + value * (1.0 - squashed))


def shift_down(piece):
    pixel = lax.broadcasted_iota(jnp.int32, piece.shape, 1)
    return jnp.where(pixel < SIDE, 0.0, pltpu.roll(piece, SIDE, 1))


def shift_up(piece):
    pixel = lax.broadcasted_iota(jnp.int32, piece.shape, 1)
    return jnp.where(pixel >= PIX - SIDE, 0.0, pltpu.roll(piece, PIX - SIDE, 1))


def conv_out(product_ref, chan):
    base = chan * 3 * HALF
    return (
        product_ref[base + HALF : base + 2 * HALF, :]
        + shift_down(product_ref[base : base + HALF, :])
        + shift_up(product_ref[base + 2 * HALF : base + 3 * HALF, :])
    )


def stack_gradient(grad_ref, out_ref):
    not_top = pixel_row(lambda pixel: pixel >= SIDE)
    not_bottom = pixel_row(lambda pixel: pixel < PIX - SIDE)
    for chan in range(2):
        piece = grad_ref[chan * HALF : (chan + 1) * HALF, :]
        base = chan * 3 * HALF
        out_ref[base : base + HALF, :] = pltpu.roll(piece, PIX - SIDE, 1) * not_bottom
        out_ref[base + HALF : base + 2 * HALF, :] = piece
        out_ref[base + 2 * HALF : base + 3 * HALF, :] = pltpu.roll(piece, SIDE, 1) * not_top


def stack_gradients(grads, out_ref):
    at = 0
    for ref in grads:
        for image in range(ref.shape[0]):
            stack_gradient(ref.at[image], out_ref.at[:, at * PIX : (at + 1) * PIX])
            at += 1


def block_offset(place_ref, position):
    return pl.multiple_of(place_ref[position], 8)


def pair_rows(place, ref, pair):
    return jnp.concatenate(
        [ref[pl.ds(block_offset(place, 2 * pair + part), ROWS), :] for part in range(2)], axis=0
    )


def side_shifts(piece, out, base):
    not_left = pixel_row(lambda pixel: pixel % SIDE != 0)
    not_right = pixel_row(lambda pixel: pixel % SIDE != SIDE - 1)
    rows = piece.shape[0]
    out[base : base + rows, :] = pltpu.roll(piece, 1, 1) * not_left
    out[base + rows : base + 2 * rows, :] = piece
    out[base + 2 * rows : base + 3 * rows, :] = pltpu.roll(piece, PIX - 1, 1) * not_right


def build_stack(place, value, mask, stacks, inputs=None):
    for pair in range(PAIRS):
        piece = (silu(pair_rows(place, value, pair)) * mask).astype(LOW)
        half, at = pair // (PAIRS // 2), pair % (PAIRS // 2)
        side_shifts(piece, stacks[half], at * PIECE)
        if inputs is not None:
            inputs[half][at * PAIR : (at + 1) * PAIR, :] = piece


def back_to_channels(place_ref, product_ref, out_ref):
    column = lax.broadcasted_iota(jnp.int32, (PAIR, PIX), 1) & (SIDE - 1)
    for pair in range(PAIRS):
        base = pair * PIECE
        first = product_ref[base : base + PAIR, :]
        middle = product_ref[base + PAIR : base + 2 * PAIR, :]
        last = product_ref[base + 2 * PAIR : base + 3 * PAIR, :]
        total = (
            middle
            + jnp.where(column == SIDE - 1, 0.0, pltpu.roll(first, PIX - 1, 1))
            + jnp.where(column == 0, 0.0, pltpu.roll(last, 1, 1))
        )
        for part in range(2):
            out_ref[pl.ds(block_offset(place_ref, 2 * pair + part), ROWS), :] = total[
                part * ROWS : (part + 1) * ROWS
            ]


def count_of(mask):
    return jnp.maximum(jnp.sum(mask, axis=1, keepdims=True), 1.0) * float(WIDTH)


def small_columns(columns):
    lane = lax.broadcasted_iota(jnp.int32, (C, 128), 1)
    result = jnp.zeros((C, 128), WIDE)
    for index, column in enumerate(columns):
        result = jnp.where(lane == index, column, result)
    return result


def small_rows(columns):
    return small_columns(columns).T[:8]


def set_rows(rows, count):
    index = lax.broadcasted_iota(jnp.int32, (count, rows[0].shape[1]), 0)
    result = jnp.zeros((count, rows[0].shape[1]), WIDE)
    for at, row in enumerate(rows):
        result = jnp.where(index == at, row, result)
    return result


def three_parts(value):
    high = value.astype(LOW).astype(WIDE)
    rest = value - high
    middle = rest.astype(LOW).astype(WIDE)
    return [high, middle, rest - middle]


def load_weight(weight, pieces):
    @pl.when(pl.program_id(0) == 0)
    def _():
        for index, source in enumerate(pieces):
            weight[index * PIECE : (index + 1) * PIECE, :] = source[...]


def load_second(weight, weight_e, pieces):
    @pl.when(pl.program_id(0) == 0)
    def _():
        for index, source in enumerate(pieces):
            rows = slice(index * PIECE, (index + 1) * PIECE)
            for chan in range(2):
                base = chan * SECOND
                weight[rows, chan * 3 * HALF : (chan + 1) * 3 * HALF] = source[
                    :, base : base + 3 * HALF
                ]
                for part in range(0 if weight_e is None else 2):
                    lane = base + 3 * HALF + part * 128
                    weight_e[chan, part, rows, :] = source[:, lane : lane + 128]


def both_rows(stacks):
    return jnp.concatenate([stack[...] for stack in stacks], axis=0)


def half_offsets(place):
    own = pl.multiple_of(place[BLOCKS] * HALF, HALF)
    other = pl.multiple_of((1 - place[BLOCKS]) * HALF, HALF)
    return own, other


def prepare_kernel(
    place,
    mine,
    theirs,
    mask_ref,
    params,
    member,
    whole_out,
    low_out,
    high_out,
    stats_out,
    value,
):
    own, other = half_offsets(place)
    value[pl.ds(own, HALF), :] = mine[0].astype(WIDE)
    value[pl.ds(other, HALF), :] = theirs[0].astype(WIDE)
    mask = mask_ref[0]
    whole_out[0] = value[...].astype(LOW)
    mean, factor = group_stats(value, member[...], mask, count_of(mask))
    stats_out[0] = small_columns((mean, factor))
    scale = factor * params[:, 0:1]
    value[...] = (value[...] - mean) * scale + params[:, 1:2]
    build_stack(place, value, mask, (low_out, high_out))


def first_kernel(
    place,
    mask_ref,
    member,
    pieces,
    stacks,
    normed_out,
    stats_out,
    weight,
    value,
    product,
):
    load_weight(weight, pieces)
    mask = mask_ref[0]
    product[...] = dot(weight[...], both_rows(stacks), TN)
    for chan in range(2):
        value[chan * HALF : (chan + 1) * HALF, :] = conv_out(product, chan)
    mean, factor = group_stats(value, member[...], mask, count_of(mask))
    normed_out[0] = (value[...] - mean) * factor
    stats_out[0] = small_columns((factor,))


def second_kernel(
    place,
    normed,
    whole,
    embed_in,
    mask_ref,
    params,
    member,
    pieces,
    low_out,
    high_out,
    residual_out,
    stats_out,
    weight,
    weight_e,
    value,
    stack,
    product,
):
    load_second(weight, weight_e, pieces)
    mask = mask_ref[0]
    count = count_of(mask)
    image = pl.program_id(0)

    def own_columns(sums):
        return jnp.where(image == 0, sums[:, :6], sums[:, 6:12])

    scales, shifts = [], []
    for chan in range(2):
        low = own_columns(dot(weight_e[chan, 0], embed_in[0], TN))
        high = own_columns(dot(weight_e[chan, 1], embed_in[1], TN))
        column = jnp.concatenate(
            [
                low[:, 0:1] + low[:, 1:2] + low[:, 2:3],
                low[:, 3:4] + low[:, 4:5] + low[:, 5:6] + high[:, 0:1] + high[:, 1:2] + high[:, 2:3],
                high[:, 3:4] + high[:, 4:5] + high[:, 5:6],
            ],
            axis=0,
        )
        scales.append(column[:HALF])
        shifts.append(column[HALF:])
    time_scale = jnp.concatenate(scales, axis=0)
    time_shift = jnp.concatenate(shifts, axis=0)
    affine = normed[0] * params[:, 2:3] + params[:, 3:4]
    value[...] = affine * (1.0 + time_scale) + time_shift
    middle = TAPS // 2
    stacks = (stack.at[:middle, :], stack.at[middle:, :])
    build_stack(place, value, mask, stacks, (low_out, high_out))
    product[...] = dot(weight[...], stack[...], TN)
    for chan in range(2):
        rows = slice(chan * HALF, (chan + 1) * HALF)
        value[rows, :] = whole[0, rows, :].astype(WIDE) + conv_out(product, chan)
    residual_out[0] = value[...]
    mean, factor = group_stats(value, member[...], mask, count)
    stats_out[0] = small_columns((mean, factor, time_scale, time_shift))


def attend_kernel(
    place,
    residual,
    stats,
    mine,
    theirs,
    mask_ref,
    params,
    member,
    bundle,
    block_out,
    send_out,
    second_grad_out,
    mixed_keep,
    mixed_send,
    small_out,
    weight_f,
    attend_in,
    project,
    output,
    gradient,
    projected,
    attend_grad,
    attended,
    projected_grad,
    key_side,
    value_side,
    value_rows,
    query_side,
    grad_side,
    scores,
    probs,
    score_grads,
    accumulated,
    value,
):
    image = pl.program_id(0)

    @pl.when(image == 0)
    def _():
        for chan in range(2):
            for pair in range(PAIRS):
                block = bundle[pair][:, chan * PACKED : (chan + 1) * PACKED].astype(WIDE)
                for part in range(2):
                    for third in range(3):
                        first = third * PAIR + part * ROWS
                        weight_f[
                            chan,
                            pl.ds(block_offset(place, 2 * pair + part), ROWS),
                            third * PACKED : (third + 1) * PACKED,
                        ] = block[first : first + ROWS]
        project[...] = jnp.concatenate(
            [weight_f[0, :, : 3 * HALF], weight_f[1, :, : 3 * HALF]], axis=1
        ).astype(LOW)
        output[...] = jnp.concatenate(
            [weight_f[0, :, 3 * HALF :], weight_f[1, :, 3 * HALF :]], axis=1
        ).astype(LOW)
        accumulated[...] = jnp.zeros_like(accumulated)

    own, other = half_offsets(place)
    mask = mask_ref[0]
    count = count_of(mask)
    gradient[pl.ds(own, HALF), :] = (mine[0].astype(WIDE) * mask).astype(LOW)
    gradient[pl.ds(other, HALF), :] = (theirs[0].astype(WIDE) * mask).astype(LOW)
    mean, factor = stats[0, :, 0:1], stats[0, :, 1:2]
    scale = factor * params[:, 4:5]
    attend_in[...] = ((residual[0] - mean) * scale + params[:, 5:6]).astype(LOW)
    projected[...] = dot(project[...], attend_in[...], TN).astype(LOW)
    attend_grad[...] = dot(output[...], gradient[...], TN).astype(LOW)

    penalty = mask - 1.0
    one = jnp.ones((1, PIX), WIDE)
    fill = jnp.zeros((KEYS - HEAD - 16, PIX), LOW)
    key_rows = jnp.concatenate(
        [set_rows([penalty * 9984.0, penalty * 16.0], 16).astype(LOW), fill], axis=0
    )
    one_rows = jnp.concatenate([set_rows([one, one, one], 16).astype(LOW), fill], axis=0)
    query_side[HEAD:, :] = one_rows
    grad_side[HEAD:, :] = jnp.zeros((KEYS - HEAD, PIX), LOW)

    def one_head(head, carry):
        chan = head // 3
        row_q = pl.multiple_of(chan * (3 * HALF) + (head - 3 * chan) * HEAD, HEAD)
        row_k = pl.multiple_of(row_q + HALF, HEAD)
        row_v = pl.multiple_of(row_q + 2 * HALF, HEAD)
        row_o = pl.multiple_of(head * HEAD, HEAD)
        queries = projected[pl.ds(row_q, HEAD), :]
        keys = projected[pl.ds(row_k, HEAD), :]
        values = jnp.concatenate([projected[pl.ds(row_v, HEAD), :], one_rows], axis=0)
        grads = attend_grad[pl.ds(row_o, HEAD), :].astype(WIDE)
        key_side[...] = jnp.concatenate([keys, key_rows], axis=0).T
        value_rows[...] = values[: HEAD + 16]
        value_side[...] = values.T
        query_side[:HEAD, :] = (queries.astype(WIDE) * HEAD**-0.5).astype(LOW)
        peak = None
        for start in range(0, PIX, CHUNK):
            part = dot(key_side[start : start + CHUNK, :], query_side[...], NN)
            scores[start : start + CHUNK, :] = part
            highest = jnp.max(part.reshape(CHUNK // 8, 8, PIX), axis=0)
            peak = highest if peak is None else jnp.maximum(peak, highest)
        peak = jnp.max(peak, axis=0, keepdims=True)
        for start in range(0, PIX, CHUNK):
            span = slice(start, start + CHUNK)
            probs[span, :] = jnp.exp(scores[span, :] - peak).astype(LOW)
        result = dot(value_rows[...], probs[...], NN)
        inverse = 1.0 / result[HEAD : HEAD + 1, :]
        result = result[:HEAD, :] * inverse
        attended[pl.ds(row_o, HEAD), :] = result.astype(LOW)
        scaled = grads * inverse
        delta = jnp.sum(scaled * result, axis=0, keepdims=True)
        grad_side[:HEAD, :] = scaled.astype(LOW)
        grad_side[HEAD : HEAD + 16, :] = set_rows(three_parts(-delta), 16).astype(LOW)
        for start in range(0, PIX, CHUNK):
            span = slice(start, start + CHUNK)
            part = dot(value_side[span, :], grad_side[...], NN)
            score_grads[span, :] = (probs[span, :].astype(WIDE) * part).astype(LOW)
        projected_grad[pl.ds(row_q, HEAD), :] = (
            dot(keys, score_grads[...], NN) * HEAD**-0.5
        ).astype(LOW)
        projected_grad[pl.ds(row_k, HEAD), :] = (
            dot(queries, score_grads[...], NT) * HEAD**-0.5
        ).astype(LOW)
        projected_grad[pl.ds(row_v, HEAD), :] = dot(grad_side[:HEAD, :], probs[...], NT).astype(
            LOW
        )
        return carry

    lax.fori_loop(0, C // HEAD, one_head, 0, unroll=3)

    value[...] = (residual[0] + dot(output[...], attended[...], NN)) * mask
    block_out[0] = value[pl.ds(own, HALF), :].astype(LOW)
    send_out[0] = value[pl.ds(other, HALF), :].astype(LOW)
    accumulated[:, TAPS:] += dot(gradient[...], attended[...], NT)
    accumulated[:, :TAPS] += dot(attend_in[...], projected_grad[...], NT)
    third = dot(project[...], projected_grad[...], NN)
    normed = (residual[0] - mean) * factor
    bias_third = jnp.sum(third, axis=1, keepdims=True)
    gain_third = jnp.sum(third * normed, axis=1, keepdims=True)
    gain = params[:, 4:5]
    sums = group_sums(member[...], lane_pair(gain * bias_third, gain * gain_third))
    first_sum, second_sum = sums[:, 0:1] / count, sums[:, 1:2] / count
    total = gradient[...].astype(WIDE) + factor * (
        third * gain - mask * (first_sum + normed * second_sum)
    )
    second_grad_out[0] = total.astype(LOW)
    small_out[0] = small_rows((gain_third, bias_third))

    @pl.when(image == pl.num_programs(0) - 1)
    def _():
        for pair in range(PAIRS):
            rows = pair_rows(place, accumulated, pair)
            out = mixed_keep if pair < PAIRS // 2 else mixed_send
            base = pair % (PAIRS // 2) * (JOINT - PIECE)
            third_rows = PAIR // 3
            out[base : base + PAIR, :] = rows[:, :TAPS].astype(out.dtype)
            out[base + PAIR : base + PAIR + third_rows, :] = jnp.concatenate(
                [rows[part * third_rows : (part + 1) * third_rows, TAPS:] for part in range(3)],
                axis=1,
            ).astype(out.dtype)


def side_stack(inputs, stack):
    for image in range(inputs.shape[1] // PIX):
        columns = slice(image * PIX, (image + 1) * PIX)
        for pair in range(PAIRS // 2):
            piece = inputs[pair * PAIR : (pair + 1) * PAIR, columns]
            side_shifts(piece, stack.at[:, columns], pair * PIECE)


def one_core_kernel(place, grads, inputs, total_out, grad_stack, stack):
    stack_gradients([grads], grad_stack)
    side_stack(inputs, stack)
    total_out[...] = dot(stack[...], grad_stack[...], NT)


def both_cores_kernel(place, grads, inputs, partial, mixed, *refs):
    outs, grad_stack, stack = refs[:-2], refs[-2], refs[-1]
    stack_gradients([grads], grad_stack)
    side_stack(inputs, stack)
    total = partial[...] + dot(stack[...], grad_stack[...], NT)
    extra = JOINT - PIECE
    for part, out in enumerate(outs):
        rows = slice(part * extra, (part + 1) * extra)
        out[:PIECE, :] = total[part * PIECE : (part + 1) * PIECE].astype(out.dtype)
        out[PIECE:, :] = (mixed[0][rows, :] + mixed[1][rows, :].astype(WIDE)).astype(out.dtype)


def own_filter_kernel(place, grads, stacks, send_out, keep_out, grad_stack):
    stack_gradients([grads], grad_stack)
    send_out[...] = dot(stacks[1][...], grad_stack[...], NT).astype(LOW)
    keep_out[...] = dot(stacks[0][...], grad_stack[...], NT)


def split_kernel(place, keep, received, *outs):
    for part, out in enumerate(outs):
        rows = slice(part * PIECE, (part + 1) * PIECE)
        out[...] = (keep[rows, :] + received[rows, :].astype(WIDE)).astype(out.dtype)


def conv_back(place, grads, weight, grad_stack, product, value):
    stack_gradient(grads.at[0], grad_stack)
    product[...] = dot(weight[...], grad_stack[...], NN)
    back_to_channels(place, product, value)


def second_back_kernel(
    place,
    grads,
    pieces,
    normed_ref,
    stats_first,
    stats,
    mask_ref,
    params,
    member,
    first_grad_out,
    small_out,
    weight,
    grad_stack,
    product,
    value,
):
    load_second(weight, None, pieces)
    conv_back(place, grads, weight, grad_stack, product, value)
    mask = mask_ref[0]
    count = count_of(mask)
    gain, bias = params[:, 2:3], params[:, 3:4]
    factor = stats_first[0, :, 0:1]
    time_scale, time_shift = 1.0 + stats[0, :, 2:3], stats[0, :, 3:4]
    normed = normed_ref[0]
    hidden = (normed * gain + bias) * time_scale + time_shift
    delta = value[...] * mask * silu_slope(hidden)
    value[...] = delta
    plain = jnp.sum(delta, axis=1, keepdims=True)
    weighted = jnp.sum(delta * normed, axis=1, keepdims=True)
    scaled = gain * time_scale
    sums = group_sums(member[...], lane_pair(scaled * plain, scaled * weighted))
    first_sum, second_sum = sums[:, 0:1] / count, sums[:, 1:2] / count
    first_grad_out[0] = (
        factor * (value[...] * scaled - mask * (first_sum + normed * second_sum))
    ).astype(LOW)
    small_out[0] = small_rows(
        (
            time_scale * weighted,
            time_scale * plain,
            gain * weighted + bias * plain,
            plain,
        )
    )


def first_back_kernel(place, *refs):
    (
        grads,
        weight,
        whole,
        stats_first,
        residual_grad,
        mask_ref,
        params,
        member,
        small_in,
        keep_out,
        send_out,
        small_out,
        grad_stack,
        product,
        value,
    ) = refs[-15:]
    conv_back(place, grads, weight, grad_stack, product, value)
    own, other = half_offsets(place)
    mask = mask_ref[0]
    count = count_of(mask)
    gain, bias = params[:, 0:1], params[:, 1:2]
    mean, factor = stats_first[0, :, 0:1], stats_first[0, :, 1:2]
    normed = (whole[0].astype(WIDE) - mean) * factor
    hidden = normed * gain + bias
    delta = value[...] * mask * silu_slope(hidden)
    value[...] = delta
    plain = jnp.sum(delta, axis=1, keepdims=True)
    weighted = jnp.sum(delta * normed, axis=1, keepdims=True)
    sums = group_sums(member[...], lane_pair(gain * plain, gain * weighted))
    first_sum, second_sum = sums[:, 0:1] / count, sums[:, 1:2] / count
    value[...] = residual_grad[0].astype(WIDE) + factor * (
        value[...] * gain - mask * (first_sum + normed * second_sum)
    )
    keep_out[0] = value[pl.ds(own, HALF), :]
    send_out[0] = value[pl.ds(other, HALF), :].astype(LOW)
    rows = small_rows((weighted, plain))
    if len(small_in) == 0:
        small_out[...] = rows
    else:
        earlier, second, third, steps = small_in
        for ref in earlier:
            rows = rows + ref[...]
        images = second.shape[0]
        second_sum, third_sum = second[0], third[0]
        for image in range(1, images):
            second_sum, third_sum = second_sum + second[image], third_sum + third[image]
        small_out[:8, :] = set_rows(
            [
                rows[0:1],
                second_sum[0:1],
                third_sum[0:1],
                rows[1:2],
                second_sum[1:2],
                third_sum[1:2],
            ],
            8,
        )
        small_out[8:, :] = set_rows(
            [second[image, 2 + kind : 3 + kind] for kind in range(2) for image in range(images)]
            + [steps[0:1]],
            8,
        )


def cut_kernel(place, own, one, two, three, mine_out, side_out, far_out, corner_out):
    total = own[...] + one[...].astype(WIDE) + two[...].astype(WIDE) + three[...].astype(WIDE)
    left = place[BLOCKS] == 0
    outs = ((mine_out, side_out), (far_out, corner_out))
    for part in range(2):
        rows = jnp.concatenate(
            [total[tap * PAIR + part * ROWS : tap * PAIR + (part + 1) * ROWS] for tap in range(3)],
            axis=0,
        )
        halves = [rows[:, : 3 * HALF], rows[:, 3 * HALF :]]
        here, away = outs[part]
        here[...] = jnp.where(left, halves[0], halves[1]).astype(here.dtype)
        away[...] = jnp.where(left, halves[1], halves[0]).astype(away.dtype)


def unpack(rows, columns):
    return jnp.concatenate(
        [rows[:, third * columns : (third + 1) * columns] for third in range(3)], axis=0
    )


def pack(rows):
    count = rows.shape[0] // 3
    return jnp.concatenate(
        [rows[third * count : (third + 1) * count] for third in range(3)], axis=1
    )


def cut_columns_kernel(place, own, one, two, three, mine_out, side_out):
    total = own[...] + one[...].astype(WIDE) + two[...].astype(WIDE) + three[...].astype(WIDE)
    left = place[BLOCKS] == 0
    wide, output = total[: PIECE + PAIR], unpack(total[PIECE + PAIR :], C)
    halves = [
        jnp.concatenate(
            [
                wide[:, half * 3 * HALF : (half + 1) * 3 * HALF],
                pack(output[:, half * HALF : (half + 1) * HALF]),
            ],
            axis=0,
        )
        for half in range(2)
    ]
    mine_out[...] = jnp.where(left, halves[0], halves[1])
    side_out[...] = jnp.where(left, halves[1], halves[0]).astype(LOW)


def cut_rows_kernel(place, own, received, near_out, far_out):
    total = own[...] + received[...].astype(WIDE)
    output = unpack(total[PIECE + PAIR :], HALF)
    for part, out in enumerate((near_out, far_out)):
        rows = [
            total[tap * PAIR + part * ROWS : tap * PAIR + (part + 1) * ROWS] for tap in range(4)
        ]
        rows.append(pack(output[part * ROWS : (part + 1) * ROWS]))
        out[...] = jnp.concatenate(rows, axis=0).astype(out.dtype)


def finish_kernel(place, own, received, filter_out, *mixed_outs):
    total = own[...]
    for ref in received:
        total = total + ref[...].astype(WIDE)
    for down in range(3):
        for across in range(3):
            filter_out[3 * down + across] = total[
                across * ROWS : (across + 1) * ROWS, down * HALF : (down + 1) * HALF
            ]
    if mixed_outs:
        mixed_outs[0][...] = total[3 * ROWS : 4 * ROWS]
        mixed_outs[1][...] = unpack(total[4 * ROWS :], HALF)


def receive_kernel(place, carried, received, out):
    for image, ref in enumerate(received):

        @pl.when(pl.program_id(0) == image)
        def _(ref=ref):
            out[...] = ref[...].astype(out.dtype)


def shape(*sizes, dtype=WIDE):
    return jax.ShapeDtypeStruct(sizes, dtype)


def per_image(*sizes, first=0):
    return pl.BlockSpec((1,) + sizes, lambda g, place: (first + g,) + (0,) * len(sizes))


def own_image(*sizes, first=0):
    return pl.BlockSpec(
        (1,) + sizes, lambda g, place: (place[BLOCKS + 1] + first + g,) + (0,) * len(sizes)
    )


def other_image(*sizes):
    return pl.BlockSpec(
        (1,) + sizes, lambda g, place: (place[BLOCKS + 2] + g,) + (0,) * len(sizes)
    )


def per_columns(*sizes, first=0):
    return pl.BlockSpec(sizes, lambda g, place: (0, first + g))


def fixed(*sizes):
    return pl.BlockSpec(sizes, lambda g, place: (0,) * len(sizes))


def whole_array(entry):
    return fixed(*entry.shape)


def run(kernel, place, images, ins, outs, scratch, aliases=None, room=24, cost=8):
    arrays, structure = jax.tree.flatten([array for array, _ in ins])
    specs = jax.tree.leaves(
        [spec for _, spec in ins], is_leaf=lambda entry: isinstance(entry, pl.BlockSpec)
    )

    def body(place, *refs):
        given = jax.tree.unflatten(structure, refs[: len(arrays)])
        kernel(place, *given, *refs[len(arrays) :])

    return pl.pallas_call(
        body,
        grid_spec=pltpu.PrefetchScalarGridSpec(
            num_scalar_prefetch=1,
            grid=(images,),
            in_specs=specs,
            out_specs=[spec for _, spec in outs],
            scratch_shapes=scratch,
        ),
        out_shape=[out for out, _ in outs],
        input_output_aliases=aliases or {},
        compiler_params=pltpu.CompilerParams(
            dimension_semantics=("arbitrary",), vmem_limit_bytes=room * 2**20
        ),
        cost_estimate=pl.CostEstimate(flops=cost * 10**9, bytes_accessed=2**20, transcendentals=0),
    )(place, *arrays)


def filter_gradient(place, inputs, grads, mixed):
    scratch = [
        pltpu.VMEM((TAPS, grads[0].shape[0] * PIX), LOW),
        pltpu.VMEM((TAPS // 2, grads[0].shape[0] * PIX), LOW),
    ]
    partial = shape(TAPS // 2, TAPS)
    ins = (grads[0], inputs[0])
    (partial,) = run(
        one_core_kernel,
        place,
        1,
        [(entry, jax.tree.map(whole_array, entry)) for entry in ins],
        [(partial, whole_array(partial))],
        scratch,
        room=24,
    )
    ins = (grads[1], inputs[1], partial, mixed)
    outs = [shape(JOINT, TAPS)] + [shape(JOINT, TAPS, dtype=LOW)] * 3
    return run(
        both_cores_kernel,
        place,
        1,
        [(entry, jax.tree.map(whole_array, entry)) for entry in ins],
        [(out, whole_array(out)) for out in outs],
        scratch,
        room=32,
    )


def own_filter_gradient(place, stacks, grads):
    ins = (grads, stacks)
    outs = [shape(TAPS // 2, TAPS, dtype=LOW), shape(TAPS // 2, TAPS)]
    return run(
        own_filter_kernel,
        place,
        1,
        [(entry, jax.tree.map(whole_array, entry)) for entry in ins],
        [(out, whole_array(out)) for out in outs],
        [pltpu.VMEM((TAPS, grads.shape[0] * PIX), LOW)],
        room=32,
        cost=1,
    )


def simple(kernel, place, ins, outs, cost):
    return run(
        kernel,
        place,
        1,
        [(entry, jax.tree.map(whole_array, entry)) for entry in ins],
        [(out, whole_array(out)) for out in outs],
        [],
        cost=cost,
    )


def on_device(
    dp,
    features,
    pixel_masks,
    timesteps,
    first_filter,
    second_filter,
    project_weight,
    output_weight,
    embed_weight,
    norm_gains,
    norm_biases,
    cotangent,
):
    chan = lax.axis_index("chan")
    left = chan == 0
    span = dp // BLOCKS
    groups = [list(range(k * span, (k + 1) * span)) for k in range(BLOCKS)]
    block = lax.axis_index("dp") // span
    images = features.shape[0] // 2

    def swap(value, mask, flip):
        pairs = [
            (2 * d + x, 2 * (d ^ (mask * span)) + (x ^ flip)) for d in range(dp) for x in range(2)
        ]
        return lax.ppermute(value, ("dp", "chan"), pairs)

    def near(value, axis):
        if span == 1:
            return value
        return lax.all_gather(value, "dp", axis=axis, tiled=True, axis_index_groups=groups)

    def halves(mine, theirs, axis):
        return jnp.concatenate(
            [jnp.where(left, mine, theirs), jnp.where(left, theirs, mine)], axis=axis
        )

    def after(value, *others):
        return lax.optimization_barrier((value, others))[0]

    def pair_up(one, two):
        taps = one.shape[0] // ROWS
        columns = one.shape[1]
        both = [v.reshape(taps, ROWS, columns) for v in (one, two)]
        return jnp.stack(both, axis=1).reshape(2 * taps * ROWS, columns)

    def gather_one(shard, extra=None):
        side = swap(shard if extra is None else jnp.concatenate([shard, extra], axis=0), 0, 1)
        far = swap(shard, 8, 0)
        both = swap(shard, 8, 1)
        count = shard.shape[0]
        rows = pair_up(halves(shard, side[:count], 1), halves(far, both, 1))
        return rows if extra is None else (rows, side[count:])

    def gather_slow(shard, late):
        rows = after(pair_up(shard, swap(shard, 8, 0)), late)
        return rows, swap(rows, 0, 1)

    def gather_two(rows):
        return [rows, swap(rows, 4, 0), swap(rows, 2, 0), swap(rows, 6, 0)]

    def gather_three(pieces):
        return [swap(rows, 1, 0) for rows in pieces]

    def scatter_one(send, keep):
        outs = [shape(PIECE, TAPS)] + [shape(PIECE, TAPS, dtype=LOW)] * 3
        return simple(split_kernel, place, [keep, swap(send, 1, 0)], outs, 1)

    def scatter_two(keep, *sends):
        arrived = [swap(send, mask, 0) for send, mask in zip(sends, (4, 2, 6))]
        outs = [shape(3 * ROWS, 3 * HALF)] + [shape(3 * ROWS, 3 * HALF, dtype=LOW)] * 3
        return simple(cut_kernel, place, [keep] + arrived, outs, 30)

    def scatter_three(keep, *sends):
        arrived = [
            swap(send, mask, flip) for send, (mask, flip) in zip(sends, ((0, 1), (8, 0), (8, 1)))
        ]
        return simple(finish_kernel, place, [keep, arrived], [shape(9, ROWS, HALF)], 1)[0]

    def joint_two(keep, *sends, late):
        arrived = [swap(send, mask, 0) for send, mask in zip(sends, (4, 2, 6))]
        outs = [shape(JOINT, 3 * HALF), shape(JOINT, 3 * HALF, dtype=LOW)]
        return simple(cut_columns_kernel, place, [after(keep, late)] + arrived, outs, 30)

    def joint_three(keep, send, late):
        outs = [shape(JOINT // 2, 3 * HALF), shape(JOINT // 2, 3 * HALF, dtype=LOW)]
        ins = [after(keep, late), swap(send, 0, 1)]
        return simple(cut_rows_kernel, place, ins, outs, 1)

    def joint_four(keep, send, late):
        outs = [shape(9, ROWS, HALF), shape(ROWS, 3 * HALF), shape(ROWS, HALF)]
        ins = [after(keep, late), [swap(send, 8, 0)]]
        return simple(finish_kernel, place, ins, outs, 1)

    def share(value, dimension):
        if span == 1:
            return value
        return lax.psum_scatter(
            value, "dp", scatter_dimension=dimension, tiled=True, axis_index_groups=groups
        )

    def parts_of(value):
        high = value.astype(LOW)
        rest = value - high.astype(WIDE)
        middle = rest.astype(LOW)
        return [high, middle, (rest - middle.astype(WIDE)).astype(LOW)]

    own_start, other_start = chan * images, (1 - chan) * images

    def others(value):
        return lax.dynamic_slice_in_dim(value, other_start, images, 0)

    theirs = swap(others(features), 0, 1)

    def filter_rows(weight):
        rows = near(weight.astype(LOW), 1).reshape(3, 3, ROWS, HALF)
        return jnp.transpose(rows, (1, 2, 0, 3)).reshape(3 * ROWS, 3 * HALF)

    norms = jnp.concatenate([norm_gains, norm_biases], axis=0)
    norm_rows = jnp.pad(jnp.concatenate(parts_of(norms), axis=1), ((0, 2), (0, 0)))
    first_one, norm_rows = gather_one(filter_rows(first_filter), norm_rows)
    their_norms = norm_rows[:6].astype(WIDE).reshape(6, 3, HALF)
    their_norms = their_norms[:, 0] + their_norms[:, 1] + their_norms[:, 2]
    norms = halves(norms, their_norms, 1)
    params = jnp.stack([norms[0], norms[3], norms[1], norms[4], norms[2], norms[5]], axis=1)
    params = jnp.pad(params, ((0, 0), (0, 2)))
    first_pieces = gather_two(first_one)

    embed_rows = jnp.transpose(near(embed_weight.astype(LOW), 1), (1, 0, 2))
    embed_rows = jnp.transpose(embed_rows.reshape(PAIR, 3, 128), (1, 0, 2))
    embed_rows = embed_rows.reshape(2, 3 * ROWS, 128)
    bundle_rows = jnp.concatenate(
        [
            near(project_weight.astype(LOW), 0).reshape(ROWS, 3 * HALF),
            near(output_weight.astype(LOW), 1).T,
        ],
        axis=1,
    )
    bundle_rows = jnp.transpose(bundle_rows.reshape(ROWS, 3, PACKED), (1, 0, 2))
    second_rows = jnp.concatenate(
        [
            filter_rows(second_filter),
            embed_rows[0],
            embed_rows[1],
            bundle_rows.reshape(3 * ROWS, PACKED),
        ],
        axis=1,
    )
    second_one = gather_slow(second_rows, first_one)
    validity = lax.dynamic_slice_in_dim(pixel_masks, own_start, images, 0).astype(WIDE)
    validity = validity.reshape(images, 1, PIX)
    member = (jnp.arange(C)[:, None] // WIDTH == jnp.arange(C)[None, :] // WIDTH).astype(LOW)
    order = jnp.array(ORDER, jnp.int32)
    place = jnp.concatenate(
        [
            jnp.bitwise_xor(block, order) * ROWS,
            jnp.stack([chan, own_start, other_start]).astype(jnp.int32),
        ]
    )

    def time_features(steps, index, embed_width):
        half_width = embed_width // 2
        power = jnp.where(index < half_width, index, index - half_width).astype(WIDE)
        frequency = jnp.exp(-math.log(10000.0) * power / half_width)
        angles = steps[:, None] * frequency[None, :]
        return jax.nn.silu(
            jnp.where(index[None, :] < half_width, jnp.cos(angles), jnp.sin(angles))
        )

    embed_width = embed_weight.shape[1] * dp
    own_steps = lax.dynamic_slice_in_dim(timesteps, own_start, images, 0).astype(WIDE)
    flat = jnp.arange(2 * 3 * ROWS)
    third, entry_row = flat // PAIR, flat % PAIR
    embed_index = (jnp.bitwise_xor(block, order)[:, None] * PAIR + entry_row).reshape(-1)
    embed_values = time_features(after(own_steps, first_one), embed_index, embed_width)
    embed_split = jnp.stack(parts_of(embed_values), axis=2)
    embed_split = embed_split.reshape(images, PAIRS, 2, 2, 3, ROWS, 3)
    embed_split = jnp.transpose(embed_split, (0, 3, 1, 4, 2, 5, 6))
    late = (third.reshape(2, 3, ROWS) == jnp.array([1, 2])[:, None, None])
    late = late[None, :, None, :, None, :, None]
    embed_parts = jnp.concatenate(
        [jnp.where(late, 0, embed_split), jnp.where(late, embed_split, 0)], axis=6
    ).reshape(images, 2, TAPS, 6)
    embed_parts = jnp.concatenate([embed_parts[image] for image in range(images)], axis=2)
    embed_parts = jnp.pad(embed_parts, ((0, 0), (0, 0), (0, 128 - 6 * images)))
    steps_row = jnp.pad(own_steps, (0, HALF - images))
    steps_row = jnp.pad(jnp.concatenate([steps_row, steps_row])[None, :], ((0, 7), (0, 0)))

    value_scratch = pltpu.VMEM((C, PIX), WIDE)
    product_scratch = pltpu.VMEM((TAPS, PIX), WIDE)
    back_scratch = [pltpu.VMEM((TAPS, PIX), LOW), product_scratch, value_scratch]
    mask_in = (validity, per_image(1, PIX))
    params_in = (params, fixed(C, 8))
    member_in = (member, fixed(C, C))
    image_low = (shape(images, C, PIX, dtype=LOW), per_image(C, PIX))
    image_wide = (shape(images, C, PIX), per_image(C, PIX))
    image_small = (shape(images, C, 128), per_image(C, 128))
    image_rows = (shape(images, 8, C), per_image(8, C))
    weight_out = (shape(TAPS, TAPS, dtype=LOW), fixed(TAPS, TAPS))
    stack_out = (shape(TAPS // 2, images * PIX, dtype=LOW), per_columns(TAPS // 2, PIX))
    input_out = (shape(C // 2, images * PIX, dtype=LOW), per_columns(C // 2, PIX))
    anywhere = pl.BlockSpec(memory_space=pl.ANY)

    prepared = run(
        prepare_kernel,
        place,
        images,
        [
            (features, own_image(HALF, PIX)),
            (theirs, per_image(HALF, PIX)),
            mask_in,
            params_in,
            member_in,
        ],
        [image_low, stack_out, stack_out, image_small],
        [value_scratch],
    )
    whole, first_low, first_high, stats_whole = prepared
    cots = others(after(cotangent, first_one))
    first_pieces = first_pieces + gather_three(after(first_pieces, first_low))
    mine, side = after(second_one, first_low)
    second_one = halves(mine[:, :SECOND], side[:, :SECOND], 1)
    bundle_one = halves(mine[:, SECOND:], side[:, SECOND:], 1)
    second_normed, stats_first, first_weight = run(
        first_kernel,
        place,
        images,
        [
            mask_in,
            member_in,
            (first_pieces, [fixed(PIECE, TAPS)] * 8),
            (after([first_low, first_high], second_one, cots, embed_parts), [per_columns(TAPS // 2, PIX)] * 2),
        ],
        [image_wide, image_small, weight_out],
        [value_scratch, product_scratch],
    )
    second_pieces = gather_two(second_one)
    second_pieces = second_pieces + gather_three(after(second_pieces, second_normed))
    bundle_pieces = gather_two(bundle_one)
    their_cots = swap(after(cots, first_low), 0, 1)
    second_low, second_high, residual, stats_second = run(
        second_kernel,
        place,
        images,
        [
            (after(second_normed, bundle_one), per_image(C, PIX)),
            (whole, per_image(C, PIX)),
            (embed_parts, fixed(2, TAPS, 128)),
            mask_in,
            params_in,
            member_in,
            (second_pieces, [fixed(PIECE, 2 * SECOND)] * 8),
        ],
        [input_out, input_out, image_wide, image_small],
        [
            pltpu.VMEM((TAPS, TAPS), LOW),
            pltpu.VMEM((2, 2, TAPS, 128), LOW),
            value_scratch,
            pltpu.VMEM((TAPS, PIX), LOW),
            product_scratch,
        ],
        room=60,
    )
    bundle_pieces = bundle_pieces + gather_three(after(bundle_pieces, residual))
    second_theirs = swap(second_high, 1, 0)
    mixed_rows = PAIRS // 2 * (JOINT - PIECE)
    block_keep, block_send, second_grad, *mixed, small_third = run(
        attend_kernel,
        place,
        images,
        [
            (residual, per_image(C, PIX)),
            (stats_second, per_image(C, 128)),
            (cotangent, own_image(HALF, PIX)),
            (their_cots, per_image(HALF, PIX)),
            mask_in,
            params_in,
            member_in,
            (bundle_pieces, [fixed(PIECE, 2 * PACKED)] * 8),
        ],
        [
            (shape(2 * images, HALF, PIX, dtype=LOW), own_image(HALF, PIX)),
            (shape(images, HALF, PIX, dtype=LOW), per_image(HALF, PIX)),
            image_low,
            (shape(mixed_rows, TAPS), fixed(mixed_rows, TAPS)),
            (shape(mixed_rows, TAPS, dtype=LOW), fixed(mixed_rows, TAPS)),
            image_rows,
        ],
        [
            pltpu.VMEM((2, C, 2 * C), WIDE),
            pltpu.VMEM((C, PIX), LOW),
            pltpu.VMEM((C, TAPS), LOW),
            pltpu.VMEM((C, C), LOW),
            pltpu.VMEM((C, PIX), LOW),
            pltpu.VMEM((TAPS, PIX), LOW),
            pltpu.VMEM((C, PIX), LOW),
            pltpu.VMEM((C, PIX), LOW),
            pltpu.VMEM((TAPS, PIX), LOW),
            pltpu.VMEM((PIX, KEYS), LOW),
            pltpu.VMEM((PIX, KEYS), LOW),
            pltpu.VMEM((HEAD + 16, PIX), LOW),
            pltpu.VMEM((KEYS, PIX), LOW),
            pltpu.VMEM((KEYS, PIX), LOW),
            pltpu.VMEM((PIX, PIX), WIDE),
            pltpu.VMEM((PIX, PIX), LOW),
            pltpu.VMEM((PIX, PIX), LOW),
            pltpu.VMEM((C, TAPS + C), WIDE),
            value_scratch,
        ],
        room=62,
        cost=60,
    )
    block_theirs = swap(block_send, 0, 1)
    mixed = [mixed[0], swap(mixed[1], 1, 0)]
    grads_theirs = swap(second_grad, 1, 0)
    joint = filter_gradient(
        place, [second_low, second_theirs], [second_grad, grads_theirs], mixed
    )
    first_grad, small_second = run(
        second_back_kernel,
        place,
        images,
        [
            (after(second_grad, joint), per_image(C, PIX)),
            (second_pieces, [fixed(PIECE, 2 * SECOND)] * 8),
            (second_normed, per_image(C, PIX)),
            (stats_first, per_image(C, 128)),
            (stats_second, per_image(C, 128)),
            mask_in,
            params_in,
            member_in,
        ],
        [image_low, image_rows],
        [pltpu.VMEM((TAPS, TAPS), LOW)] + back_scratch,
        room=32,
    )
    masked_out = lax.dynamic_update_slice_in_dim(
        after(block_keep, joint), block_theirs, other_start, 0
    )
    send, keep = own_filter_gradient(
        place, [first_low, first_high], after(first_grad, masked_out)
    )
    first_part = scatter_one(send, keep)
    joint = joint_two(*joint, late=send)
    input_grad, input_theirs, smalls = None, [], []
    back_grad = after(first_grad, first_part, joint)
    for image in range(images):
        last = image == images - 1
        small_in = (smalls, small_second, small_third, steps_row) if last else ()
        carried = [] if input_grad is None else [(input_grad, anywhere)]
        small_shape = shape(16 if last else 8, C)
        input_grad, input_send, small = run(
            first_back_kernel,
            place,
            1,
            carried
            + [
                (back_grad, per_image(C, PIX, first=image)),
                (first_weight, fixed(TAPS, TAPS)),
                (whole, per_image(C, PIX, first=image)),
                (stats_whole, per_image(C, 128, first=image)),
                (second_grad, per_image(C, PIX, first=image)),
                (validity, per_image(1, PIX, first=image)),
                params_in,
                member_in,
                (small_in, jax.tree.map(whole_array, small_in)),
            ],
            [
                (shape(2 * images, HALF, PIX), own_image(HALF, PIX, first=image)),
                (shape(1, HALF, PIX, dtype=LOW), per_image(HALF, PIX)),
                (small_shape, whole_array(small_shape)),
            ],
            back_scratch,
            {1: 0} if carried else None,
        )
        smalls.append(small)
        input_theirs.append(swap(input_send, 0, 1))
        if image == 0:
            joint = joint_three(*joint, late=small)
            back_grad = after(back_grad, joint)
    first_part = scatter_two(*first_part)
    message = after(smalls[-1], input_theirs[:-1])

    def merge(arrived):
        total = sum(message[:8] for message in arrived)
        return jnp.concatenate([total] + [message[8:] for message in arrived], axis=0)

    message = after(merge([message, swap(message, 1, 0)]), first_part)
    joint = joint_four(*joint, late=first_part)
    grad_first = share(scatter_three(*first_part), 1)
    grad_second = share(joint[0], 1)
    grad_project = share(joint[1].reshape(ROWS, 3, HALF), 0)
    grad_output = share(joint[2].T, 1)
    (input_grad,) = run(
        receive_kernel,
        place,
        images,
        [(input_grad, anywhere), (input_theirs, [fixed(1, HALF, PIX)] * images)],
        [(shape(2 * images, HALF, PIX), other_image(HALF, PIX))],
        [],
        {1: 0},
        cost=1,
    )

    message = merge([message] + [swap(message, m, 0) for m in (4, 2, 6)])
    one, two = after(message[:, :HALF], input_theirs[-1]), message[:, HALF:]
    own, away = jnp.where(left, one, two), jnp.where(left, two, one)
    message = merge([own, swap(away, 0, 1), swap(own, 8, 0), swap(away, 8, 1)])
    total, entries = message[:6], message[8:]
    if span > 1:
        total = lax.psum(total, "dp", axis_index_groups=groups)
        entries = lax.all_gather(entries, "dp", axis=0, tiled=True, axis_index_groups=groups)
    entries = entries.reshape(-1, 8, HALF)
    all_steps = entries[:, 2 * images, :images].reshape(-1)
    scale_grads = entries[:, :images].reshape(-1, HALF)
    shift_grads = entries[:, images : 2 * images].reshape(-1, HALF)
    rows = embed_weight.shape[1]
    row_index = lax.axis_index("dp") * rows + jnp.arange(rows)
    all_embed = time_features(all_steps, row_index, embed_width)
    grad_embed = jnp.einsum(
        "be,kbd->ked",
        all_embed,
        jnp.stack([scale_grads, shift_grads]),
        precision=lax.Precision.HIGHEST,
    )
    return (
        masked_out,
        input_grad,
        grad_first,
        grad_second,
        grad_project,
        grad_output,
        grad_embed,
        total[:3],
        total[3:],
    )


def solution(mesh):
    in_specs = (
        P("dp", "chan", None),
        P("dp", None),
        P("dp"),
        P(None, "dp", "chan"),
        P(None, "dp", "chan"),
        P("dp", None, "chan"),
        P("chan", "dp"),
        P(None, "dp", "chan"),
        P(None, "chan"),
        P(None, "chan"),
        P("dp", "chan", None),
    )
    out_specs = (
        P("dp", "chan", None),
        P("dp", "chan", None),
        P(None, "dp", "chan"),
        P(None, "dp", "chan"),
        P("dp", None, "chan"),
        P("chan", "dp"),
        P(None, "dp", "chan"),
        P(None, "chan"),
        P(None, "chan"),
    )
    return jax.shard_map(
        functools.partial(on_device, mesh.shape["dp"]),
        mesh=mesh,
        in_specs=in_specs,
        out_specs=out_specs,
        check_vma=False,
    )
```

```python
import functools
import math

import jax
import jax.numpy as jnp
from jax import lax
from jax.experimental import pallas as pl
from jax.experimental.pallas import tpu as pltpu
from jax.sharding import PartitionSpec as P

C = 384
HALF = 192
HEAD = 64
GROUPS = 32
WIDTH = C // GROUPS
SIDE = 32
PIX = SIDE * SIDE
BLOCKS = 16
ROWS = C // BLOCKS
TAPS = 3 * C
EPSILON = 1e-05
SECOND = 3 * HALF + 256
MIXED = 4 * HALF
PACKED = MIXED // 3
PAIR = 2 * ROWS
PIECE = 3 * PAIR
JOINT = PIECE + PAIR + PAIR // 3
PAIRS = BLOCKS // 2
KEYS = 128
CHUNK = 256
PART = 512
LOW = jnp.bfloat16
WIDE = jnp.float32
ORDER = (0, 8, 4, 12, 2, 10, 6, 14, 1, 9, 5, 13, 3, 11, 7, 15)

NN = (((1,), (0,)), ((), ()))
NT = (((1,), (1,)), ((), ()))
TN = (((0,), (0,)), ((), ()))


def dot(left, right, dims):
    return lax.dot_general(left, right, dims, preferred_element_type=WIDE)


def pixel_row(keep):
    pixel = lax.broadcasted_iota(jnp.int32, (1, PIX), 1)
    return jnp.where(keep(pixel), 1.0, 0.0).astype(LOW)


def lane_pair(first, second):
    lane = lax.broadcasted_iota(jnp.int32, (C, 128), 1)
    return jnp.where(lane == 0, first, jnp.where(lane == 1, second, 0.0))


def group_sums(member, values):
    high = values.astype(LOW)
    rest = values - high.astype(WIDE)
    middle = rest.astype(LOW)
    low = (rest - middle.astype(WIDE)).astype(LOW)
    return dot(member, high, NN) + dot(member, middle, NN) + dot(member, low, NN)


def group_sum(member, column):
    return group_sums(member, jnp.broadcast_to(column, (C, 128)))[:, 0:1]


def group_stats(value_ref, member, mask, count):
    mean = group_sum(member, jnp.sum(value_ref[...] * mask, axis=1, keepdims=True)) / count
    centred = value_ref[...] - mean
    variance = (
        group_sum(member, jnp.sum(centred * centred * mask, axis=1, keepdims=True)) / count
    )
    return mean, lax.rsqrt(variance + EPSILON)


def silu(value):
    return value / (1.0 + jnp.exp(-value))


def silu_slope(value):
    squashed = 1.0 / (1.0 + jnp.exp(-value))
    return squashed * (1.0 + value * (1.0 - squashed))


def shift_down(piece):
    pixel = lax.broadcasted_iota(jnp.int32, piece.shape, 1)
    return jnp.where(pixel < SIDE, 0.0, pltpu.roll(piece, SIDE, 1))


def shift_up(piece):
    pixel = lax.broadcasted_iota(jnp.int32, piece.shape, 1)
    return jnp.where(pixel >= PIX - SIDE, 0.0, pltpu.roll(piece, PIX - SIDE, 1))


def conv_out(product_ref, chan):
    base = chan * 3 * HALF
    return (
        product_ref[base + HALF : base + 2 * HALF, :]
        + shift_down(product_ref[base : base + HALF, :])
        + shift_up(product_ref[base + 2 * HALF : base + 3 * HALF, :])
    )


def stack_gradient(grad_ref, out_ref):
    not_top = pixel_row(lambda pixel: pixel >= SIDE)
    not_bottom = pixel_row(lambda pixel: pixel < PIX - SIDE)
    for chan in range(2):
        piece = grad_ref[chan * HALF : (chan + 1) * HALF, :]
        base = chan * 3 * HALF
        out_ref[base : base + HALF, :] = pltpu.roll(piece, PIX - SIDE, 1) * not_bottom
        out_ref[base + HALF : base + 2 * HALF, :] = piece
        out_ref[base + 2 * HALF : base + 3 * HALF, :] = pltpu.roll(piece, SIDE, 1) * not_top


def stack_gradients(grads, out_ref):
    at = 0
    for ref in grads:
        for image in range(ref.shape[0]):
            stack_gradient(ref.at[image], out_ref.at[:, at * PIX : (at + 1) * PIX])
            at += 1


def block_offset(place_ref, position):
    return pl.multiple_of(place_ref[position], 8)


def pair_rows(place, ref, pair):
    return jnp.concatenate(
        [ref[pl.ds(block_offset(place, 2 * pair + part), ROWS), :] for part in range(2)], axis=0
    )


def side_shifts(piece, out, base):
    not_left = pixel_row(lambda pixel: pixel % SIDE != 0)
    not_right = pixel_row(lambda pixel: pixel % SIDE != SIDE - 1)
    rows = piece.shape[0]
    out[base : base + rows, :] = pltpu.roll(piece, 1, 1) * not_left
    out[base + rows : base + 2 * rows, :] = piece
    out[base + 2 * rows : base + 3 * rows, :] = pltpu.roll(piece, PIX - 1, 1) * not_right


def build_stack(place, value, mask, stacks, inputs=None):
    for pair in range(PAIRS):
        piece = (silu(pair_rows(place, value, pair)) * mask).astype(LOW)
        half, at = pair // (PAIRS // 2), pair % (PAIRS // 2)
        side_shifts(piece, stacks[half], at * PIECE)
        if inputs is not None:
            inputs[half][at * PAIR : (at + 1) * PAIR, :] = piece


def back_to_channels(place_ref, product_ref, out_ref):
    pixels = product_ref.shape[1]
    column = lax.broadcasted_iota(jnp.int32, (PAIR, pixels), 1) & (SIDE - 1)
    for pair in range(PAIRS):
        base = pair * PIECE
        first = product_ref[base : base + PAIR, :]
        middle = product_ref[base + PAIR : base + 2 * PAIR, :]
        last = product_ref[base + 2 * PAIR : base + 3 * PAIR, :]
        total = (
            middle
            + jnp.where(column == SIDE - 1, 0.0, pltpu.roll(first, pixels - 1, 1))
            + jnp.where(column == 0, 0.0, pltpu.roll(last, 1, 1))
        )
        for part in range(2):
            out_ref[pl.ds(block_offset(place_ref, 2 * pair + part), ROWS), :] = total[
                part * ROWS : (part + 1) * ROWS
            ]


def count_of(mask):
    return jnp.maximum(jnp.sum(mask, axis=1, keepdims=True), 1.0) * float(WIDTH)


def small_columns(columns):
    lane = lax.broadcasted_iota(jnp.int32, (C, 128), 1)
    result = jnp.zeros((C, 128), WIDE)
    for index, column in enumerate(columns):
        result = jnp.where(lane == index, column, result)
    return result


def small_rows(columns):
    return small_columns(columns).T[:8]


def columns_of(rows):
    return jnp.concatenate([rows, jnp.zeros((120, C), WIDE)], axis=0).T


def join_halves(place, mine, theirs, out):
    own, other = half_offsets(place)
    out[pl.ds(own, HALF), :] = mine[0].astype(out.dtype)
    out[pl.ds(other, HALF), :] = theirs[0].astype(out.dtype)


def set_rows(rows, count):
    index = lax.broadcasted_iota(jnp.int32, (count, rows[0].shape[1]), 0)
    result = jnp.zeros((count, rows[0].shape[1]), WIDE)
    for at, row in enumerate(rows):
        result = jnp.where(index == at, row, result)
    return result


def three_parts(value):
    high = value.astype(LOW).astype(WIDE)
    rest = value - high
    middle = rest.astype(LOW).astype(WIDE)
    return [high, middle, rest - middle]


def load_weight(weight, pieces):
    @pl.when(pl.program_id(0) == 0)
    def _():
        for index, source in enumerate(pieces):
            weight[index * PIECE : (index + 1) * PIECE, :] = source[...]


def load_second(weight, weight_e, pieces):
    @pl.when(pl.program_id(0) == 0)
    def _():
        for index, source in enumerate(pieces):
            rows = slice(index * PIECE, (index + 1) * PIECE)
            for chan in range(2):
                base = chan * SECOND
                weight[rows, chan * 3 * HALF : (chan + 1) * 3 * HALF] = source[
                    :, base : base + 3 * HALF
                ]
                for part in range(0 if weight_e is None else 2):
                    lane = base + 3 * HALF + part * 128
                    weight_e[chan, part, rows, :] = source[:, lane : lane + 128]


def both_rows(stacks):
    return jnp.concatenate([stack[...] for stack in stacks], axis=0)


def half_offsets(place):
    own = pl.multiple_of(place[BLOCKS] * HALF, HALF)
    other = pl.multiple_of((1 - place[BLOCKS]) * HALF, HALF)
    return own, other


def prepare_kernel(
    place,
    mine,
    theirs,
    mask_ref,
    params,
    member,
    low_out,
    high_out,
    stats_out,
    value,
):
    join_halves(place, mine, theirs, value)
    mask = mask_ref[0]
    mean, factor = group_stats(value, member[...], mask, count_of(mask))
    stats_out[0] = small_rows((mean, factor))
    scale = factor * params[:, 0:1]
    value[...] = (value[...] - mean) * scale + params[:, 1:2]
    build_stack(place, value, mask, (low_out, high_out))


def first_kernel(
    place,
    mask_ref,
    member,
    pieces,
    stacks,
    normed_out,
    stats_out,
    weight,
    value,
    product,
):
    load_weight(weight, pieces)
    mask = mask_ref[0]
    product[...] = dot(weight[...], both_rows(stacks), TN)
    for chan in range(2):
        value[chan * HALF : (chan + 1) * HALF, :] = conv_out(product, chan)
    mean, factor = group_stats(value, member[...], mask, count_of(mask))
    normed_out[0] = (value[...] - mean) * factor
    stats_out[0] = small_rows((factor,))


def second_kernel(
    place,
    normed,
    stats_first,
    mine,
    theirs,
    embed_in,
    mask_ref,
    params,
    member,
    pieces,
    low_out,
    high_out,
    residual_out,
    stats_out,
    weight,
    weight_e,
    value,
    stack,
    product,
):
    load_second(weight, weight_e, pieces)
    mask = mask_ref[0]
    count = count_of(mask)
    image = pl.program_id(0)

    def own_columns(sums):
        return jnp.where(image == 0, sums[:, :6], sums[:, 6:12])

    scales, shifts = [], []
    for chan in range(2):
        low = own_columns(dot(weight_e[chan, 0], embed_in[0], TN))
        high = own_columns(dot(weight_e[chan, 1], embed_in[1], TN))
        column = jnp.concatenate(
            [
                low[:, 0:1] + low[:, 1:2] + low[:, 2:3],
                low[:, 3:4] + low[:, 4:5] + low[:, 5:6] + high[:, 0:1] + high[:, 1:2] + high[:, 2:3],
                high[:, 3:4] + high[:, 4:5] + high[:, 5:6],
            ],
            axis=0,
        )
        scales.append(column[:HALF])
        shifts.append(column[HALF:])
    time_scale = jnp.concatenate(scales, axis=0)
    time_shift = jnp.concatenate(shifts, axis=0)
    affine = normed[0] * params[:, 2:3] + params[:, 3:4]
    value[...] = affine * (1.0 + time_scale) + time_shift
    middle = TAPS // 2
    stacks = (stack.at[:middle, :], stack.at[middle:, :])
    build_stack(place, value, mask, stacks, (low_out, high_out))
    product[...] = dot(weight[...], stack[...], TN)
    for chan in range(2):
        rows = slice(chan * HALF, (chan + 1) * HALF)
        value[rows, :] = conv_out(product, chan)
    own, other = half_offsets(place)
    value[pl.ds(own, HALF), :] += mine[0].astype(WIDE)
    value[pl.ds(other, HALF), :] += theirs[0].astype(WIDE)
    residual_out[0] = value[...]
    mean, factor = group_stats(value, member[...], mask, count)
    first_factor = columns_of(stats_first[0])[:, 0:1]
    stats_out[0] = small_rows((mean, factor, time_scale, time_shift, first_factor))


def attend_kernel(
    place,
    residual,
    stats,
    mine,
    theirs,
    mask_ref,
    params,
    member,
    bundle,
    block_out,
    send_out,
    second_grad_out,
    mixed_keep,
    mixed_send,
    small_out,
    weight_f,
    attend_in,
    project,
    output,
    gradient,
    projected,
    attend_grad,
    attended,
    projected_grad,
    key_side,
    value_side,
    value_rows,
    query_side,
    grad_side,
    scores,
    probs,
    score_grads,
    accumulated,
    value,
):
    image = pl.program_id(0)

    @pl.when(image == 0)
    def _():
        for chan in range(2):
            for pair in range(PAIRS):
                block = bundle[pair][:, chan * PACKED : (chan + 1) * PACKED].astype(WIDE)
                for part in range(2):
                    for third in range(3):
                        first = third * PAIR + part * ROWS
                        weight_f[
                            chan,
                            pl.ds(block_offset(place, 2 * pair + part), ROWS),
                            third * PACKED : (third + 1) * PACKED,
                        ] = block[first : first + ROWS]
        project[...] = jnp.concatenate(
            [weight_f[0, :, : 3 * HALF], weight_f[1, :, : 3 * HALF]], axis=1
        ).astype(LOW)
        output[...] = jnp.concatenate(
            [weight_f[0, :, 3 * HALF :], weight_f[1, :, 3 * HALF :]], axis=1
        ).astype(LOW)
        accumulated[...] = jnp.zeros_like(accumulated)

    own, other = half_offsets(place)
    mask = mask_ref[0]
    count = count_of(mask)
    gradient[pl.ds(own, HALF), :] = (mine[0].astype(WIDE) * mask).astype(LOW)
    gradient[pl.ds(other, HALF), :] = (theirs[0].astype(WIDE) * mask).astype(LOW)
    columns = columns_of(stats[0])
    mean, factor = columns[:, 0:1], columns[:, 1:2]
    scale = factor * params[:, 4:5]
    attend_in[...] = ((residual[0] - mean) * scale + params[:, 5:6]).astype(LOW)
    projected[...] = dot(project[...], attend_in[...], TN).astype(LOW)
    attend_grad[...] = dot(output[...], gradient[...], TN).astype(LOW)

    penalty = mask - 1.0
    one = jnp.ones((1, PIX), WIDE)
    fill = jnp.zeros((KEYS - HEAD - 16, PIX), LOW)
    key_rows = jnp.concatenate(
        [set_rows([penalty * 9984.0, penalty * 16.0], 16).astype(LOW), fill], axis=0
    )
    one_rows = jnp.concatenate([set_rows([one, one, one], 16).astype(LOW), fill], axis=0)
    query_side[HEAD:, :] = one_rows
    grad_side[HEAD:, :] = jnp.zeros((KEYS - HEAD, PIX), LOW)

    def one_head(head, carry):
        chan = head // 3
        row_q = pl.multiple_of(chan * (3 * HALF) + (head - 3 * chan) * HEAD, HEAD)
        row_k = pl.multiple_of(row_q + HALF, HEAD)
        row_v = pl.multiple_of(row_q + 2 * HALF, HEAD)
        row_o = pl.multiple_of(head * HEAD, HEAD)
        queries = projected[pl.ds(row_q, HEAD), :]
        keys = projected[pl.ds(row_k, HEAD), :]
        values = jnp.concatenate([projected[pl.ds(row_v, HEAD), :], one_rows], axis=0)
        grads = attend_grad[pl.ds(row_o, HEAD), :].astype(WIDE)
        key_side[...] = jnp.concatenate([keys, key_rows], axis=0).T
        value_rows[...] = values[: HEAD + 16]
        value_side[...] = values.T
        query_side[:HEAD, :] = (queries.astype(WIDE) * HEAD**-0.5).astype(LOW)
        peak = None
        for start in range(0, PIX, CHUNK):
            part = dot(key_side[start : start + CHUNK, :], query_side[...], NN)
            scores[start : start + CHUNK, :] = part
            highest = jnp.max(part.reshape(CHUNK // 8, 8, PIX), axis=0)
            peak = highest if peak is None else jnp.maximum(peak, highest)
        peak = jnp.max(peak, axis=0, keepdims=True)
        for start in range(0, PIX, CHUNK):
            span = slice(start, start + CHUNK)
            probs[span, :] = jnp.exp(scores[span, :] - peak).astype(LOW)
        result = dot(value_rows[...], probs[...], NN)
        inverse = 1.0 / result[HEAD : HEAD + 1, :]
        result = result[:HEAD, :] * inverse
        attended[pl.ds(row_o, HEAD), :] = result.astype(LOW)
        scaled = grads * inverse
        delta = jnp.sum(scaled * result, axis=0, keepdims=True)
        grad_side[:HEAD, :] = scaled.astype(LOW)
        grad_side[HEAD : HEAD + 16, :] = set_rows(three_parts(-delta), 16).astype(LOW)
        for start in range(0, PIX, CHUNK):
            span = slice(start, start + CHUNK)
            part = dot(value_side[span, :], grad_side[...], NN)
            score_grads[span, :] = (probs[span, :].astype(WIDE) * part).astype(LOW)
        projected_grad[pl.ds(row_q, HEAD), :] = (
            dot(keys, score_grads[...], NN) * HEAD**-0.5
        ).astype(LOW)
        projected_grad[pl.ds(row_k, HEAD), :] = (
            dot(queries, score_grads[...], NT) * HEAD**-0.5
        ).astype(LOW)
        projected_grad[pl.ds(row_v, HEAD), :] = dot(grad_side[:HEAD, :], probs[...], NT).astype(
            LOW
        )
        return carry

    lax.fori_loop(0, C // HEAD, one_head, 0, unroll=3)

    value[...] = (residual[0] + dot(output[...], attended[...], NN)) * mask
    block_out[0] = value[pl.ds(own, HALF), :].astype(LOW)
    send_out[0] = value[pl.ds(other, HALF), :].astype(LOW)
    accumulated[:, TAPS:] += dot(gradient[...], attended[...], NT)
    accumulated[:, :TAPS] += dot(attend_in[...], projected_grad[...], NT)
    third = dot(project[...], projected_grad[...], NN)
    normed = (residual[0] - mean) * factor
    bias_third = jnp.sum(third, axis=1, keepdims=True)
    gain_third = jnp.sum(third * normed, axis=1, keepdims=True)
    gain = params[:, 4:5]
    sums = group_sums(member[...], lane_pair(gain * bias_third, gain * gain_third))
    first_sum, second_sum = sums[:, 0:1] / count, sums[:, 1:2] / count
    total = gradient[...].astype(WIDE) + factor * (
        third * gain - mask * (first_sum + normed * second_sum)
    )
    second_grad_out[0] = total.astype(LOW)
    small_out[0] = small_rows((gain_third, bias_third))

    @pl.when(image == pl.num_programs(0) - 1)
    def _():
        for pair in range(PAIRS):
            rows = pair_rows(place, accumulated, pair)
            out = mixed_keep if pair < PAIRS // 2 else mixed_send
            base = pair % (PAIRS // 2) * (JOINT - PIECE)
            third_rows = PAIR // 3
            out[base : base + PAIR, :] = rows[:, :TAPS].astype(out.dtype)
            out[base + PAIR : base + PAIR + third_rows, :] = jnp.concatenate(
                [rows[part * third_rows : (part + 1) * third_rows, TAPS:] for part in range(3)],
                axis=1,
            ).astype(out.dtype)


def side_stack(inputs, stack):
    for image in range(inputs.shape[1] // PIX):
        columns = slice(image * PIX, (image + 1) * PIX)
        for pair in range(PAIRS // 2):
            piece = inputs[pair * PAIR : (pair + 1) * PAIR, columns]
            side_shifts(piece, stack.at[:, columns], pair * PIECE)


def one_core_kernel(place, grads, inputs, total_out, grad_stack, stack):
    stack_gradients([grads], grad_stack)
    side_stack(inputs, stack)
    total_out[...] = dot(stack[...], grad_stack[...], NT)


def both_cores_kernel(place, grads, inputs, partial, mixed, *refs):
    outs, grad_stack, stack = refs[:-2], refs[-2], refs[-1]
    stack_gradients([grads], grad_stack)
    side_stack(inputs, stack)
    total = partial[...] + dot(stack[...], grad_stack[...], NT)
    extra = JOINT - PIECE
    for part, out in enumerate(outs):
        rows = slice(part * extra, (part + 1) * extra)
        out[:PIECE, :] = total[part * PIECE : (part + 1) * PIECE].astype(out.dtype)
        out[PIECE:, :] = (mixed[0][rows, :] + mixed[1][rows, :].astype(WIDE)).astype(out.dtype)


def own_filter_kernel(place, grads, stacks, send_out, keep_out, grad_stack):
    stack_gradients([grads], grad_stack)
    total = dot(both_rows(stacks), grad_stack[...], NT)
    keep_out[...] = total[: TAPS // 2]
    send_out[...] = total[TAPS // 2 :].astype(LOW)


def split_kernel(place, keep, received, *outs):
    for part, out in enumerate(outs):
        rows = slice(part * PIECE, (part + 1) * PIECE)
        out[...] = (keep[rows, :] + received[rows, :].astype(WIDE)).astype(out.dtype)


def lane_sums(value):
    return sum(value[:, lane : lane + 128] for lane in range(0, value.shape[1], 128))


def conv_back(place, grads, weight, grad_stack, product, value, slope_of, mask, normed_of):
    stack_gradient(grads.at[0], grad_stack)
    spans = [slice(start, start + PART) for start in range(0, PIX, PART)]
    plain = weighted = None
    for index in range(len(spans) + 1):
        if index < len(spans):
            span = spans[index]
            product[:, span] = dot(weight[...], grad_stack[:, span], NN)
        if index > 0:
            span = spans[index - 1]
            back_to_channels(place, product.at[:, span], value.at[:, span])
            normed = normed_of(span)
            delta = value[:, span] * mask[:, span] * slope_of(normed)
            value[:, span] = delta
            sums = lane_sums(delta), lane_sums(delta * normed)
            plain = sums[0] if plain is None else plain + sums[0]
            weighted = sums[1] if weighted is None else weighted + sums[1]
    return [jnp.sum(sums, axis=1, keepdims=True) for sums in (plain, weighted)]


def second_back_kernel(
    place,
    grads,
    pieces,
    normed_ref,
    stats,
    mask_ref,
    params,
    member,
    first_grad_out,
    small_out,
    weight,
    grad_stack,
    product,
    value,
):
    load_second(weight, None, pieces)
    mask = mask_ref[0]
    count = count_of(mask)
    gain, bias = params[:, 2:3], params[:, 3:4]
    columns = columns_of(stats[0])
    factor = columns[:, 4:5]
    time_scale, time_shift = 1.0 + columns[:, 2:3], columns[:, 3:4]

    def slope_of(normed):
        return silu_slope((normed * gain + bias) * time_scale + time_shift)

    plain, weighted = conv_back(
        place,
        grads,
        weight,
        grad_stack,
        product,
        value,
        slope_of,
        mask,
        lambda span: normed_ref[0, :, span],
    )
    normed = normed_ref[0]
    scaled = gain * time_scale
    sums = group_sums(member[...], lane_pair(scaled * plain, scaled * weighted))
    first_sum, second_sum = sums[:, 0:1] / count, sums[:, 1:2] / count
    first_grad_out[0] = (
        factor * (value[...] * scaled - mask * (first_sum + normed * second_sum))
    ).astype(LOW)
    small_out[0] = small_rows(
        (
            time_scale * weighted,
            time_scale * plain,
            gain * weighted + bias * plain,
            plain,
        )
    )


def first_back_kernel(place, *refs):
    (
        grads,
        weight,
        mine,
        theirs,
        stats_first,
        residual_grad,
        mask_ref,
        params,
        member,
        small_in,
        keep_out,
        send_out,
        small_out,
        grad_stack,
        product,
        value,
        whole,
    ) = refs[-17:]
    join_halves(place, mine, theirs, whole)
    own, other = half_offsets(place)
    mask = mask_ref[0]
    count = count_of(mask)
    gain, bias = params[:, 0:1], params[:, 1:2]
    columns = columns_of(stats_first[0])
    mean, factor = columns[:, 0:1], columns[:, 1:2]

    def normed_of(span):
        return (whole[:, span].astype(WIDE) - mean) * factor

    plain, weighted = conv_back(
        place,
        grads,
        weight,
        grad_stack,
        product,
        value,
        lambda normed: silu_slope(normed * gain + bias),
        mask,
        normed_of,
    )
    normed = normed_of(slice(None))
    sums = group_sums(member[...], lane_pair(gain * plain, gain * weighted))
    first_sum, second_sum = sums[:, 0:1] / count, sums[:, 1:2] / count
    value[...] = residual_grad[0].astype(WIDE) + factor * (
        value[...] * gain - mask * (first_sum + normed * second_sum)
    )
    keep_out[0] = value[pl.ds(own, HALF), :]
    send_out[0] = value[pl.ds(other, HALF), :].astype(LOW)
    rows = small_rows((weighted, plain))
    if len(small_in) == 0:
        small_out[...] = rows
    else:
        earlier, second, third, steps = small_in
        for ref in earlier:
            rows = rows + ref[...]
        images = second.shape[0]
        second_sum, third_sum = second[0], third[0]
        for image in range(1, images):
            second_sum, third_sum = second_sum + second[image], third_sum + third[image]
        small_out[:8, :] = set_rows(
            [
                rows[0:1],
                second_sum[0:1],
                third_sum[0:1],
                rows[1:2],
                second_sum[1:2],
                third_sum[1:2],
            ],
            8,
        )
        small_out[8:, :] = set_rows(
            [second[image, 2 + kind : 3 + kind] for kind in range(2) for image in range(images)]
            + [steps[0:1]],
            8,
        )


def cut_kernel(place, own, one, two, three, mine_out, side_out, far_out, corner_out):
    total = own[...] + one[...].astype(WIDE) + two[...].astype(WIDE) + three[...].astype(WIDE)
    left = place[BLOCKS] == 0
    outs = ((mine_out, side_out), (far_out, corner_out))
    for part in range(2):
        rows = jnp.concatenate(
            [total[tap * PAIR + part * ROWS : tap * PAIR + (part + 1) * ROWS] for tap in range(3)],
            axis=0,
        )
        halves = [rows[:, : 3 * HALF], rows[:, 3 * HALF :]]
        here, away = outs[part]
        here[...] = jnp.where(left, halves[0], halves[1]).astype(here.dtype)
        away[...] = jnp.where(left, halves[1], halves[0]).astype(away.dtype)


def unpack(rows, columns):
    return jnp.concatenate(
        [rows[:, third * columns : (third + 1) * columns] for third in range(3)], axis=0
    )


def pack(rows):
    count = rows.shape[0] // 3
    return jnp.concatenate(
        [rows[third * count : (third + 1) * count] for third in range(3)], axis=1
    )


def cut_columns_kernel(place, own, one, two, three, mine_out, side_out):
    total = own[...] + one[...].astype(WIDE) + two[...].astype(WIDE) + three[...].astype(WIDE)
    left = place[BLOCKS] == 0
    wide, output = total[: PIECE + PAIR], unpack(total[PIECE + PAIR :], C)
    halves = [
        jnp.concatenate(
            [
                wide[:, half * 3 * HALF : (half + 1) * 3 * HALF],
                pack(output[:, half * HALF : (half + 1) * HALF]),
            ],
            axis=0,
        )
        for half in range(2)
    ]
    mine_out[...] = jnp.where(left, halves[0], halves[1])
    side_out[...] = jnp.where(left, halves[1], halves[0]).astype(LOW)


def cut_rows_kernel(place, own, received, near_out, far_out):
    total = own[...] + received[...].astype(WIDE)
    output = unpack(total[PIECE + PAIR :], HALF)
    for part, out in enumerate((near_out, far_out)):
        rows = [
            total[tap * PAIR + part * ROWS : tap * PAIR + (part + 1) * ROWS] for tap in range(4)
        ]
        rows.append(pack(output[part * ROWS : (part + 1) * ROWS]))
        out[...] = jnp.concatenate(rows, axis=0).astype(out.dtype)


def finish_kernel(place, own, received, filter_out, *mixed_outs):
    total = own[...]
    for ref in received:
        total = total + ref[...].astype(WIDE)
    for down in range(3):
        for across in range(3):
            filter_out[3 * down + across] = total[
                across * ROWS : (across + 1) * ROWS, down * HALF : (down + 1) * HALF
            ]
    if mixed_outs:
        mixed_outs[0][...] = total[3 * ROWS : 4 * ROWS]
        mixed_outs[1][...] = unpack(total[4 * ROWS :], HALF)


def receive_kernel(place, carried, received, out):
    for image, ref in enumerate(received):

        @pl.when(pl.program_id(0) == image)
        def _(ref=ref):
            out[...] = ref[...].astype(out.dtype)


def shape(*sizes, dtype=WIDE):
    return jax.ShapeDtypeStruct(sizes, dtype)


def per_image(*sizes, first=0):
    return pl.BlockSpec((1,) + sizes, lambda g, place: (first + g,) + (0,) * len(sizes))


def own_image(*sizes, first=0):
    return pl.BlockSpec(
        (1,) + sizes, lambda g, place: (place[BLOCKS + 1] + first + g,) + (0,) * len(sizes)
    )


def other_image(*sizes):
    return pl.BlockSpec(
        (1,) + sizes, lambda g, place: (place[BLOCKS + 2] + g,) + (0,) * len(sizes)
    )


def per_columns(*sizes, first=0):
    return pl.BlockSpec(sizes, lambda g, place: (0, first + g))


def fixed(*sizes):
    return pl.BlockSpec(sizes, lambda g, place: (0,) * len(sizes))


def whole_array(entry):
    return fixed(*entry.shape)


def run(kernel, place, images, ins, outs, scratch, aliases=None, room=24, cost=8):
    arrays, structure = jax.tree.flatten([array for array, _ in ins])
    specs = jax.tree.leaves(
        [spec for _, spec in ins], is_leaf=lambda entry: isinstance(entry, pl.BlockSpec)
    )

    def body(place, *refs):
        given = jax.tree.unflatten(structure, refs[: len(arrays)])
        kernel(place, *given, *refs[len(arrays) :])

    return pl.pallas_call(
        body,
        grid_spec=pltpu.PrefetchScalarGridSpec(
            num_scalar_prefetch=1,
            grid=(images,),
            in_specs=specs,
            out_specs=[spec for _, spec in outs],
            scratch_shapes=scratch,
        ),
        out_shape=[out for out, _ in outs],
        input_output_aliases=aliases or {},
        compiler_params=pltpu.CompilerParams(
            dimension_semantics=("arbitrary",), vmem_limit_bytes=room * 2**20
        ),
        cost_estimate=pl.CostEstimate(flops=cost * 10**9, bytes_accessed=2**20, transcendentals=0),
    )(place, *arrays)


def filter_gradient(place, inputs, grads, mixed):
    scratch = [
        pltpu.VMEM((TAPS, grads[0].shape[0] * PIX), LOW),
        pltpu.VMEM((TAPS // 2, grads[0].shape[0] * PIX), LOW),
    ]
    partial = shape(TAPS // 2, TAPS)
    ins = (grads[0], inputs[0])
    (partial,) = run(
        one_core_kernel,
        place,
        1,
        [(entry, jax.tree.map(whole_array, entry)) for entry in ins],
        [(partial, whole_array(partial))],
        scratch,
        room=24,
    )
    ins = (grads[1], inputs[1], partial, mixed)
    outs = [shape(JOINT, TAPS)] + [shape(JOINT, TAPS, dtype=LOW)] * 3
    return run(
        both_cores_kernel,
        place,
        1,
        [(entry, jax.tree.map(whole_array, entry)) for entry in ins],
        [(out, whole_array(out)) for out in outs],
        scratch,
        room=32,
    )


def own_filter_gradient(place, stacks, grads):
    ins = (grads, stacks)
    outs = [shape(TAPS // 2, TAPS, dtype=LOW), shape(TAPS // 2, TAPS)]
    return run(
        own_filter_kernel,
        place,
        1,
        [(entry, jax.tree.map(whole_array, entry)) for entry in ins],
        [(out, whole_array(out)) for out in outs],
        [pltpu.VMEM((TAPS, grads.shape[0] * PIX), LOW)],
        room=32,
        cost=1,
    )


def simple(kernel, place, ins, outs, cost):
    return run(
        kernel,
        place,
        1,
        [(entry, jax.tree.map(whole_array, entry)) for entry in ins],
        [(out, whole_array(out)) for out in outs],
        [],
        cost=cost,
    )


def on_device(
    dp,
    features,
    pixel_masks,
    timesteps,
    first_filter,
    second_filter,
    project_weight,
    output_weight,
    embed_weight,
    norm_gains,
    norm_biases,
    cotangent,
):
    chan = lax.axis_index("chan")
    left = chan == 0
    span = dp // BLOCKS
    groups = [list(range(k * span, (k + 1) * span)) for k in range(BLOCKS)]
    block = lax.axis_index("dp") // span
    images = features.shape[0] // 2

    def swap(value, mask, flip):
        pairs = [
            (2 * d + x, 2 * (d ^ (mask * span)) + (x ^ flip)) for d in range(dp) for x in range(2)
        ]
        return lax.ppermute(value, ("dp", "chan"), pairs)

    def near(value, axis):
        if span == 1:
            return value
        return lax.all_gather(value, "dp", axis=axis, tiled=True, axis_index_groups=groups)

    def halves(mine, theirs, axis):
        return jnp.concatenate(
            [jnp.where(left, mine, theirs), jnp.where(left, theirs, mine)], axis=axis
        )

    def after(value, *others):
        return lax.optimization_barrier((value, others))[0]

    def pair_up(one, two):
        taps = one.shape[0] // ROWS
        columns = one.shape[1]
        both = [v.reshape(taps, ROWS, columns) for v in (one, two)]
        return jnp.stack(both, axis=1).reshape(2 * taps * ROWS, columns)

    def gather_one(shard, extra=None):
        side = swap(shard if extra is None else jnp.concatenate([shard, extra], axis=0), 0, 1)
        far = swap(shard, 8, 0)
        both = swap(shard, 8, 1)
        count = shard.shape[0]
        rows = pair_up(halves(shard, side[:count], 1), halves(far, both, 1))
        return rows if extra is None else (rows, side[count:])

    def gather_slow(shard, late):
        rows = after(pair_up(shard, swap(shard, 8, 0)), late)
        return rows, swap(rows, 0, 1)

    def gather_two(rows):
        return [rows, swap(rows, 4, 0), swap(rows, 2, 0), swap(rows, 6, 0)]

    def gather_three(pieces):
        return [swap(rows, 1, 0) for rows in pieces]

    def scatter_one(send, keep):
        outs = [shape(PIECE, TAPS)] + [shape(PIECE, TAPS, dtype=LOW)] * 3
        return simple(split_kernel, place, [keep, swap(send, 1, 0)], outs, 1)

    def scatter_two(keep, *sends):
        arrived = [swap(send, mask, 0) for send, mask in zip(sends, (4, 2, 6))]
        outs = [shape(3 * ROWS, 3 * HALF)] + [shape(3 * ROWS, 3 * HALF, dtype=LOW)] * 3
        return simple(cut_kernel, place, [keep] + arrived, outs, 30)

    def scatter_three(keep, *sends):
        arrived = [
            swap(send, mask, flip) for send, (mask, flip) in zip(sends, ((0, 1), (8, 0), (8, 1)))
        ]
        return simple(finish_kernel, place, [keep, arrived], [shape(9, ROWS, HALF)], 1)[0]

    def joint_two(keep, *sends, late):
        arrived = [swap(send, mask, 0) for send, mask in zip(sends, (4, 2, 6))]
        outs = [shape(JOINT, 3 * HALF), shape(JOINT, 3 * HALF, dtype=LOW)]
        return simple(cut_columns_kernel, place, [after(keep, late)] + arrived, outs, 30)

    def joint_three(keep, send, late):
        outs = [shape(JOINT // 2, 3 * HALF), shape(JOINT // 2, 3 * HALF, dtype=LOW)]
        ins = [after(keep, late), swap(send, 0, 1)]
        return simple(cut_rows_kernel, place, ins, outs, 1)

    def joint_four(keep, send, late):
        outs = [shape(9, ROWS, HALF), shape(ROWS, 3 * HALF), shape(ROWS, HALF)]
        ins = [after(keep, late), [swap(send, 8, 0)]]
        return simple(finish_kernel, place, ins, outs, 1)

    def share(value, dimension):
        if span == 1:
            return value
        return lax.psum_scatter(
            value, "dp", scatter_dimension=dimension, tiled=True, axis_index_groups=groups
        )

    def parts_of(value):
        high = value.astype(LOW)
        rest = value - high.astype(WIDE)
        middle = rest.astype(LOW)
        return [high, middle, (rest - middle.astype(WIDE)).astype(LOW)]

    own_start, other_start = chan * images, (1 - chan) * images

    def others(value):
        return lax.dynamic_slice_in_dim(value, other_start, images, 0)

    theirs = swap(others(features), 0, 1)

    def filter_rows(weight):
        rows = near(weight.astype(LOW), 1).reshape(3, 3, ROWS, HALF)
        return jnp.transpose(rows, (1, 2, 0, 3)).reshape(3 * ROWS, 3 * HALF)

    norms = jnp.concatenate([norm_gains, norm_biases], axis=0)
    norm_rows = jnp.pad(jnp.concatenate(parts_of(norms), axis=1), ((0, 2), (0, 0)))
    first_one, norm_rows = gather_one(filter_rows(first_filter), norm_rows)
    their_norms = norm_rows[:6].astype(WIDE).reshape(6, 3, HALF)
    their_norms = their_norms[:, 0] + their_norms[:, 1] + their_norms[:, 2]
    norms = halves(norms, their_norms, 1)
    params = jnp.stack([norms[0], norms[3], norms[1], norms[4], norms[2], norms[5]], axis=1)
    params = jnp.pad(params, ((0, 0), (0, 2)))
    first_pieces = gather_two(first_one)

    embed_rows = jnp.transpose(near(embed_weight.astype(LOW), 1), (1, 0, 2))
    embed_rows = jnp.transpose(embed_rows.reshape(PAIR, 3, 128), (1, 0, 2))
    embed_rows = embed_rows.reshape(2, 3 * ROWS, 128)
    bundle_rows = jnp.concatenate(
        [
            near(project_weight.astype(LOW), 0).reshape(ROWS, 3 * HALF),
            near(output_weight.astype(LOW), 1).T,
        ],
        axis=1,
    )
    bundle_rows = jnp.transpose(bundle_rows.reshape(ROWS, 3, PACKED), (1, 0, 2))
    second_rows = jnp.concatenate(
        [
            filter_rows(second_filter),
            embed_rows[0],
            embed_rows[1],
            bundle_rows.reshape(3 * ROWS, PACKED),
        ],
        axis=1,
    )
    second_one = gather_slow(second_rows, first_one)
    validity = lax.dynamic_slice_in_dim(pixel_masks, own_start, images, 0).astype(WIDE)
    validity = validity.reshape(images, 1, PIX)
    member = (jnp.arange(C)[:, None] // WIDTH == jnp.arange(C)[None, :] // WIDTH).astype(LOW)
    order = jnp.array(ORDER, jnp.int32)
    place = jnp.concatenate(
        [
            jnp.bitwise_xor(block, order) * ROWS,
            jnp.stack([chan, own_start, other_start]).astype(jnp.int32),
        ]
    )

    def time_features(steps, index, embed_width):
        half_width = embed_width // 2
        power = jnp.where(index < half_width, index, index - half_width).astype(WIDE)
        frequency = jnp.exp(-math.log(10000.0) * power / half_width)
        angles = steps[:, None] * frequency[None, :]
        return jax.nn.silu(
            jnp.where(index[None, :] < half_width, jnp.cos(angles), jnp.sin(angles))
        )

    embed_width = embed_weight.shape[1] * dp
    own_steps = lax.dynamic_slice_in_dim(timesteps, own_start, images, 0).astype(WIDE)
    flat = jnp.arange(2 * 3 * ROWS)
    third, entry_row = flat // PAIR, flat % PAIR
    embed_index = (jnp.bitwise_xor(block, order)[:, None] * PAIR + entry_row).reshape(-1)
    embed_values = time_features(after(own_steps, first_one), embed_index, embed_width)
    embed_split = jnp.stack(parts_of(embed_values), axis=2)
    embed_split = embed_split.reshape(images, PAIRS, 2, 2, 3, ROWS, 3)
    embed_split = jnp.transpose(embed_split, (0, 3, 1, 4, 2, 5, 6))
    late = (third.reshape(2, 3, ROWS) == jnp.array([1, 2])[:, None, None])
    late = late[None, :, None, :, None, :, None]
    embed_parts = jnp.concatenate(
        [jnp.where(late, 0, embed_split), jnp.where(late, embed_split, 0)], axis=6
    ).reshape(images, 2, TAPS, 6)
    embed_parts = jnp.concatenate([embed_parts[image] for image in range(images)], axis=2)
    embed_parts = jnp.pad(embed_parts, ((0, 0), (0, 0), (0, 128 - 6 * images)))
    steps_row = jnp.pad(own_steps, (0, HALF - images))
    steps_row = jnp.pad(jnp.concatenate([steps_row, steps_row])[None, :], ((0, 7), (0, 0)))

    value_scratch = pltpu.VMEM((C, PIX), WIDE)
    product_scratch = pltpu.VMEM((TAPS, PIX), WIDE)
    back_scratch = [pltpu.VMEM((TAPS, PIX), LOW), product_scratch, value_scratch]
    mask_in = (validity, per_image(1, PIX))
    params_in = (params, fixed(C, 8))
    member_in = (member, fixed(C, C))
    image_low = (shape(images, C, PIX, dtype=LOW), per_image(C, PIX))
    image_wide = (shape(images, C, PIX), per_image(C, PIX))
    image_rows = (shape(images, 8, C), per_image(8, C))
    weight_out = (shape(TAPS, TAPS, dtype=LOW), fixed(TAPS, TAPS))
    stack_out = (shape(TAPS // 2, images * PIX, dtype=LOW), per_columns(TAPS // 2, PIX))
    input_out = (shape(C // 2, images * PIX, dtype=LOW), per_columns(C // 2, PIX))
    anywhere = pl.BlockSpec(memory_space=pl.ANY)

    prepared = run(
        prepare_kernel,
        place,
        images,
        [
            (features, own_image(HALF, PIX)),
            (theirs, per_image(HALF, PIX)),
            mask_in,
            params_in,
            member_in,
        ],
        [stack_out, stack_out, image_rows],
        [value_scratch],
    )
    first_low, first_high, stats_whole = prepared
    cots = others(after(cotangent, first_one))
    first_pieces = first_pieces + gather_three(after(first_pieces, first_low))
    mine, side = after(second_one, first_low)
    second_one = halves(mine[:, :SECOND], side[:, :SECOND], 1)
    bundle_one = halves(mine[:, SECOND:], side[:, SECOND:], 1)
    second_normed, stats_first, first_weight = run(
        first_kernel,
        place,
        images,
        [
            mask_in,
            member_in,
            (first_pieces, [fixed(PIECE, TAPS)] * 8),
            (after([first_low, first_high], second_one, cots, embed_parts, steps_row), [per_columns(TAPS // 2, PIX)] * 2),
        ],
        [image_wide, image_rows, weight_out],
        [value_scratch, product_scratch],
    )
    second_pieces = gather_two(second_one)
    second_pieces = second_pieces + gather_three(after(second_pieces, second_normed))
    bundle_pieces = gather_two(bundle_one)
    their_cots = swap(after(cots, first_low), 0, 1)
    second_low, second_high, residual, stats_second = run(
        second_kernel,
        place,
        images,
        [
            (after(second_normed, bundle_one), per_image(C, PIX)),
            (stats_first, per_image(8, C)),
            (features, own_image(HALF, PIX)),
            (theirs, per_image(HALF, PIX)),
            (embed_parts, fixed(2, TAPS, 128)),
            mask_in,
            params_in,
            member_in,
            (second_pieces, [fixed(PIECE, 2 * SECOND)] * 8),
        ],
        [input_out, input_out, image_wide, image_rows],
        [
            pltpu.VMEM((TAPS, TAPS), LOW),
            pltpu.VMEM((2, 2, TAPS, 128), LOW),
            value_scratch,
            pltpu.VMEM((TAPS, PIX), LOW),
            product_scratch,
        ],
        room=60,
    )
    bundle_pieces = bundle_pieces + gather_three(after(bundle_pieces, residual))
    second_theirs = swap(second_high, 1, 0)
    mixed_rows = PAIRS // 2 * (JOINT - PIECE)
    block_keep, block_send, second_grad, *mixed, small_third = run(
        attend_kernel,
        place,
        images,
        [
            (residual, per_image(C, PIX)),
            (stats_second, per_image(8, C)),
            (cotangent, own_image(HALF, PIX)),
            (their_cots, per_image(HALF, PIX)),
            mask_in,
            params_in,
            member_in,
            (bundle_pieces, [fixed(PIECE, 2 * PACKED)] * 8),
        ],
        [
            (shape(2 * images, HALF, PIX, dtype=LOW), own_image(HALF, PIX)),
            (shape(images, HALF, PIX, dtype=LOW), per_image(HALF, PIX)),
            image_low,
            (shape(mixed_rows, TAPS), fixed(mixed_rows, TAPS)),
            (shape(mixed_rows, TAPS, dtype=LOW), fixed(mixed_rows, TAPS)),
            image_rows,
        ],
        [
            pltpu.VMEM((2, C, 2 * C), WIDE),
            pltpu.VMEM((C, PIX), LOW),
            pltpu.VMEM((C, TAPS), LOW),
            pltpu.VMEM((C, C), LOW),
            pltpu.VMEM((C, PIX), LOW),
            pltpu.VMEM((TAPS, PIX), LOW),
            pltpu.VMEM((C, PIX), LOW),
            pltpu.VMEM((C, PIX), LOW),
            pltpu.VMEM((TAPS, PIX), LOW),
            pltpu.VMEM((PIX, KEYS), LOW),
            pltpu.VMEM((PIX, KEYS), LOW),
            pltpu.VMEM((HEAD + 16, PIX), LOW),
            pltpu.VMEM((KEYS, PIX), LOW),
            pltpu.VMEM((KEYS, PIX), LOW),
            pltpu.VMEM((PIX, PIX), WIDE),
            pltpu.VMEM((PIX, PIX), LOW),
            pltpu.VMEM((PIX, PIX), LOW),
            pltpu.VMEM((C, TAPS + C), WIDE),
            value_scratch,
        ],
        room=62,
        cost=60,
    )
    block_theirs = swap(block_send, 0, 1)
    mixed = [mixed[0], swap(mixed[1], 1, 0)]
    grads_theirs = swap(second_grad, 1, 0)
    joint = filter_gradient(
        place, [second_low, second_theirs], [second_grad, grads_theirs], mixed
    )
    first_grad, small_second = run(
        second_back_kernel,
        place,
        images,
        [
            (after(second_grad, joint), per_image(C, PIX)),
            (second_pieces, [fixed(PIECE, 2 * SECOND)] * 8),
            (second_normed, per_image(C, PIX)),
            (stats_second, per_image(8, C)),
            mask_in,
            params_in,
            member_in,
        ],
        [image_low, image_rows],
        [pltpu.VMEM((TAPS, TAPS), LOW)] + back_scratch,
        room=32,
    )
    masked_out = lax.dynamic_update_slice_in_dim(
        after(block_keep, joint), block_theirs, other_start, 0
    )
    send, keep = own_filter_gradient(
        place, [first_low, first_high], after(first_grad, masked_out)
    )
    first_part = scatter_one(send, keep)
    joint = joint_two(*joint, late=send)
    input_grad, input_theirs, smalls = None, [], []
    back_grad = after(first_grad, first_part, joint)
    for image in range(images):
        last = image == images - 1
        small_in = (smalls, small_second, small_third, steps_row) if last else ()
        carried = [] if input_grad is None else [(input_grad, anywhere)]
        small_shape = shape(16 if last else 8, C)
        input_grad, input_send, small = run(
            first_back_kernel,
            place,
            1,
            carried
            + [
                (back_grad, per_image(C, PIX, first=image)),
                (first_weight, fixed(TAPS, TAPS)),
                (features, own_image(HALF, PIX, first=image)),
                (theirs, per_image(HALF, PIX, first=image)),
                (stats_whole, per_image(8, C, first=image)),
                (second_grad, per_image(C, PIX, first=image)),
                (validity, per_image(1, PIX, first=image)),
                params_in,
                member_in,
                (small_in, jax.tree.map(whole_array, small_in)),
            ],
            [
                (shape(2 * images, HALF, PIX), own_image(HALF, PIX, first=image)),
                (shape(1, HALF, PIX, dtype=LOW), per_image(HALF, PIX)),
                (small_shape, whole_array(small_shape)),
            ],
            back_scratch + [pltpu.VMEM((C, PIX), LOW)],
            {1: 0} if carried else None,
        )
        smalls.append(small)
        input_theirs.append(swap(input_send, 0, 1))
        if image == 0:
            joint = joint_three(*joint, late=small)
            back_grad = after(back_grad, joint)
    first_part = scatter_two(*first_part)
    message = after(smalls[-1], input_theirs[:-1])

    def merge(arrived):
        total = sum(message[:8] for message in arrived)
        return jnp.concatenate([total] + [message[8:] for message in arrived], axis=0)

    message = after(merge([message, swap(message, 1, 0)]), first_part)
    joint = joint_four(*joint, late=first_part)
    grad_first = share(scatter_three(*first_part), 1)
    grad_second = share(joint[0], 1)
    grad_project = share(joint[1].reshape(ROWS, 3, HALF), 0)
    grad_output = share(joint[2].T, 1)
    (input_grad,) = run(
        receive_kernel,
        place,
        images,
        [(input_grad, anywhere), (input_theirs, [fixed(1, HALF, PIX)] * images)],
        [(shape(2 * images, HALF, PIX), other_image(HALF, PIX))],
        [],
        {1: 0},
        cost=1,
    )

    message = merge([message, swap(message, 4, 0)])
    message = merge([message, swap(message, 2, 0)])
    one, two = after(message[:, :HALF], input_theirs[-1]), message[:, HALF:]
    own, away = jnp.where(left, one, two), jnp.where(left, two, one)
    message = merge([own, swap(away, 0, 1), swap(own, 8, 0), swap(away, 8, 1)])
    total, entries = message[:6], message[8:]
    if span > 1:
        total = lax.psum(total, "dp", axis_index_groups=groups)
        entries = lax.all_gather(entries, "dp", axis=0, tiled=True, axis_index_groups=groups)
    entries = entries.reshape(-1, 8, HALF)
    all_steps = entries[:, 2 * images, :images].reshape(-1)
    scale_grads = entries[:, :images].reshape(-1, HALF)
    shift_grads = entries[:, images : 2 * images].reshape(-1, HALF)
    rows = embed_weight.shape[1]
    row_index = lax.axis_index("dp") * rows + jnp.arange(rows)
    all_embed = time_features(all_steps, row_index, embed_width)
    grad_embed = jnp.einsum(
        "be,kbd->ked",
        all_embed,
        jnp.stack([scale_grads, shift_grads]),
        precision=lax.Precision.HIGHEST,
    )
    return (
        masked_out,
        input_grad,
        grad_first,
        grad_second,
        grad_project,
        grad_output,
        grad_embed,
        total[:3],
        total[3:],
    )


def solution(mesh):
    in_specs = (
        P("dp", "chan", None),
        P("dp", None),
        P("dp"),
        P(None, "dp", "chan"),
        P(None, "dp", "chan"),
        P("dp", None, "chan"),
        P("chan", "dp"),
        P(None, "dp", "chan"),
        P(None, "chan"),
        P(None, "chan"),
        P("dp", "chan", None),
    )
    out_specs = (
        P("dp", "chan", None),
        P("dp", "chan", None),
        P(None, "dp", "chan"),
        P(None, "dp", "chan"),
        P("dp", None, "chan"),
        P("chan", "dp"),
        P(None, "dp", "chan"),
        P(None, "chan"),
        P(None, "chan"),
    )
    return jax.shard_map(
        functools.partial(on_device, mesh.shape["dp"]),
        mesh=mesh,
        in_specs=in_specs,
        out_specs=out_specs,
        check_vma=False,
    )
```

```python
import functools
import math

import jax
import jax.numpy as jnp
from jax import lax
from jax.experimental import pallas as pl
from jax.experimental.pallas import tpu as pltpu
from jax.sharding import PartitionSpec as P

C = 384
HALF = 192
HEAD = 64
GROUPS = 32
WIDTH = C // GROUPS
SIDE = 32
PIX = SIDE * SIDE
BLOCKS = 16
ROWS = C // BLOCKS
TAPS = 3 * C
EPSILON = 1e-05
SECOND = 3 * HALF + 256
MIXED = 4 * HALF
PACKED = MIXED // 3
PAIR = 2 * ROWS
PIECE = 3 * PAIR
JOINT = PIECE + PAIR + PAIR // 3
PAIRS = BLOCKS // 2
KEYS = 128
CHUNK = 256
PART = 512
LOW = jnp.bfloat16
WIDE = jnp.float32
ORDER = (0, 8, 4, 12, 2, 10, 6, 14, 1, 9, 5, 13, 3, 11, 7, 15)

NN = (((1,), (0,)), ((), ()))
NT = (((1,), (1,)), ((), ()))
TN = (((0,), (0,)), ((), ()))


def dot(left, right, dims):
    return lax.dot_general(left, right, dims, preferred_element_type=WIDE)


def pixel_row(keep):
    pixel = lax.broadcasted_iota(jnp.int32, (1, PIX), 1)
    return jnp.where(keep(pixel), 1.0, 0.0).astype(LOW)


def lane_pair(first, second):
    lane = lax.broadcasted_iota(jnp.int32, (C, 128), 1)
    return jnp.where(lane == 0, first, jnp.where(lane == 1, second, 0.0))


def group_sums(member, values):
    high = values.astype(LOW)
    rest = values - high.astype(WIDE)
    middle = rest.astype(LOW)
    low = (rest - middle.astype(WIDE)).astype(LOW)
    return dot(member, high, NN) + dot(member, middle, NN) + dot(member, low, NN)


def group_sum(member, column):
    return group_sums(member, jnp.broadcast_to(column, (C, 128)))[:, 0:1]


def group_stats(value_ref, member, mask, count):
    mean = group_sum(member, jnp.sum(value_ref[...] * mask, axis=1, keepdims=True)) / count
    centred = value_ref[...] - mean
    variance = (
        group_sum(member, jnp.sum(centred * centred * mask, axis=1, keepdims=True)) / count
    )
    return mean, lax.rsqrt(variance + EPSILON)


def silu(value):
    return value / (1.0 + jnp.exp(-value))


def silu_slope(value):
    squashed = 1.0 / (1.0 + jnp.exp(-value))
    return squashed * (1.0 + value * (1.0 - squashed))


def shift_down(piece):
    pixel = lax.broadcasted_iota(jnp.int32, piece.shape, 1)
    return jnp.where(pixel < SIDE, 0.0, pltpu.roll(piece, SIDE, 1))


def shift_up(piece):
    pixel = lax.broadcasted_iota(jnp.int32, piece.shape, 1)
    return jnp.where(pixel >= PIX - SIDE, 0.0, pltpu.roll(piece, PIX - SIDE, 1))


def conv_out(product_ref, chan):
    base = chan * 3 * HALF
    return (
        product_ref[base + HALF : base + 2 * HALF, :]
        + shift_down(product_ref[base : base + HALF, :])
        + shift_up(product_ref[base + 2 * HALF : base + 3 * HALF, :])
    )


def stack_gradient(grad_ref, out_ref):
    not_top = pixel_row(lambda pixel: pixel >= SIDE)
    not_bottom = pixel_row(lambda pixel: pixel < PIX - SIDE)
    for chan in range(2):
        piece = grad_ref[chan * HALF : (chan + 1) * HALF, :]
        base = chan * 3 * HALF
        out_ref[base : base + HALF, :] = pltpu.roll(piece, PIX - SIDE, 1) * not_bottom
        out_ref[base + HALF : base + 2 * HALF, :] = piece
        out_ref[base + 2 * HALF : base + 3 * HALF, :] = pltpu.roll(piece, SIDE, 1) * not_top


def stack_gradients(grads, out_ref):
    at = 0
    for ref in grads:
        for image in range(ref.shape[0]):
            stack_gradient(ref.at[image], out_ref.at[:, at * PIX : (at + 1) * PIX])
            at += 1


def block_offset(place_ref, position):
    return pl.multiple_of(place_ref[position], 8)


def pair_rows(place, ref, pair):
    return jnp.concatenate(
        [ref[pl.ds(block_offset(place, 2 * pair + part), ROWS), :] for part in range(2)], axis=0
    )


def side_shifts(piece, out, base):
    not_left = pixel_row(lambda pixel: pixel % SIDE != 0)
    not_right = pixel_row(lambda pixel: pixel % SIDE != SIDE - 1)
    rows = piece.shape[0]
    out[base : base + rows, :] = pltpu.roll(piece, 1, 1) * not_left
    out[base + rows : base + 2 * rows, :] = piece
    out[base + 2 * rows : base + 3 * rows, :] = pltpu.roll(piece, PIX - 1, 1) * not_right


def build_stack(place, value, mask, stacks, inputs=None):
    for pair in range(PAIRS):
        piece = (silu(pair_rows(place, value, pair)) * mask).astype(LOW)
        half, at = pair // (PAIRS // 2), pair % (PAIRS // 2)
        side_shifts(piece, stacks[half], at * PIECE)
        if inputs is not None:
            inputs[half][at * PAIR : (at + 1) * PAIR, :] = piece


def back_to_channels(place_ref, product_ref, out_ref):
    pixels = product_ref.shape[1]
    column = lax.broadcasted_iota(jnp.int32, (PAIR, pixels), 1) & (SIDE - 1)
    for pair in range(PAIRS):
        base = pair * PIECE
        first = product_ref[base : base + PAIR, :]
        middle = product_ref[base + PAIR : base + 2 * PAIR, :]
        last = product_ref[base + 2 * PAIR : base + 3 * PAIR, :]
        total = (
            middle
            + jnp.where(column == SIDE - 1, 0.0, pltpu.roll(first, pixels - 1, 1))
            + jnp.where(column == 0, 0.0, pltpu.roll(last, 1, 1))
        )
        for part in range(2):
            out_ref[pl.ds(block_offset(place_ref, 2 * pair + part), ROWS), :] = total[
                part * ROWS : (part + 1) * ROWS
            ]


def count_of(mask):
    return jnp.maximum(jnp.sum(mask, axis=1, keepdims=True), 1.0) * float(WIDTH)


def small_columns(columns):
    lane = lax.broadcasted_iota(jnp.int32, (C, 128), 1)
    result = jnp.zeros((C, 128), WIDE)
    for index, column in enumerate(columns):
        result = jnp.where(lane == index, column, result)
    return result


def small_rows(columns):
    return small_columns(columns).T[:8]


def columns_of(rows):
    return jnp.concatenate([rows, jnp.zeros((120, C), WIDE)], axis=0).T


def join_halves(place, mine, theirs, out):
    own, other = half_offsets(place)
    out[pl.ds(own, HALF), :] = mine[0].astype(out.dtype)
    out[pl.ds(other, HALF), :] = theirs[0].astype(out.dtype)


def set_rows(rows, count):
    index = lax.broadcasted_iota(jnp.int32, (count, rows[0].shape[1]), 0)
    result = jnp.zeros((count, rows[0].shape[1]), WIDE)
    for at, row in enumerate(rows):
        result = jnp.where(index == at, row, result)
    return result


def three_parts(value):
    high = value.astype(LOW).astype(WIDE)
    rest = value - high
    middle = rest.astype(LOW).astype(WIDE)
    return [high, middle, rest - middle]


def load_weight(weight, pieces):
    @pl.when(pl.program_id(0) == 0)
    def _():
        for index, source in enumerate(pieces):
            weight[index * PIECE : (index + 1) * PIECE, :] = source[...]


def load_second(weight, weight_e, pieces):
    @pl.when(pl.program_id(0) == 0)
    def _():
        for index, source in enumerate(pieces):
            rows = slice(index * PIECE, (index + 1) * PIECE)
            for chan in range(2):
                base = chan * SECOND
                weight[rows, chan * 3 * HALF : (chan + 1) * 3 * HALF] = source[
                    :, base : base + 3 * HALF
                ]
                for part in range(0 if weight_e is None else 2):
                    lane = base + 3 * HALF + part * 128
                    weight_e[chan, part, rows, :] = source[:, lane : lane + 128]


def both_rows(stacks):
    return jnp.concatenate([stack[...] for stack in stacks], axis=0)


def half_offsets(place):
    own = pl.multiple_of(place[BLOCKS] * HALF, HALF)
    other = pl.multiple_of((1 - place[BLOCKS]) * HALF, HALF)
    return own, other


def prepare_kernel(
    place,
    mine,
    theirs,
    mask_ref,
    params,
    member,
    low_out,
    high_out,
    stats_out,
    value,
):
    join_halves(place, mine, theirs, value)
    mask = mask_ref[0]
    mean, factor = group_stats(value, member[...], mask, count_of(mask))
    stats_out[0] = small_rows((mean, factor))
    scale = factor * params[:, 0:1]
    value[...] = (value[...] - mean) * scale + params[:, 1:2]
    build_stack(place, value, mask, (low_out, high_out))


def first_kernel(
    place,
    mask_ref,
    member,
    pieces,
    stacks,
    normed_out,
    stats_out,
    weight,
    value,
    product,
):
    load_weight(weight, pieces)
    mask = mask_ref[0]
    product[...] = dot(weight[...], both_rows(stacks), TN)
    for chan in range(2):
        value[chan * HALF : (chan + 1) * HALF, :] = conv_out(product, chan)
    mean, factor = group_stats(value, member[...], mask, count_of(mask))
    normed_out[0] = (value[...] - mean) * factor
    stats_out[0] = small_rows((factor,))


def second_kernel(
    place,
    normed,
    stats_first,
    mine,
    theirs,
    embed_in,
    mask_ref,
    params,
    member,
    pieces,
    low_out,
    high_out,
    residual_out,
    stats_out,
    weight,
    weight_e,
    value,
    stack,
    product,
):
    load_second(weight, weight_e, pieces)
    mask = mask_ref[0]
    count = count_of(mask)
    image = pl.program_id(0)

    def own_columns(sums):
        return jnp.where(image == 0, sums[:, :6], sums[:, 6:12])

    scales, shifts = [], []
    for chan in range(2):
        low = own_columns(dot(weight_e[chan, 0], embed_in[0], TN))
        high = own_columns(dot(weight_e[chan, 1], embed_in[1], TN))
        column = jnp.concatenate(
            [
                low[:, 0:1] + low[:, 1:2] + low[:, 2:3],
                low[:, 3:4] + low[:, 4:5] + low[:, 5:6] + high[:, 0:1] + high[:, 1:2] + high[:, 2:3],
                high[:, 3:4] + high[:, 4:5] + high[:, 5:6],
            ],
            axis=0,
        )
        scales.append(column[:HALF])
        shifts.append(column[HALF:])
    time_scale = jnp.concatenate(scales, axis=0)
    time_shift = jnp.concatenate(shifts, axis=0)
    affine = normed[0] * params[:, 2:3] + params[:, 3:4]
    value[...] = affine * (1.0 + time_scale) + time_shift
    middle = TAPS // 2
    stacks = (stack.at[:middle, :], stack.at[middle:, :])
    build_stack(place, value, mask, stacks, (low_out, high_out))
    product[...] = dot(weight[...], stack[...], TN)
    for chan in range(2):
        rows = slice(chan * HALF, (chan + 1) * HALF)
        value[rows, :] = conv_out(product, chan)
    own, other = half_offsets(place)
    value[pl.ds(own, HALF), :] += mine[0].astype(WIDE)
    value[pl.ds(other, HALF), :] += theirs[0].astype(WIDE)
    residual_out[0] = value[...]
    mean, factor = group_stats(value, member[...], mask, count)
    first_factor = columns_of(stats_first[0])[:, 0:1]
    stats_out[0] = small_rows((mean, factor, time_scale, time_shift, first_factor))


def attend_kernel(
    place,
    residual,
    stats,
    mine,
    theirs,
    mask_ref,
    params,
    member,
    bundle,
    block_out,
    send_out,
    second_grad_out,
    mixed_keep,
    mixed_send,
    small_out,
    weight_f,
    attend_in,
    project,
    output,
    gradient,
    projected,
    attend_grad,
    attended,
    projected_grad,
    key_side,
    value_side,
    value_rows,
    query_side,
    grad_side,
    scores,
    probs,
    score_grads,
    accumulated,
    value,
):
    image = pl.program_id(0)

    @pl.when(image == 0)
    def _():
        for chan in range(2):
            for pair in range(PAIRS):
                block = bundle[pair][:, chan * PACKED : (chan + 1) * PACKED].astype(WIDE)
                for part in range(2):
                    for third in range(3):
                        first = third * PAIR + part * ROWS
                        weight_f[
                            chan,
                            pl.ds(block_offset(place, 2 * pair + part), ROWS),
                            third * PACKED : (third + 1) * PACKED,
                        ] = block[first : first + ROWS]
        project[...] = jnp.concatenate(
            [weight_f[0, :, : 3 * HALF], weight_f[1, :, : 3 * HALF]], axis=1
        ).astype(LOW)
        output[...] = jnp.concatenate(
            [weight_f[0, :, 3 * HALF :], weight_f[1, :, 3 * HALF :]], axis=1
        ).astype(LOW)
        accumulated[...] = jnp.zeros_like(accumulated)

    own, other = half_offsets(place)
    mask = mask_ref[0]
    count = count_of(mask)
    gradient[pl.ds(own, HALF), :] = (mine[0].astype(WIDE) * mask).astype(LOW)
    gradient[pl.ds(other, HALF), :] = (theirs[0].astype(WIDE) * mask).astype(LOW)
    columns = columns_of(stats[0])
    mean, factor = columns[:, 0:1], columns[:, 1:2]
    scale = factor * params[:, 4:5]
    attend_in[...] = ((residual[0] - mean) * scale + params[:, 5:6]).astype(LOW)
    projected[...] = dot(project[...], attend_in[...], TN).astype(LOW)
    attend_grad[...] = dot(output[...], gradient[...], TN).astype(LOW)

    penalty = mask - 1.0
    one = jnp.ones((1, PIX), WIDE)
    fill = jnp.zeros((KEYS - HEAD - 16, PIX), LOW)
    key_rows = jnp.concatenate(
        [set_rows([penalty * 9984.0, penalty * 16.0], 16).astype(LOW), fill], axis=0
    )
    one_rows = jnp.concatenate([set_rows([one, one, one], 16).astype(LOW), fill], axis=0)
    query_side[HEAD:, :] = one_rows
    grad_side[HEAD:, :] = jnp.zeros((KEYS - HEAD, PIX), LOW)

    def one_head(head, carry):
        chan = head // 3
        row_q = pl.multiple_of(chan * (3 * HALF) + (head - 3 * chan) * HEAD, HEAD)
        row_k = pl.multiple_of(row_q + HALF, HEAD)
        row_v = pl.multiple_of(row_q + 2 * HALF, HEAD)
        row_o = pl.multiple_of(head * HEAD, HEAD)
        queries = projected[pl.ds(row_q, HEAD), :]
        keys = projected[pl.ds(row_k, HEAD), :]
        values = jnp.concatenate([projected[pl.ds(row_v, HEAD), :], one_rows], axis=0)
        grads = attend_grad[pl.ds(row_o, HEAD), :].astype(WIDE)
        key_side[...] = jnp.concatenate([keys, key_rows], axis=0).T
        value_rows[...] = values[: HEAD + 16]
        value_side[...] = values.T
        query_side[:HEAD, :] = (queries.astype(WIDE) * HEAD**-0.5).astype(LOW)
        peak = None
        for start in range(0, PIX, CHUNK):
            part = dot(key_side[start : start + CHUNK, :], query_side[...], NN)
            scores[start : start + CHUNK, :] = part
            highest = jnp.max(part.reshape(CHUNK // 8, 8, PIX), axis=0)
            peak = highest if peak is None else jnp.maximum(peak, highest)
        peak = jnp.max(peak, axis=0, keepdims=True)
        for start in range(0, PIX, CHUNK):
            span = slice(start, start + CHUNK)
            probs[span, :] = jnp.exp(scores[span, :] - peak).astype(LOW)
        result = dot(value_rows[...], probs[...], NN)
        inverse = 1.0 / result[HEAD : HEAD + 1, :]
        result = result[:HEAD, :] * inverse
        attended[pl.ds(row_o, HEAD), :] = result.astype(LOW)
        scaled = grads * inverse
        delta = jnp.sum(scaled * result, axis=0, keepdims=True)
        grad_side[:HEAD, :] = scaled.astype(LOW)
        grad_side[HEAD : HEAD + 16, :] = set_rows(three_parts(-delta), 16).astype(LOW)
        for start in range(0, PIX, CHUNK):
            span = slice(start, start + CHUNK)
            part = dot(value_side[span, :], grad_side[...], NN)
            score_grads[span, :] = (probs[span, :].astype(WIDE) * part).astype(LOW)
        projected_grad[pl.ds(row_q, HEAD), :] = (
            dot(keys, score_grads[...], NN) * HEAD**-0.5
        ).astype(LOW)
        projected_grad[pl.ds(row_k, HEAD), :] = (
            dot(queries, score_grads[...], NT) * HEAD**-0.5
        ).astype(LOW)
        projected_grad[pl.ds(row_v, HEAD), :] = dot(grad_side[:HEAD, :], probs[...], NT).astype(
            LOW
        )
        return carry

    lax.fori_loop(0, C // HEAD, one_head, 0, unroll=6)

    value[...] = (residual[0] + dot(output[...], attended[...], NN)) * mask
    block_out[0] = value[pl.ds(own, HALF), :].astype(LOW)
    send_out[0] = value[pl.ds(other, HALF), :].astype(LOW)
    accumulated[:, TAPS:] += dot(gradient[...], attended[...], NT)
    accumulated[:, :TAPS] += dot(attend_in[...], projected_grad[...], NT)
    third = dot(project[...], projected_grad[...], NN)
    normed = (residual[0] - mean) * factor
    bias_third = jnp.sum(third, axis=1, keepdims=True)
    gain_third = jnp.sum(third * normed, axis=1, keepdims=True)
    gain = params[:, 4:5]
    sums = group_sums(member[...], lane_pair(gain * bias_third, gain * gain_third))
    first_sum, second_sum = sums[:, 0:1] / count, sums[:, 1:2] / count
    total = gradient[...].astype(WIDE) + factor * (
        third * gain - mask * (first_sum + normed * second_sum)
    )
    second_grad_out[0] = total.astype(LOW)
    small_out[0] = small_rows((gain_third, bias_third))

    @pl.when(image == pl.num_programs(0) - 1)
    def _():
        for pair in range(PAIRS):
            rows = pair_rows(place, accumulated, pair)
            out = mixed_keep if pair < PAIRS // 2 else mixed_send
            base = pair % (PAIRS // 2) * (JOINT - PIECE)
            third_rows = PAIR // 3
            out[base : base + PAIR, :] = rows[:, :TAPS].astype(out.dtype)
            out[base + PAIR : base + PAIR + third_rows, :] = jnp.concatenate(
                [rows[part * third_rows : (part + 1) * third_rows, TAPS:] for part in range(3)],
                axis=1,
            ).astype(out.dtype)


def side_stack(inputs, stack):
    for image in range(inputs.shape[1] // PIX):
        columns = slice(image * PIX, (image + 1) * PIX)
        for pair in range(PAIRS // 2):
            piece = inputs[pair * PAIR : (pair + 1) * PAIR, columns]
            side_shifts(piece, stack.at[:, columns], pair * PIECE)


def one_core_kernel(place, grads, inputs, total_out, grad_stack, stack):
    stack_gradients([grads], grad_stack)
    side_stack(inputs, stack)
    total_out[...] = dot(stack[...], grad_stack[...], NT)


def both_cores_kernel(place, grads, inputs, partial, mixed, *refs):
    outs, grad_stack, stack = refs[:-2], refs[-2], refs[-1]
    stack_gradients([grads], grad_stack)
    side_stack(inputs, stack)
    total = partial[...] + dot(stack[...], grad_stack[...], NT)
    extra = JOINT - PIECE
    for part, out in enumerate(outs):
        rows = slice(part * extra, (part + 1) * extra)
        out[:PIECE, :] = total[part * PIECE : (part + 1) * PIECE].astype(out.dtype)
        out[PIECE:, :] = (mixed[0][rows, :] + mixed[1][rows, :].astype(WIDE)).astype(out.dtype)


def own_filter_kernel(place, grads, stacks, send_out, keep_out, grad_stack):
    stack_gradients([grads], grad_stack)
    total = dot(both_rows(stacks), grad_stack[...], NT)
    keep_out[...] = total[: TAPS // 2]
    send_out[...] = total[TAPS // 2 :].astype(LOW)


def split_kernel(place, keep, received, *outs):
    for part, out in enumerate(outs):
        rows = slice(part * PIECE, (part + 1) * PIECE)
        out[...] = (keep[rows, :] + received[rows, :].astype(WIDE)).astype(out.dtype)


def lane_sums(value):
    return sum(value[:, lane : lane + 128] for lane in range(0, value.shape[1], 128))


def conv_back(place, grads, weight, grad_stack, product, value, slope_of, mask, normed_of):
    stack_gradient(grads.at[0], grad_stack)
    spans = [slice(start, start + PART) for start in range(0, PIX, PART)]
    plain = weighted = None
    for index in range(len(spans) + 1):
        if index < len(spans):
            span = spans[index]
            product[:, span] = dot(weight[...], grad_stack[:, span], NN)
        if index > 0:
            span = spans[index - 1]
            back_to_channels(place, product.at[:, span], value.at[:, span])
            normed = normed_of(span)
            delta = value[:, span] * mask[:, span] * slope_of(normed)
            value[:, span] = delta
            sums = lane_sums(delta), lane_sums(delta * normed)
            plain = sums[0] if plain is None else plain + sums[0]
            weighted = sums[1] if weighted is None else weighted + sums[1]
    return [jnp.sum(sums, axis=1, keepdims=True) for sums in (plain, weighted)]


def second_back_kernel(
    place,
    grads,
    pieces,
    normed_ref,
    stats,
    mask_ref,
    params,
    member,
    first_grad_out,
    small_out,
    weight,
    grad_stack,
    product,
    value,
):
    load_second(weight, None, pieces)
    mask = mask_ref[0]
    count = count_of(mask)
    gain, bias = params[:, 2:3], params[:, 3:4]
    columns = columns_of(stats[0])
    factor = columns[:, 4:5]
    time_scale, time_shift = 1.0 + columns[:, 2:3], columns[:, 3:4]

    def slope_of(normed):
        return silu_slope((normed * gain + bias) * time_scale + time_shift)

    plain, weighted = conv_back(
        place,
        grads,
        weight,
        grad_stack,
        product,
        value,
        slope_of,
        mask,
        lambda span: normed_ref[0, :, span],
    )
    normed = normed_ref[0]
    scaled = gain * time_scale
    sums = group_sums(member[...], lane_pair(scaled * plain, scaled * weighted))
    first_sum, second_sum = sums[:, 0:1] / count, sums[:, 1:2] / count
    first_grad_out[0] = (
        factor * (value[...] * scaled - mask * (first_sum + normed * second_sum))
    ).astype(LOW)
    small_out[0] = small_rows(
        (
            time_scale * weighted,
            time_scale * plain,
            gain * weighted + bias * plain,
            plain,
        )
    )


def first_back_kernel(place, *refs):
    (
        grads,
        weight,
        mine,
        theirs,
        stats_first,
        residual_grad,
        mask_ref,
        params,
        member,
        small_in,
        keep_out,
        send_out,
        small_out,
        grad_stack,
        product,
        value,
        whole,
    ) = refs[-17:]
    join_halves(place, mine, theirs, whole)
    own, other = half_offsets(place)
    mask = mask_ref[0]
    count = count_of(mask)
    gain, bias = params[:, 0:1], params[:, 1:2]
    columns = columns_of(stats_first[0])
    mean, factor = columns[:, 0:1], columns[:, 1:2]

    def normed_of(span):
        return (whole[:, span].astype(WIDE) - mean) * factor

    plain, weighted = conv_back(
        place,
        grads,
        weight,
        grad_stack,
        product,
        value,
        lambda normed: silu_slope(normed * gain + bias),
        mask,
        normed_of,
    )
    normed = normed_of(slice(None))
    sums = group_sums(member[...], lane_pair(gain * plain, gain * weighted))
    first_sum, second_sum = sums[:, 0:1] / count, sums[:, 1:2] / count
    value[...] = residual_grad[0].astype(WIDE) + factor * (
        value[...] * gain - mask * (first_sum + normed * second_sum)
    )
    keep_out[0] = value[pl.ds(own, HALF), :]
    send_out[0] = value[pl.ds(other, HALF), :].astype(LOW)
    rows = small_rows((weighted, plain))
    if len(small_in) == 0:
        small_out[...] = rows
    else:
        earlier, second, third, steps = small_in
        for ref in earlier:
            rows = rows + ref[...]
        images = second.shape[0]
        second_sum, third_sum = second[0], third[0]
        for image in range(1, images):
            second_sum, third_sum = second_sum + second[image], third_sum + third[image]
        small_out[:8, :] = set_rows(
            [
                rows[0:1],
                second_sum[0:1],
                third_sum[0:1],
                rows[1:2],
                second_sum[1:2],
                third_sum[1:2],
            ],
            8,
        )
        small_out[8:, :] = set_rows(
            [second[image, 2 + kind : 3 + kind] for kind in range(2) for image in range(images)]
            + [steps[0:1]],
            8,
        )


def cut_kernel(place, own, one, two, three, mine_out, side_out, far_out, corner_out):
    total = own[...] + one[...].astype(WIDE) + two[...].astype(WIDE) + three[...].astype(WIDE)
    left = place[BLOCKS] == 0
    outs = ((mine_out, side_out), (far_out, corner_out))
    for part in range(2):
        rows = jnp.concatenate(
            [total[tap * PAIR + part * ROWS : tap * PAIR + (part + 1) * ROWS] for tap in range(3)],
            axis=0,
        )
        halves = [rows[:, : 3 * HALF], rows[:, 3 * HALF :]]
        here, away = outs[part]
        here[...] = jnp.where(left, halves[0], halves[1]).astype(here.dtype)
        away[...] = jnp.where(left, halves[1], halves[0]).astype(away.dtype)


def unpack(rows, columns):
    return jnp.concatenate(
        [rows[:, third * columns : (third + 1) * columns] for third in range(3)], axis=0
    )


def pack(rows):
    count = rows.shape[0] // 3
    return jnp.concatenate(
        [rows[third * count : (third + 1) * count] for third in range(3)], axis=1
    )


def cut_columns_kernel(place, own, one, two, three, mine_out, side_out):
    total = own[...] + one[...].astype(WIDE) + two[...].astype(WIDE) + three[...].astype(WIDE)
    left = place[BLOCKS] == 0
    wide, output = total[: PIECE + PAIR], unpack(total[PIECE + PAIR :], C)
    halves = [
        jnp.concatenate(
            [
                wide[:, half * 3 * HALF : (half + 1) * 3 * HALF],
                pack(output[:, half * HALF : (half + 1) * HALF]),
            ],
            axis=0,
        )
        for half in range(2)
    ]
    mine_out[...] = jnp.where(left, halves[0], halves[1])
    side_out[...] = jnp.where(left, halves[1], halves[0]).astype(LOW)


def cut_rows_kernel(place, own, received, near_out, far_out):
    total = own[...] + received[...].astype(WIDE)
    output = unpack(total[PIECE + PAIR :], HALF)
    for part, out in enumerate((near_out, far_out)):
        rows = [
            total[tap * PAIR + part * ROWS : tap * PAIR + (part + 1) * ROWS] for tap in range(4)
        ]
        rows.append(pack(output[part * ROWS : (part + 1) * ROWS]))
        out[...] = jnp.concatenate(rows, axis=0).astype(out.dtype)


def finish_kernel(place, own, received, filter_out, *mixed_outs):
    total = own[...]
    for ref in received:
        total = total + ref[...].astype(WIDE)
    for down in range(3):
        for across in range(3):
            filter_out[3 * down + across] = total[
                across * ROWS : (across + 1) * ROWS, down * HALF : (down + 1) * HALF
            ]
    if mixed_outs:
        mixed_outs[0][...] = total[3 * ROWS : 4 * ROWS]
        mixed_outs[1][...] = unpack(total[4 * ROWS :], HALF)


def receive_kernel(place, carried, received, out):
    for image, ref in enumerate(received):

        @pl.when(pl.program_id(0) == image)
        def _(ref=ref):
            out[...] = ref[...].astype(out.dtype)


def shape(*sizes, dtype=WIDE):
    return jax.ShapeDtypeStruct(sizes, dtype)


def per_image(*sizes, first=0):
    return pl.BlockSpec((1,) + sizes, lambda g, place: (first + g,) + (0,) * len(sizes))


def own_image(*sizes, first=0):
    return pl.BlockSpec(
        (1,) + sizes, lambda g, place: (place[BLOCKS + 1] + first + g,) + (0,) * len(sizes)
    )


def other_image(*sizes):
    return pl.BlockSpec(
        (1,) + sizes, lambda g, place: (place[BLOCKS + 2] + g,) + (0,) * len(sizes)
    )


def per_columns(*sizes, first=0):
    return pl.BlockSpec(sizes, lambda g, place: (0, first + g))


def fixed(*sizes):
    return pl.BlockSpec(sizes, lambda g, place: (0,) * len(sizes))


def whole_array(entry):
    return fixed(*entry.shape)


def run(kernel, place, images, ins, outs, scratch, aliases=None, room=24, cost=8):
    arrays, structure = jax.tree.flatten([array for array, _ in ins])
    specs = jax.tree.leaves(
        [spec for _, spec in ins], is_leaf=lambda entry: isinstance(entry, pl.BlockSpec)
    )

    def body(place, *refs):
        given = jax.tree.unflatten(structure, refs[: len(arrays)])
        kernel(place, *given, *refs[len(arrays) :])

    return pl.pallas_call(
        body,
        grid_spec=pltpu.PrefetchScalarGridSpec(
            num_scalar_prefetch=1,
            grid=(images,),
            in_specs=specs,
            out_specs=[spec for _, spec in outs],
            scratch_shapes=scratch,
        ),
        out_shape=[out for out, _ in outs],
        input_output_aliases=aliases or {},
        compiler_params=pltpu.CompilerParams(
            dimension_semantics=("arbitrary",), vmem_limit_bytes=room * 2**20
        ),
        cost_estimate=pl.CostEstimate(flops=cost * 10**9, bytes_accessed=2**20, transcendentals=0),
    )(place, *arrays)


def filter_gradient(place, inputs, grads, mixed):
    scratch = [
        pltpu.VMEM((TAPS, grads[0].shape[0] * PIX), LOW),
        pltpu.VMEM((TAPS // 2, grads[0].shape[0] * PIX), LOW),
    ]
    partial = shape(TAPS // 2, TAPS)
    ins = (grads[0], inputs[0])
    (partial,) = run(
        one_core_kernel,
        place,
        1,
        [(entry, jax.tree.map(whole_array, entry)) for entry in ins],
        [(partial, whole_array(partial))],
        scratch,
        room=24,
    )
    ins = (grads[1], inputs[1], partial, mixed)
    outs = [shape(JOINT, TAPS)] + [shape(JOINT, TAPS, dtype=LOW)] * 3
    return run(
        both_cores_kernel,
        place,
        1,
        [(entry, jax.tree.map(whole_array, entry)) for entry in ins],
        [(out, whole_array(out)) for out in outs],
        scratch,
        room=32,
    )


def own_filter_gradient(place, stacks, grads):
    ins = (grads, stacks)
    outs = [shape(TAPS // 2, TAPS, dtype=LOW), shape(TAPS // 2, TAPS)]
    return run(
        own_filter_kernel,
        place,
        1,
        [(entry, jax.tree.map(whole_array, entry)) for entry in ins],
        [(out, whole_array(out)) for out in outs],
        [pltpu.VMEM((TAPS, grads.shape[0] * PIX), LOW)],
        room=32,
        cost=1,
    )


def simple(kernel, place, ins, outs, cost):
    return run(
        kernel,
        place,
        1,
        [(entry, jax.tree.map(whole_array, entry)) for entry in ins],
        [(out, whole_array(out)) for out in outs],
        [],
        cost=cost,
    )


def on_device(
    dp,
    features,
    pixel_masks,
    timesteps,
    first_filter,
    second_filter,
    project_weight,
    output_weight,
    embed_weight,
    norm_gains,
    norm_biases,
    cotangent,
):
    chan = lax.axis_index("chan")
    left = chan == 0
    span = dp // BLOCKS
    groups = [list(range(k * span, (k + 1) * span)) for k in range(BLOCKS)]
    block = lax.axis_index("dp") // span
    images = features.shape[0] // 2

    def swap(value, mask, flip):
        pairs = [
            (2 * d + x, 2 * (d ^ (mask * span)) + (x ^ flip)) for d in range(dp) for x in range(2)
        ]
        return lax.ppermute(value, ("dp", "chan"), pairs)

    def near(value, axis):
        if span == 1:
            return value
        return lax.all_gather(value, "dp", axis=axis, tiled=True, axis_index_groups=groups)

    def halves(mine, theirs, axis):
        return jnp.concatenate(
            [jnp.where(left, mine, theirs), jnp.where(left, theirs, mine)], axis=axis
        )

    def after(value, *others):
        return lax.optimization_barrier((value, others))[0]

    def pair_up(one, two):
        taps = one.shape[0] // ROWS
        columns = one.shape[1]
        both = [v.reshape(taps, ROWS, columns) for v in (one, two)]
        return jnp.stack(both, axis=1).reshape(2 * taps * ROWS, columns)

    def gather_one(shard, extra=None):
        side = swap(shard if extra is None else jnp.concatenate([shard, extra], axis=0), 0, 1)
        far = swap(shard, 8, 0)
        both = swap(shard, 8, 1)
        count = shard.shape[0]
        rows = pair_up(halves(shard, side[:count], 1), halves(far, both, 1))
        return rows if extra is None else (rows, side[count:])

    def gather_slow(shard, late):
        rows = after(pair_up(shard, swap(shard, 8, 0)), late)
        return rows, swap(rows, 0, 1)

    def gather_two(rows):
        return [rows, swap(rows, 4, 0), swap(rows, 2, 0), swap(rows, 6, 0)]

    def gather_three(pieces):
        return [swap(rows, 1, 0) for rows in pieces]

    def scatter_one(send, keep):
        outs = [shape(PIECE, TAPS)] + [shape(PIECE, TAPS, dtype=LOW)] * 3
        return simple(split_kernel, place, [keep, swap(send, 1, 0)], outs, 1)

    def scatter_two(keep, *sends):
        arrived = [swap(send, mask, 0) for send, mask in zip(sends, (4, 2, 6))]
        outs = [shape(3 * ROWS, 3 * HALF)] + [shape(3 * ROWS, 3 * HALF, dtype=LOW)] * 3
        return simple(cut_kernel, place, [keep] + arrived, outs, 30)

    def scatter_three(keep, *sends):
        arrived = [
            swap(send, mask, flip) for send, (mask, flip) in zip(sends, ((0, 1), (8, 0), (8, 1)))
        ]
        return simple(finish_kernel, place, [keep, arrived], [shape(9, ROWS, HALF)], 1)[0]

    def joint_two(keep, *sends, late):
        arrived = [swap(send, mask, 0) for send, mask in zip(sends, (4, 2, 6))]
        outs = [shape(JOINT, 3 * HALF), shape(JOINT, 3 * HALF, dtype=LOW)]
        return simple(cut_columns_kernel, place, [after(keep, late)] + arrived, outs, 30)

    def joint_three(keep, send, late):
        outs = [shape(JOINT // 2, 3 * HALF), shape(JOINT // 2, 3 * HALF, dtype=LOW)]
        ins = [after(keep, late), swap(send, 0, 1)]
        return simple(cut_rows_kernel, place, ins, outs, 1)

    def joint_four(keep, send, late):
        outs = [shape(9, ROWS, HALF), shape(ROWS, 3 * HALF), shape(ROWS, HALF)]
        ins = [after(keep, late), [swap(send, 8, 0)]]
        return simple(finish_kernel, place, ins, outs, 1)

    def share(value, dimension):
        if span == 1:
            return value
        return lax.psum_scatter(
            value, "dp", scatter_dimension=dimension, tiled=True, axis_index_groups=groups
        )

    def parts_of(value):
        high = value.astype(LOW)
        rest = value - high.astype(WIDE)
        middle = rest.astype(LOW)
        return [high, middle, (rest - middle.astype(WIDE)).astype(LOW)]

    own_start, other_start = chan * images, (1 - chan) * images

    def others(value):
        return lax.dynamic_slice_in_dim(value, other_start, images, 0)

    theirs = swap(others(features), 0, 1)

    def filter_rows(weight):
        rows = near(weight.astype(LOW), 1).reshape(3, 3, ROWS, HALF)
        return jnp.transpose(rows, (1, 2, 0, 3)).reshape(3 * ROWS, 3 * HALF)

    norms = jnp.concatenate([norm_gains, norm_biases], axis=0)
    norm_rows = jnp.pad(jnp.concatenate(parts_of(norms), axis=1), ((0, 2), (0, 0)))
    first_one, norm_rows = gather_one(filter_rows(first_filter), norm_rows)
    their_norms = norm_rows[:6].astype(WIDE).reshape(6, 3, HALF)
    their_norms = their_norms[:, 0] + their_norms[:, 1] + their_norms[:, 2]
    norms = halves(norms, their_norms, 1)
    params = jnp.stack([norms[0], norms[3], norms[1], norms[4], norms[2], norms[5]], axis=1)
    params = jnp.pad(params, ((0, 0), (0, 2)))
    first_pieces = gather_two(first_one)

    embed_rows = jnp.transpose(near(embed_weight.astype(LOW), 1), (1, 0, 2))
    embed_rows = jnp.transpose(embed_rows.reshape(PAIR, 3, 128), (1, 0, 2))
    embed_rows = embed_rows.reshape(2, 3 * ROWS, 128)
    bundle_rows = jnp.concatenate(
        [
            near(project_weight.astype(LOW), 0).reshape(ROWS, 3 * HALF),
            near(output_weight.astype(LOW), 1).T,
        ],
        axis=1,
    )
    bundle_rows = jnp.transpose(bundle_rows.reshape(ROWS, 3, PACKED), (1, 0, 2))
    second_rows = jnp.concatenate(
        [
            filter_rows(second_filter),
            embed_rows[0],
            embed_rows[1],
            bundle_rows.reshape(3 * ROWS, PACKED),
        ],
        axis=1,
    )
    second_one = gather_slow(second_rows, first_one)
    validity = lax.dynamic_slice_in_dim(pixel_masks, own_start, images, 0).astype(WIDE)
    validity = validity.reshape(images, 1, PIX)
    member = (jnp.arange(C)[:, None] // WIDTH == jnp.arange(C)[None, :] // WIDTH).astype(LOW)
    order = jnp.array(ORDER, jnp.int32)
    place = jnp.concatenate(
        [
            jnp.bitwise_xor(block, order) * ROWS,
            jnp.stack([chan, own_start, other_start]).astype(jnp.int32),
        ]
    )

    def time_features(steps, index, embed_width):
        half_width = embed_width // 2
        power = jnp.where(index < half_width, index, index - half_width).astype(WIDE)
        frequency = jnp.exp(-math.log(10000.0) * power / half_width)
        angles = steps[:, None] * frequency[None, :]
        return jax.nn.silu(
            jnp.where(index[None, :] < half_width, jnp.cos(angles), jnp.sin(angles))
        )

    embed_width = embed_weight.shape[1] * dp
    own_steps = lax.dynamic_slice_in_dim(timesteps, own_start, images, 0).astype(WIDE)
    flat = jnp.arange(2 * 3 * ROWS)
    third, entry_row = flat // PAIR, flat % PAIR
    embed_index = (jnp.bitwise_xor(block, order)[:, None] * PAIR + entry_row).reshape(-1)
    embed_values = time_features(after(own_steps, first_one), embed_index, embed_width)
    embed_split = jnp.stack(parts_of(embed_values), axis=2)
    embed_split = embed_split.reshape(images, PAIRS, 2, 2, 3, ROWS, 3)
    embed_split = jnp.transpose(embed_split, (0, 3, 1, 4, 2, 5, 6))
    late = (third.reshape(2, 3, ROWS) == jnp.array([1, 2])[:, None, None])
    late = late[None, :, None, :, None, :, None]
    embed_parts = jnp.concatenate(
        [jnp.where(late, 0, embed_split), jnp.where(late, embed_split, 0)], axis=6
    ).reshape(images, 2, TAPS, 6)
    embed_parts = jnp.concatenate([embed_parts[image] for image in range(images)], axis=2)
    embed_parts = jnp.pad(embed_parts, ((0, 0), (0, 0), (0, 128 - 6 * images)))
    steps_row = jnp.pad(own_steps, (0, HALF - images))
    steps_row = jnp.pad(jnp.concatenate([steps_row, steps_row])[None, :], ((0, 7), (0, 0)))

    value_scratch = pltpu.VMEM((C, PIX), WIDE)
    product_scratch = pltpu.VMEM((TAPS, PIX), WIDE)
    back_scratch = [pltpu.VMEM((TAPS, PIX), LOW), product_scratch, value_scratch]
    mask_in = (validity, per_image(1, PIX))
    params_in = (params, fixed(C, 8))
    member_in = (member, fixed(C, C))
    image_low = (shape(images, C, PIX, dtype=LOW), per_image(C, PIX))
    image_wide = (shape(images, C, PIX), per_image(C, PIX))
    image_rows = (shape(images, 8, C), per_image(8, C))
    weight_out = (shape(TAPS, TAPS, dtype=LOW), fixed(TAPS, TAPS))
    stack_out = (shape(TAPS // 2, images * PIX, dtype=LOW), per_columns(TAPS // 2, PIX))
    input_out = (shape(C // 2, images * PIX, dtype=LOW), per_columns(C // 2, PIX))
    anywhere = pl.BlockSpec(memory_space=pl.ANY)

    prepared = run(
        prepare_kernel,
        place,
        images,
        [
            (features, own_image(HALF, PIX)),
            (theirs, per_image(HALF, PIX)),
            mask_in,
            params_in,
            member_in,
        ],
        [stack_out, stack_out, image_rows],
        [value_scratch],
    )
    first_low, first_high, stats_whole = prepared
    cots = others(after(cotangent, first_one))
    first_pieces = first_pieces + gather_three(after(first_pieces, first_low))
    mine, side = after(second_one, first_low)
    second_one = halves(mine[:, :SECOND], side[:, :SECOND], 1)
    bundle_one = halves(mine[:, SECOND:], side[:, SECOND:], 1)
    second_normed, stats_first, first_weight = run(
        first_kernel,
        place,
        images,
        [
            mask_in,
            member_in,
            (first_pieces, [fixed(PIECE, TAPS)] * 8),
            (after([first_low, first_high], second_one, cots, embed_parts, steps_row), [per_columns(TAPS // 2, PIX)] * 2),
        ],
        [image_wide, image_rows, weight_out],
        [value_scratch, product_scratch],
    )
    second_pieces = gather_two(second_one)
    second_pieces = second_pieces + gather_three(after(second_pieces, second_normed))
    bundle_pieces = gather_two(bundle_one)
    their_cots = swap(after(cots, first_low), 0, 1)
    second_low, second_high, residual, stats_second = run(
        second_kernel,
        place,
        images,
        [
            (after(second_normed, bundle_one), per_image(C, PIX)),
            (stats_first, per_image(8, C)),
            (features, own_image(HALF, PIX)),
            (theirs, per_image(HALF, PIX)),
            (embed_parts, fixed(2, TAPS, 128)),
            mask_in,
            params_in,
            member_in,
            (second_pieces, [fixed(PIECE, 2 * SECOND)] * 8),
        ],
        [input_out, input_out, image_wide, image_rows],
        [
            pltpu.VMEM((TAPS, TAPS), LOW),
            pltpu.VMEM((2, 2, TAPS, 128), LOW),
            value_scratch,
            pltpu.VMEM((TAPS, PIX), LOW),
            product_scratch,
        ],
        room=60,
    )
    bundle_pieces = bundle_pieces + gather_three(after(bundle_pieces, residual))
    second_theirs = swap(second_high, 1, 0)
    mixed_rows = PAIRS // 2 * (JOINT - PIECE)
    block_keep, block_send, second_grad, *mixed, small_third = run(
        attend_kernel,
        place,
        images,
        [
            (residual, per_image(C, PIX)),
            (stats_second, per_image(8, C)),
            (cotangent, own_image(HALF, PIX)),
            (their_cots, per_image(HALF, PIX)),
            mask_in,
            params_in,
            member_in,
            (bundle_pieces, [fixed(PIECE, 2 * PACKED)] * 8),
        ],
        [
            (shape(2 * images, HALF, PIX, dtype=LOW), own_image(HALF, PIX)),
            (shape(images, HALF, PIX, dtype=LOW), per_image(HALF, PIX)),
            image_low,
            (shape(mixed_rows, TAPS), fixed(mixed_rows, TAPS)),
            (shape(mixed_rows, TAPS, dtype=LOW), fixed(mixed_rows, TAPS)),
            image_rows,
        ],
        [
            pltpu.VMEM((2, C, 2 * C), WIDE),
            pltpu.VMEM((C, PIX), LOW),
            pltpu.VMEM((C, TAPS), LOW),
            pltpu.VMEM((C, C), LOW),
            pltpu.VMEM((C, PIX), LOW),
            pltpu.VMEM((TAPS, PIX), LOW),
            pltpu.VMEM((C, PIX), LOW),
            pltpu.VMEM((C, PIX), LOW),
            pltpu.VMEM((TAPS, PIX), LOW),
            pltpu.VMEM((PIX, KEYS), LOW),
            pltpu.VMEM((PIX, KEYS), LOW),
            pltpu.VMEM((HEAD + 16, PIX), LOW),
            pltpu.VMEM((KEYS, PIX), LOW),
            pltpu.VMEM((KEYS, PIX), LOW),
            pltpu.VMEM((PIX, PIX), WIDE),
            pltpu.VMEM((PIX, PIX), LOW),
            pltpu.VMEM((PIX, PIX), LOW),
            pltpu.VMEM((C, TAPS + C), WIDE),
            value_scratch,
        ],
        room=62,
        cost=60,
    )
    block_theirs = swap(block_send, 0, 1)
    mixed = [mixed[0], swap(mixed[1], 1, 0)]
    grads_theirs = swap(second_grad, 1, 0)
    joint = filter_gradient(
        place, [second_low, second_theirs], [second_grad, grads_theirs], mixed
    )
    first_grad, small_second = run(
        second_back_kernel,
        place,
        images,
        [
            (after(second_grad, joint), per_image(C, PIX)),
            (second_pieces, [fixed(PIECE, 2 * SECOND)] * 8),
            (second_normed, per_image(C, PIX)),
            (stats_second, per_image(8, C)),
            mask_in,
            params_in,
            member_in,
        ],
        [image_low, image_rows],
        [pltpu.VMEM((TAPS, TAPS), LOW)] + back_scratch,
        room=32,
    )
    masked_out = lax.dynamic_update_slice_in_dim(
        after(block_keep, joint), block_theirs, other_start, 0
    )
    send, keep = own_filter_gradient(
        place, [first_low, first_high], after(first_grad, masked_out)
    )
    first_part = scatter_one(send, keep)
    joint = joint_two(*joint, late=send)
    input_grad, input_theirs, smalls = None, [], []
    back_grad = after(first_grad, first_part, joint)
    for image in range(images):
        last = image == images - 1
        small_in = (smalls, small_second, small_third, steps_row) if last else ()
        carried = [] if input_grad is None else [(input_grad, anywhere)]
        small_shape = shape(16 if last else 8, C)
        input_grad, input_send, small = run(
            first_back_kernel,
            place,
            1,
            carried
            + [
                (back_grad, per_image(C, PIX, first=image)),
                (first_weight, fixed(TAPS, TAPS)),
                (features, own_image(HALF, PIX, first=image)),
                (theirs, per_image(HALF, PIX, first=image)),
                (stats_whole, per_image(8, C, first=image)),
                (second_grad, per_image(C, PIX, first=image)),
                (validity, per_image(1, PIX, first=image)),
                params_in,
                member_in,
                (small_in, jax.tree.map(whole_array, small_in)),
            ],
            [
                (shape(2 * images, HALF, PIX), own_image(HALF, PIX, first=image)),
                (shape(1, HALF, PIX, dtype=LOW), per_image(HALF, PIX)),
                (small_shape, whole_array(small_shape)),
            ],
            back_scratch + [pltpu.VMEM((C, PIX), LOW)],
            {1: 0} if carried else None,
        )
        smalls.append(small)
        input_theirs.append(swap(input_send, 0, 1))
        if image == 0:
            joint = joint_three(*joint, late=small)
            back_grad = after(back_grad, joint)
    first_part = scatter_two(*first_part)
    message = after(smalls[-1], input_theirs[:-1])

    def merge(arrived):
        total = sum(message[:8] for message in arrived)
        return jnp.concatenate([total] + [message[8:] for message in arrived], axis=0)

    message = after(merge([message, swap(message, 1, 0)]), first_part)
    joint = joint_four(*joint, late=first_part)
    grad_first = share(scatter_three(*first_part), 1)
    grad_second = share(joint[0], 1)
    grad_project = share(joint[1].reshape(ROWS, 3, HALF), 0)
    grad_output = share(joint[2].T, 1)
    (input_grad,) = run(
        receive_kernel,
        place,
        images,
        [(input_grad, anywhere), (input_theirs, [fixed(1, HALF, PIX)] * images)],
        [(shape(2 * images, HALF, PIX), other_image(HALF, PIX))],
        [],
        {1: 0},
        cost=1,
    )

    message = merge([message, swap(message, 4, 0)])
    message = merge([message, swap(message, 2, 0)])
    one, two = after(message[:, :HALF], input_theirs[-1]), message[:, HALF:]
    own, away = jnp.where(left, one, two), jnp.where(left, two, one)
    message = merge([own, swap(away, 0, 1), swap(own, 8, 0), swap(away, 8, 1)])
    total, entries = message[:6], message[8:]
    if span > 1:
        total = lax.psum(total, "dp", axis_index_groups=groups)
        entries = lax.all_gather(entries, "dp", axis=0, tiled=True, axis_index_groups=groups)
    entries = entries.reshape(-1, 8, HALF)
    all_steps = entries[:, 2 * images, :images].reshape(-1)
    scale_grads = entries[:, :images].reshape(-1, HALF)
    shift_grads = entries[:, images : 2 * images].reshape(-1, HALF)
    rows = embed_weight.shape[1]
    row_index = lax.axis_index("dp") * rows + jnp.arange(rows)
    all_embed = time_features(all_steps, row_index, embed_width)
    grad_embed = jnp.einsum(
        "be,kbd->ked",
        all_embed,
        jnp.stack([scale_grads, shift_grads]),
        precision=lax.Precision.HIGHEST,
    )
    return (
        masked_out,
        input_grad,
        grad_first,
        grad_second,
        grad_project,
        grad_output,
        grad_embed,
        total[:3],
        total[3:],
    )


def solution(mesh):
    in_specs = (
        P("dp", "chan", None),
        P("dp", None),
        P("dp"),
        P(None, "dp", "chan"),
        P(None, "dp", "chan"),
        P("dp", None, "chan"),
        P("chan", "dp"),
        P(None, "dp", "chan"),
        P(None, "chan"),
        P(None, "chan"),
        P("dp", "chan", None),
    )
    out_specs = (
        P("dp", "chan", None),
        P("dp", "chan", None),
        P(None, "dp", "chan"),
        P(None, "dp", "chan"),
        P("dp", None, "chan"),
        P("chan", "dp"),
        P(None, "dp", "chan"),
        P(None, "chan"),
        P(None, "chan"),
    )
    return jax.shard_map(
        functools.partial(on_device, mesh.shape["dp"]),
        mesh=mesh,
        in_specs=in_specs,
        out_specs=out_specs,
        check_vma=False,
    )
```

```python
import functools
import math

import jax
import jax.numpy as jnp
from jax import lax
from jax.experimental import pallas as pl
from jax.experimental.pallas import tpu as pltpu
from jax.sharding import PartitionSpec as P

C = 384
HALF = 192
HEAD = 64
GROUPS = 32
WIDTH = C // GROUPS
SIDE = 32
PIX = SIDE * SIDE
BLOCKS = 16
ROWS = C // BLOCKS
TAPS = 3 * C
EPSILON = 1e-05
SECOND = 3 * HALF + 256
MIXED = 4 * HALF
PACKED = MIXED // 3
PAIR = 2 * ROWS
PIECE = 3 * PAIR
JOINT = PIECE + PAIR + PAIR // 3
PAIRS = BLOCKS // 2
KEYS = 128
CHUNK = 256
PART = 512
LOW = jnp.bfloat16
WIDE = jnp.float32
ORDER = (0, 8, 4, 12, 2, 10, 6, 14, 1, 9, 5, 13, 3, 11, 7, 15)

NN = (((1,), (0,)), ((), ()))
NT = (((1,), (1,)), ((), ()))
TN = (((0,), (0,)), ((), ()))


def dot(left, right, dims):
    return lax.dot_general(left, right, dims, preferred_element_type=WIDE)


def pixel_row(keep):
    pixel = lax.broadcasted_iota(jnp.int32, (1, PIX), 1)
    return jnp.where(keep(pixel), 1.0, 0.0).astype(LOW)


def lane_pair(first, second):
    lane = lax.broadcasted_iota(jnp.int32, (C, 128), 1)
    return jnp.where(lane == 0, first, jnp.where(lane == 1, second, 0.0))


def group_sums(member, values):
    high = values.astype(LOW)
    rest = values - high.astype(WIDE)
    middle = rest.astype(LOW)
    low = (rest - middle.astype(WIDE)).astype(LOW)
    return dot(member, high, NN) + dot(member, middle, NN) + dot(member, low, NN)


def group_sum(member, column):
    return group_sums(member, jnp.broadcast_to(column, (C, 128)))[:, 0:1]


def group_stats(value_ref, member, mask, count):
    mean = group_sum(member, jnp.sum(value_ref[...] * mask, axis=1, keepdims=True)) / count
    centred = value_ref[...] - mean
    variance = (
        group_sum(member, jnp.sum(centred * centred * mask, axis=1, keepdims=True)) / count
    )
    return mean, lax.rsqrt(variance + EPSILON)


def silu(value):
    return value / (1.0 + jnp.exp(-value))


def silu_slope(value):
    squashed = 1.0 / (1.0 + jnp.exp(-value))
    return squashed * (1.0 + value * (1.0 - squashed))


def shift_down(piece):
    pixel = lax.broadcasted_iota(jnp.int32, piece.shape, 1)
    return jnp.where(pixel < SIDE, 0.0, pltpu.roll(piece, SIDE, 1))


def shift_up(piece):
    pixel = lax.broadcasted_iota(jnp.int32, piece.shape, 1)
    return jnp.where(pixel >= PIX - SIDE, 0.0, pltpu.roll(piece, PIX - SIDE, 1))


def conv_out(product_ref, chan):
    base = chan * 3 * HALF
    return (
        product_ref[base + HALF : base + 2 * HALF, :]
        + shift_down(product_ref[base : base + HALF, :])
        + shift_up(product_ref[base + 2 * HALF : base + 3 * HALF, :])
    )


def stack_gradient(grad_ref, out_ref):
    not_top = pixel_row(lambda pixel: pixel >= SIDE)
    not_bottom = pixel_row(lambda pixel: pixel < PIX - SIDE)
    for chan in range(2):
        piece = grad_ref[chan * HALF : (chan + 1) * HALF, :]
        base = chan * 3 * HALF
        out_ref[base : base + HALF, :] = pltpu.roll(piece, PIX - SIDE, 1) * not_bottom
        out_ref[base + HALF : base + 2 * HALF, :] = piece
        out_ref[base + 2 * HALF : base + 3 * HALF, :] = pltpu.roll(piece, SIDE, 1) * not_top


def stack_gradients(grads, out_ref):
    at = 0
    for ref in grads:
        for image in range(ref.shape[0]):
            stack_gradient(ref.at[image], out_ref.at[:, at * PIX : (at + 1) * PIX])
            at += 1


def block_offset(place_ref, position):
    return pl.multiple_of(place_ref[position], 8)


def pair_rows(place, ref, pair):
    return jnp.concatenate(
        [ref[pl.ds(block_offset(place, 2 * pair + part), ROWS), :] for part in range(2)], axis=0
    )


def side_shifts(piece, out, base):
    not_left = pixel_row(lambda pixel: pixel % SIDE != 0)
    not_right = pixel_row(lambda pixel: pixel % SIDE != SIDE - 1)
    rows = piece.shape[0]
    out[base : base + rows, :] = pltpu.roll(piece, 1, 1) * not_left
    out[base + rows : base + 2 * rows, :] = piece
    out[base + 2 * rows : base + 3 * rows, :] = pltpu.roll(piece, PIX - 1, 1) * not_right


def build_stack(place, value, mask, stacks, inputs=None):
    for pair in range(PAIRS):
        piece = (silu(pair_rows(place, value, pair)) * mask).astype(LOW)
        half, at = pair // (PAIRS // 2), pair % (PAIRS // 2)
        side_shifts(piece, stacks[half], at * PIECE)
        if inputs is not None:
            inputs[half][at * PAIR : (at + 1) * PAIR, :] = piece


def back_to_channels(place_ref, product_ref, out_ref):
    pixels = product_ref.shape[1]
    column = lax.broadcasted_iota(jnp.int32, (PAIR, pixels), 1) & (SIDE - 1)
    for pair in range(PAIRS):
        base = pair * PIECE
        first = product_ref[base : base + PAIR, :]
        middle = product_ref[base + PAIR : base + 2 * PAIR, :]
        last = product_ref[base + 2 * PAIR : base + 3 * PAIR, :]
        total = (
            middle
            + jnp.where(column == SIDE - 1, 0.0, pltpu.roll(first, pixels - 1, 1))
            + jnp.where(column == 0, 0.0, pltpu.roll(last, 1, 1))
        )
        for part in range(2):
            out_ref[pl.ds(block_offset(place_ref, 2 * pair + part), ROWS), :] = total[
                part * ROWS : (part + 1) * ROWS
            ]


def count_of(mask):
    return jnp.maximum(jnp.sum(mask, axis=1, keepdims=True), 1.0) * float(WIDTH)


def small_columns(columns):
    lane = lax.broadcasted_iota(jnp.int32, (C, 128), 1)
    result = jnp.zeros((C, 128), WIDE)
    for index, column in enumerate(columns):
        result = jnp.where(lane == index, column, result)
    return result


def small_rows(columns):
    return small_columns(columns).T[:8]


def columns_of(rows):
    return jnp.concatenate([rows, jnp.zeros((120, C), WIDE)], axis=0).T


def join_halves(place, mine, theirs, out):
    own, other = half_offsets(place)
    out[pl.ds(own, HALF), :] = mine[0].astype(out.dtype)
    out[pl.ds(other, HALF), :] = theirs[0].astype(out.dtype)


def set_rows(rows, count):
    index = lax.broadcasted_iota(jnp.int32, (count, rows[0].shape[1]), 0)
    result = jnp.zeros((count, rows[0].shape[1]), WIDE)
    for at, row in enumerate(rows):
        result = jnp.where(index == at, row, result)
    return result


def three_parts(value):
    high = value.astype(LOW).astype(WIDE)
    rest = value - high
    middle = rest.astype(LOW).astype(WIDE)
    return [high, middle, rest - middle]


def load_weight(weight, pieces):
    @pl.when(pl.program_id(0) == 0)
    def _():
        for index, source in enumerate(pieces):
            weight[index * PIECE : (index + 1) * PIECE, :] = source[...]


def load_second(weight, weight_e, pieces):
    @pl.when(pl.program_id(0) == 0)
    def _():
        for index, source in enumerate(pieces):
            rows = slice(index * PIECE, (index + 1) * PIECE)
            for chan in range(2):
                base = chan * SECOND
                weight[rows, chan * 3 * HALF : (chan + 1) * 3 * HALF] = source[
                    :, base : base + 3 * HALF
                ]
                for part in range(0 if weight_e is None else 2):
                    lane = base + 3 * HALF + part * 128
                    weight_e[chan, part, rows, :] = source[:, lane : lane + 128]


def both_rows(stacks):
    return jnp.concatenate([stack[...] for stack in stacks], axis=0)


def half_offsets(place):
    own = pl.multiple_of(place[BLOCKS] * HALF, HALF)
    other = pl.multiple_of((1 - place[BLOCKS]) * HALF, HALF)
    return own, other


def prepare_kernel(
    place,
    mine,
    theirs,
    mask_ref,
    params,
    member,
    low_out,
    high_out,
    stats_out,
    value,
):
    join_halves(place, mine, theirs, value)
    mask = mask_ref[0]
    mean, factor = group_stats(value, member[...], mask, count_of(mask))
    stats_out[0] = small_rows((mean, factor))
    scale = factor * params[:, 0:1]
    value[...] = (value[...] - mean) * scale + params[:, 1:2]
    build_stack(place, value, mask, (low_out, high_out))


def first_kernel(
    place,
    mask_ref,
    member,
    pieces,
    stacks,
    normed_out,
    stats_out,
    weight,
    value,
    product,
):
    load_weight(weight, pieces)
    mask = mask_ref[0]
    product[...] = dot(weight[...], both_rows(stacks), TN)
    for chan in range(2):
        value[chan * HALF : (chan + 1) * HALF, :] = conv_out(product, chan)
    mean, factor = group_stats(value, member[...], mask, count_of(mask))
    normed_out[0] = (value[...] - mean) * factor
    stats_out[0] = small_rows((factor,))


def second_kernel(
    place,
    normed,
    stats_first,
    mine,
    theirs,
    embed_in,
    mask_ref,
    params,
    member,
    pieces,
    low_out,
    high_out,
    residual_out,
    stats_out,
    weight,
    weight_e,
    sums,
    value,
    stack,
    product,
):
    load_second(weight, weight_e, pieces)
    mask = mask_ref[0]
    count = count_of(mask)
    image = pl.program_id(0)

    @pl.when(image == 0)
    def _():
        for chan in range(2):
            for part in range(2):
                sums[chan, part] = dot(weight_e[chan, part], embed_in[part], TN)

    def own_columns(both):
        return jnp.where(image == 0, both[:, :6], both[:, 6:12])

    scales, shifts = [], []
    for chan in range(2):
        low, high = own_columns(sums[chan, 0]), own_columns(sums[chan, 1])
        column = jnp.concatenate(
            [
                low[:, 0:1] + low[:, 1:2] + low[:, 2:3],
                low[:, 3:4] + low[:, 4:5] + low[:, 5:6] + high[:, 0:1] + high[:, 1:2] + high[:, 2:3],
                high[:, 3:4] + high[:, 4:5] + high[:, 5:6],
            ],
            axis=0,
        )
        scales.append(column[:HALF])
        shifts.append(column[HALF:])
    time_scale = jnp.concatenate(scales, axis=0)
    time_shift = jnp.concatenate(shifts, axis=0)
    affine = normed[0] * params[:, 2:3] + params[:, 3:4]
    value[...] = affine * (1.0 + time_scale) + time_shift
    middle = TAPS // 2
    stacks = (stack.at[:middle, :], stack.at[middle:, :])
    build_stack(place, value, mask, stacks, (low_out, high_out))
    product[...] = dot(weight[...], stack[...], TN)
    for chan in range(2):
        rows = slice(chan * HALF, (chan + 1) * HALF)
        value[rows, :] = conv_out(product, chan)
    own, other = half_offsets(place)
    value[pl.ds(own, HALF), :] += mine[0].astype(WIDE)
    value[pl.ds(other, HALF), :] += theirs[0].astype(WIDE)
    residual_out[0] = value[...]
    mean, factor = group_stats(value, member[...], mask, count)
    first_factor = columns_of(stats_first[0])[:, 0:1]
    stats_out[0] = small_rows((mean, factor, time_scale, time_shift, first_factor))


def attend_kernel(
    place,
    residual,
    stats,
    mine,
    theirs,
    mask_ref,
    params,
    member,
    bundle,
    block_out,
    send_out,
    second_grad_out,
    mixed_keep,
    mixed_send,
    small_out,
    weight_f,
    attend_in,
    project,
    output,
    gradient,
    projected,
    attend_grad,
    attended,
    projected_grad,
    key_side,
    value_side,
    value_rows,
    query_side,
    grad_side,
    scores,
    probs,
    score_grads,
    accumulated,
    value,
):
    image = pl.program_id(0)

    @pl.when(image == 0)
    def _():
        for chan in range(2):
            for pair in range(PAIRS):
                block = bundle[pair][:, chan * PACKED : (chan + 1) * PACKED].astype(WIDE)
                for part in range(2):
                    for third in range(3):
                        first = third * PAIR + part * ROWS
                        weight_f[
                            chan,
                            pl.ds(block_offset(place, 2 * pair + part), ROWS),
                            third * PACKED : (third + 1) * PACKED,
                        ] = block[first : first + ROWS]
        project[...] = jnp.concatenate(
            [weight_f[0, :, : 3 * HALF], weight_f[1, :, : 3 * HALF]], axis=1
        ).astype(LOW)
        output[...] = jnp.concatenate(
            [weight_f[0, :, 3 * HALF :], weight_f[1, :, 3 * HALF :]], axis=1
        ).astype(LOW)
        accumulated[...] = jnp.zeros_like(accumulated)

    own, other = half_offsets(place)
    mask = mask_ref[0]
    count = count_of(mask)
    gradient[pl.ds(own, HALF), :] = (mine[0].astype(WIDE) * mask).astype(LOW)
    gradient[pl.ds(other, HALF), :] = (theirs[0].astype(WIDE) * mask).astype(LOW)
    columns = columns_of(stats[0])
    mean, factor = columns[:, 0:1], columns[:, 1:2]
    scale = factor * params[:, 4:5]
    attend_in[...] = ((residual[0] - mean) * scale + params[:, 5:6]).astype(LOW)
    projected[...] = dot(project[...], attend_in[...], TN).astype(LOW)
    attend_grad[...] = dot(output[...], gradient[...], TN).astype(LOW)

    penalty = mask - 1.0
    one = jnp.ones((1, PIX), WIDE)
    fill = jnp.zeros((KEYS - HEAD - 16, PIX), LOW)
    key_rows = jnp.concatenate(
        [set_rows([penalty * 9984.0, penalty * 16.0], 16).astype(LOW), fill], axis=0
    )
    one_rows = jnp.concatenate([set_rows([one, one, one], 16).astype(LOW), fill], axis=0)
    query_side[HEAD:, :] = one_rows
    grad_side[HEAD:, :] = jnp.zeros((KEYS - HEAD, PIX), LOW)

    def one_head(head, carry):
        chan = head // 3
        row_q = pl.multiple_of(chan * (3 * HALF) + (head - 3 * chan) * HEAD, HEAD)
        row_k = pl.multiple_of(row_q + HALF, HEAD)
        row_v = pl.multiple_of(row_q + 2 * HALF, HEAD)
        row_o = pl.multiple_of(head * HEAD, HEAD)
        queries = projected[pl.ds(row_q, HEAD), :]
        keys = projected[pl.ds(row_k, HEAD), :]
        values = jnp.concatenate([projected[pl.ds(row_v, HEAD), :], one_rows], axis=0)
        grads = attend_grad[pl.ds(row_o, HEAD), :].astype(WIDE)
        key_side[...] = jnp.concatenate([keys, key_rows], axis=0).T
        value_rows[...] = values[: HEAD + 16]
        value_side[...] = values.T
        query_side[:HEAD, :] = (queries.astype(WIDE) * HEAD**-0.5).astype(LOW)
        peak = None
        for start in range(0, PIX, CHUNK):
            part = dot(key_side[start : start + CHUNK, :], query_side[...], NN)
            scores[start : start + CHUNK, :] = part
            highest = jnp.max(part.reshape(CHUNK // 8, 8, PIX), axis=0)
            peak = highest if peak is None else jnp.maximum(peak, highest)
        peak = jnp.max(peak, axis=0, keepdims=True)
        for start in range(0, PIX, CHUNK):
            span = slice(start, start + CHUNK)
            probs[span, :] = jnp.exp(scores[span, :] - peak).astype(LOW)
        result = dot(value_rows[...], probs[...], NN)
        inverse = 1.0 / result[HEAD : HEAD + 1, :]
        result = result[:HEAD, :] * inverse
        attended[pl.ds(row_o, HEAD), :] = result.astype(LOW)
        scaled = grads * inverse
        delta = jnp.sum(scaled * result, axis=0, keepdims=True)
        grad_side[:HEAD, :] = scaled.astype(LOW)
        grad_side[HEAD : HEAD + 16, :] = set_rows(three_parts(-delta), 16).astype(LOW)
        for start in range(0, PIX, CHUNK):
            span = slice(start, start + CHUNK)
            part = dot(value_side[span, :], grad_side[...], NN)
            score_grads[span, :] = (probs[span, :].astype(WIDE) * part).astype(LOW)
        projected_grad[pl.ds(row_q, HEAD), :] = (
            dot(keys, score_grads[...], NN) * HEAD**-0.5
        ).astype(LOW)
        projected_grad[pl.ds(row_k, HEAD), :] = (
            dot(queries, score_grads[...], NT) * HEAD**-0.5
        ).astype(LOW)
        projected_grad[pl.ds(row_v, HEAD), :] = dot(grad_side[:HEAD, :], probs[...], NT).astype(
            LOW
        )
        return carry

    lax.fori_loop(0, C // HEAD, one_head, 0, unroll=6)

    value[...] = (residual[0] + dot(output[...], attended[...], NN)) * mask
    block_out[0] = value[pl.ds(own, HALF), :].astype(LOW)
    send_out[0] = value[pl.ds(other, HALF), :].astype(LOW)
    accumulated[:, TAPS:] += dot(gradient[...], attended[...], NT)
    accumulated[:, :TAPS] += dot(attend_in[...], projected_grad[...], NT)
    third = dot(project[...], projected_grad[...], NN)
    normed = (residual[0] - mean) * factor
    bias_third = jnp.sum(third, axis=1, keepdims=True)
    gain_third = jnp.sum(third * normed, axis=1, keepdims=True)
    gain = params[:, 4:5]
    sums = group_sums(member[...], lane_pair(gain * bias_third, gain * gain_third))
    first_sum, second_sum = sums[:, 0:1] / count, sums[:, 1:2] / count
    total = gradient[...].astype(WIDE) + factor * (
        third * gain - mask * (first_sum + normed * second_sum)
    )
    second_grad_out[0] = total.astype(LOW)
    small_out[0] = small_rows((gain_third, bias_third))

    @pl.when(image == pl.num_programs(0) - 1)
    def _():
        for pair in range(PAIRS):
            rows = pair_rows(place, accumulated, pair)
            out = mixed_keep if pair < PAIRS // 2 else mixed_send
            base = pair % (PAIRS // 2) * (JOINT - PIECE)
            third_rows = PAIR // 3
            out[base : base + PAIR, :] = rows[:, :TAPS].astype(out.dtype)
            out[base + PAIR : base + PAIR + third_rows, :] = jnp.concatenate(
                [rows[part * third_rows : (part + 1) * third_rows, TAPS:] for part in range(3)],
                axis=1,
            ).astype(out.dtype)


def side_stack(inputs, stack):
    for image in range(inputs.shape[1] // PIX):
        columns = slice(image * PIX, (image + 1) * PIX)
        for pair in range(PAIRS // 2):
            piece = inputs[pair * PAIR : (pair + 1) * PAIR, columns]
            side_shifts(piece, stack.at[:, columns], pair * PIECE)


def one_core_kernel(place, grads, inputs, total_out, grad_stack, stack):
    stack_gradients([grads], grad_stack)
    side_stack(inputs, stack)
    total_out[...] = dot(stack[...], grad_stack[...], NT)


def both_cores_kernel(place, grads, inputs, partial, mixed, *refs):
    outs, grad_stack, stack = refs[:-2], refs[-2], refs[-1]
    stack_gradients([grads], grad_stack)
    side_stack(inputs, stack)
    total = partial[...] + dot(stack[...], grad_stack[...], NT)
    extra = JOINT - PIECE
    for part, out in enumerate(outs):
        rows = slice(part * extra, (part + 1) * extra)
        out[:PIECE, :] = total[part * PIECE : (part + 1) * PIECE].astype(out.dtype)
        out[PIECE:, :] = (mixed[0][rows, :] + mixed[1][rows, :].astype(WIDE)).astype(out.dtype)


def own_filter_kernel(place, grads, stacks, send_out, keep_out, grad_stack):
    stack_gradients([grads], grad_stack)
    total = dot(both_rows(stacks), grad_stack[...], NT)
    keep_out[...] = total[: TAPS // 2]
    send_out[...] = total[TAPS // 2 :].astype(LOW)


def split_kernel(place, keep, received, *outs):
    for part, out in enumerate(outs):
        rows = slice(part * PIECE, (part + 1) * PIECE)
        out[...] = (keep[rows, :] + received[rows, :].astype(WIDE)).astype(out.dtype)


def lane_sums(value):
    return sum(value[:, lane : lane + 128] for lane in range(0, value.shape[1], 128))


def conv_back(place, grads, weight, grad_stack, product, value, slope_of, mask, normed_of):
    stack_gradient(grads.at[0], grad_stack)
    spans = [slice(start, start + PART) for start in range(0, PIX, PART)]
    plain = weighted = None
    for index in range(len(spans) + 1):
        if index < len(spans):
            span = spans[index]
            product[:, span] = dot(weight[...], grad_stack[:, span], NN)
        if index > 0:
            span = spans[index - 1]
            back_to_channels(place, product.at[:, span], value.at[:, span])
            normed = normed_of(span)
            delta = value[:, span] * mask[:, span] * slope_of(normed)
            value[:, span] = delta
            sums = lane_sums(delta), lane_sums(delta * normed)
            plain = sums[0] if plain is None else plain + sums[0]
            weighted = sums[1] if weighted is None else weighted + sums[1]
    return [jnp.sum(sums, axis=1, keepdims=True) for sums in (plain, weighted)]


def second_back_kernel(
    place,
    grads,
    pieces,
    normed_ref,
    stats,
    mask_ref,
    params,
    member,
    first_grad_out,
    small_out,
    weight,
    grad_stack,
    product,
    value,
):
    load_second(weight, None, pieces)
    mask = mask_ref[0]
    count = count_of(mask)
    gain, bias = params[:, 2:3], params[:, 3:4]
    columns = columns_of(stats[0])
    factor = columns[:, 4:5]
    time_scale, time_shift = 1.0 + columns[:, 2:3], columns[:, 3:4]

    def slope_of(normed):
        return silu_slope((normed * gain + bias) * time_scale + time_shift)

    plain, weighted = conv_back(
        place,
        grads,
        weight,
        grad_stack,
        product,
        value,
        slope_of,
        mask,
        lambda span: normed_ref[0, :, span],
    )
    normed = normed_ref[0]
    scaled = gain * time_scale
    sums = group_sums(member[...], lane_pair(scaled * plain, scaled * weighted))
    first_sum, second_sum = sums[:, 0:1] / count, sums[:, 1:2] / count
    first_grad_out[0] = (
        factor * (value[...] * scaled - mask * (first_sum + normed * second_sum))
    ).astype(LOW)
    small_out[0] = small_rows(
        (
            time_scale * weighted,
            time_scale * plain,
            gain * weighted + bias * plain,
            plain,
        )
    )


def first_back_kernel(place, *refs):
    (
        grads,
        weight,
        mine,
        theirs,
        stats_first,
        residual_grad,
        mask_ref,
        params,
        member,
        small_in,
        keep_out,
        send_out,
        small_out,
        grad_stack,
        product,
        value,
        whole,
    ) = refs[-17:]
    join_halves(place, mine, theirs, whole)
    own, other = half_offsets(place)
    mask = mask_ref[0]
    count = count_of(mask)
    gain, bias = params[:, 0:1], params[:, 1:2]
    columns = columns_of(stats_first[0])
    mean, factor = columns[:, 0:1], columns[:, 1:2]

    def normed_of(span):
        return (whole[:, span].astype(WIDE) - mean) * factor

    plain, weighted = conv_back(
        place,
        grads,
        weight,
        grad_stack,
        product,
        value,
        lambda normed: silu_slope(normed * gain + bias),
        mask,
        normed_of,
    )
    normed = normed_of(slice(None))
    sums = group_sums(member[...], lane_pair(gain * plain, gain * weighted))
    first_sum, second_sum = sums[:, 0:1] / count, sums[:, 1:2] / count
    value[...] = residual_grad[0].astype(WIDE) + factor * (
        value[...] * gain - mask * (first_sum + normed * second_sum)
    )
    keep_out[0] = value[pl.ds(own, HALF), :]
    send_out[0] = value[pl.ds(other, HALF), :].astype(LOW)
    rows = small_rows((weighted, plain))
    if len(small_in) == 0:
        small_out[...] = rows
    else:
        earlier, second, third, steps = small_in
        for ref in earlier:
            rows = rows + ref[...]
        images = second.shape[0]
        second_sum, third_sum = second[0], third[0]
        for image in range(1, images):
            second_sum, third_sum = second_sum + second[image], third_sum + third[image]
        small_out[:8, :] = set_rows(
            [
                rows[0:1],
                second_sum[0:1],
                third_sum[0:1],
                rows[1:2],
                second_sum[1:2],
                third_sum[1:2],
            ],
            8,
        )
        small_out[8:, :] = set_rows(
            [second[image, 2 + kind : 3 + kind] for kind in range(2) for image in range(images)]
            + [steps[0:1]],
            8,
        )


def cut_kernel(place, own, one, two, three, mine_out, side_out, far_out, corner_out):
    total = own[...] + one[...].astype(WIDE) + two[...].astype(WIDE) + three[...].astype(WIDE)
    left = place[BLOCKS] == 0
    outs = ((mine_out, side_out), (far_out, corner_out))
    for part in range(2):
        rows = jnp.concatenate(
            [total[tap * PAIR + part * ROWS : tap * PAIR + (part + 1) * ROWS] for tap in range(3)],
            axis=0,
        )
        halves = [rows[:, : 3 * HALF], rows[:, 3 * HALF :]]
        here, away = outs[part]
        here[...] = jnp.where(left, halves[0], halves[1]).astype(here.dtype)
        away[...] = jnp.where(left, halves[1], halves[0]).astype(away.dtype)


def unpack(rows, columns):
    return jnp.concatenate(
        [rows[:, third * columns : (third + 1) * columns] for third in range(3)], axis=0
    )


def pack(rows):
    count = rows.shape[0] // 3
    return jnp.concatenate(
        [rows[third * count : (third + 1) * count] for third in range(3)], axis=1
    )


def cut_columns_kernel(place, own, one, two, three, mine_out, side_out):
    total = own[...] + one[...].astype(WIDE) + two[...].astype(WIDE) + three[...].astype(WIDE)
    left = place[BLOCKS] == 0
    wide, output = total[: PIECE + PAIR], unpack(total[PIECE + PAIR :], C)
    halves = [
        jnp.concatenate(
            [
                wide[:, half * 3 * HALF : (half + 1) * 3 * HALF],
                pack(output[:, half * HALF : (half + 1) * HALF]),
            ],
            axis=0,
        )
        for half in range(2)
    ]
    mine_out[...] = jnp.where(left, halves[0], halves[1])
    side_out[...] = jnp.where(left, halves[1], halves[0]).astype(LOW)


def cut_rows_kernel(place, own, received, near_out, far_out):
    total = own[...] + received[...].astype(WIDE)
    output = unpack(total[PIECE + PAIR :], HALF)
    for part, out in enumerate((near_out, far_out)):
        rows = [
            total[tap * PAIR + part * ROWS : tap * PAIR + (part + 1) * ROWS] for tap in range(4)
        ]
        rows.append(pack(output[part * ROWS : (part + 1) * ROWS]))
        out[...] = jnp.concatenate(rows, axis=0).astype(out.dtype)


def finish_kernel(place, own, received, filter_out, *mixed_outs):
    total = own[...]
    for ref in received:
        total = total + ref[...].astype(WIDE)
    for down in range(3):
        for across in range(3):
            filter_out[3 * down + across] = total[
                across * ROWS : (across + 1) * ROWS, down * HALF : (down + 1) * HALF
            ]
    if mixed_outs:
        mixed_outs[0][...] = total[3 * ROWS : 4 * ROWS]
        mixed_outs[1][...] = unpack(total[4 * ROWS :], HALF)


def receive_kernel(place, carried, received, out):
    for image, ref in enumerate(received):

        @pl.when(pl.program_id(0) == image)
        def _(ref=ref):
            out[...] = ref[...].astype(out.dtype)


def shape(*sizes, dtype=WIDE):
    return jax.ShapeDtypeStruct(sizes, dtype)


def per_image(*sizes, first=0):
    return pl.BlockSpec((1,) + sizes, lambda g, place: (first + g,) + (0,) * len(sizes))


def own_image(*sizes, first=0):
    return pl.BlockSpec(
        (1,) + sizes, lambda g, place: (place[BLOCKS + 1] + first + g,) + (0,) * len(sizes)
    )


def other_image(*sizes):
    return pl.BlockSpec(
        (1,) + sizes, lambda g, place: (place[BLOCKS + 2] + g,) + (0,) * len(sizes)
    )


def per_columns(*sizes, first=0):
    return pl.BlockSpec(sizes, lambda g, place: (0, first + g))


def fixed(*sizes):
    return pl.BlockSpec(sizes, lambda g, place: (0,) * len(sizes))


def whole_array(entry):
    return fixed(*entry.shape)


def run(kernel, place, images, ins, outs, scratch, aliases=None, room=24, cost=8):
    arrays, structure = jax.tree.flatten([array for array, _ in ins])
    specs = jax.tree.leaves(
        [spec for _, spec in ins], is_leaf=lambda entry: isinstance(entry, pl.BlockSpec)
    )

    def body(place, *refs):
        given = jax.tree.unflatten(structure, refs[: len(arrays)])
        kernel(place, *given, *refs[len(arrays) :])

    return pl.pallas_call(
        body,
        grid_spec=pltpu.PrefetchScalarGridSpec(
            num_scalar_prefetch=1,
            grid=(images,),
            in_specs=specs,
            out_specs=[spec for _, spec in outs],
            scratch_shapes=scratch,
        ),
        out_shape=[out for out, _ in outs],
        input_output_aliases=aliases or {},
        compiler_params=pltpu.CompilerParams(
            dimension_semantics=("arbitrary",), vmem_limit_bytes=room * 2**20
        ),
        cost_estimate=pl.CostEstimate(flops=cost * 10**9, bytes_accessed=2**20, transcendentals=0),
    )(place, *arrays)


def filter_gradient(place, inputs, grads, mixed):
    scratch = [
        pltpu.VMEM((TAPS, grads[0].shape[0] * PIX), LOW),
        pltpu.VMEM((TAPS // 2, grads[0].shape[0] * PIX), LOW),
    ]
    partial = shape(TAPS // 2, TAPS)
    ins = (grads[0], inputs[0])
    (partial,) = run(
        one_core_kernel,
        place,
        1,
        [(entry, jax.tree.map(whole_array, entry)) for entry in ins],
        [(partial, whole_array(partial))],
        scratch,
        room=24,
    )
    ins = (grads[1], inputs[1], partial, mixed)
    outs = [shape(JOINT, TAPS)] + [shape(JOINT, TAPS, dtype=LOW)] * 3
    return run(
        both_cores_kernel,
        place,
        1,
        [(entry, jax.tree.map(whole_array, entry)) for entry in ins],
        [(out, whole_array(out)) for out in outs],
        scratch,
        room=32,
    )


def own_filter_gradient(place, stacks, grads):
    ins = (grads, stacks)
    outs = [shape(TAPS // 2, TAPS, dtype=LOW), shape(TAPS // 2, TAPS)]
    return run(
        own_filter_kernel,
        place,
        1,
        [(entry, jax.tree.map(whole_array, entry)) for entry in ins],
        [(out, whole_array(out)) for out in outs],
        [pltpu.VMEM((TAPS, grads.shape[0] * PIX), LOW)],
        room=32,
        cost=1,
    )


def simple(kernel, place, ins, outs, cost):
    return run(
        kernel,
        place,
        1,
        [(entry, jax.tree.map(whole_array, entry)) for entry in ins],
        [(out, whole_array(out)) for out in outs],
        [],
        cost=cost,
    )


def on_device(
    dp,
    features,
    pixel_masks,
    timesteps,
    first_filter,
    second_filter,
    project_weight,
    output_weight,
    embed_weight,
    norm_gains,
    norm_biases,
    cotangent,
):
    chan = lax.axis_index("chan")
    left = chan == 0
    span = dp // BLOCKS
    groups = [list(range(k * span, (k + 1) * span)) for k in range(BLOCKS)]
    block = lax.axis_index("dp") // span
    images = features.shape[0] // 2

    def swap(value, mask, flip):
        pairs = [
            (2 * d + x, 2 * (d ^ (mask * span)) + (x ^ flip)) for d in range(dp) for x in range(2)
        ]
        return lax.ppermute(value, ("dp", "chan"), pairs)

    def near(value, axis):
        if span == 1:
            return value
        return lax.all_gather(value, "dp", axis=axis, tiled=True, axis_index_groups=groups)

    def halves(mine, theirs, axis):
        return jnp.concatenate(
            [jnp.where(left, mine, theirs), jnp.where(left, theirs, mine)], axis=axis
        )

    def after(value, *others):
        return lax.optimization_barrier((value, others))[0]

    def pair_up(one, two):
        taps = one.shape[0] // ROWS
        columns = one.shape[1]
        both = [v.reshape(taps, ROWS, columns) for v in (one, two)]
        return jnp.stack(both, axis=1).reshape(2 * taps * ROWS, columns)

    def gather_one(shard, extra=None):
        side = swap(shard if extra is None else jnp.concatenate([shard, extra], axis=0), 0, 1)
        far = swap(shard, 8, 0)
        both = swap(shard, 8, 1)
        count = shard.shape[0]
        rows = pair_up(halves(shard, side[:count], 1), halves(far, both, 1))
        return rows if extra is None else (rows, side[count:])

    def gather_slow(shard, late):
        rows = after(pair_up(shard, swap(shard, 8, 0)), late)
        return rows, swap(rows, 0, 1)

    def gather_two(rows):
        return [rows, swap(rows, 4, 0), swap(rows, 2, 0), swap(rows, 6, 0)]

    def gather_three(pieces):
        return [swap(rows, 1, 0) for rows in pieces]

    def scatter_one(send, keep):
        outs = [shape(PIECE, TAPS)] + [shape(PIECE, TAPS, dtype=LOW)] * 3
        return simple(split_kernel, place, [keep, swap(send, 1, 0)], outs, 1)

    def scatter_two(keep, *sends):
        arrived = [swap(send, mask, 0) for send, mask in zip(sends, (4, 2, 6))]
        outs = [shape(3 * ROWS, 3 * HALF)] + [shape(3 * ROWS, 3 * HALF, dtype=LOW)] * 3
        return simple(cut_kernel, place, [keep] + arrived, outs, 30)

    def scatter_three(keep, *sends):
        arrived = [
            swap(send, mask, flip) for send, (mask, flip) in zip(sends, ((0, 1), (8, 0), (8, 1)))
        ]
        return simple(finish_kernel, place, [keep, arrived], [shape(9, ROWS, HALF)], 1)[0]

    def joint_two(keep, *sends, late):
        arrived = [swap(send, mask, 0) for send, mask in zip(sends, (4, 2, 6))]
        outs = [shape(JOINT, 3 * HALF), shape(JOINT, 3 * HALF, dtype=LOW)]
        return simple(cut_columns_kernel, place, [after(keep, late)] + arrived, outs, 30)

    def joint_three(keep, send, late):
        outs = [shape(JOINT // 2, 3 * HALF), shape(JOINT // 2, 3 * HALF, dtype=LOW)]
        ins = [after(keep, late), swap(send, 0, 1)]
        return simple(cut_rows_kernel, place, ins, outs, 1)

    def joint_four(keep, send, late):
        outs = [shape(9, ROWS, HALF), shape(ROWS, 3 * HALF), shape(ROWS, HALF)]
        ins = [after(keep, late), [swap(send, 8, 0)]]
        return simple(finish_kernel, place, ins, outs, 1)

    def share(value, dimension):
        if span == 1:
            return value
        return lax.psum_scatter(
            value, "dp", scatter_dimension=dimension, tiled=True, axis_index_groups=groups
        )

    def parts_of(value):
        high = value.astype(LOW)
        rest = value - high.astype(WIDE)
        middle = rest.astype(LOW)
        return [high, middle, (rest - middle.astype(WIDE)).astype(LOW)]

    own_start, other_start = chan * images, (1 - chan) * images

    def others(value):
        return lax.dynamic_slice_in_dim(value, other_start, images, 0)

    theirs = swap(others(features), 0, 1)

    def filter_rows(weight):
        rows = near(weight.astype(LOW), 1).reshape(3, 3, ROWS, HALF)
        return jnp.transpose(rows, (1, 2, 0, 3)).reshape(3 * ROWS, 3 * HALF)

    norms = jnp.concatenate([norm_gains, norm_biases], axis=0)
    norm_rows = jnp.pad(jnp.concatenate(parts_of(norms), axis=1), ((0, 2), (0, 0)))
    first_one, norm_rows = gather_one(filter_rows(first_filter), norm_rows)
    their_norms = norm_rows[:6].astype(WIDE).reshape(6, 3, HALF)
    their_norms = their_norms[:, 0] + their_norms[:, 1] + their_norms[:, 2]
    norms = halves(norms, their_norms, 1)
    params = jnp.stack([norms[0], norms[3], norms[1], norms[4], norms[2], norms[5]], axis=1)
    params = jnp.pad(params, ((0, 0), (0, 2)))
    first_pieces = gather_two(first_one)

    embed_rows = jnp.transpose(near(embed_weight.astype(LOW), 1), (1, 0, 2))
    embed_rows = jnp.transpose(embed_rows.reshape(PAIR, 3, 128), (1, 0, 2))
    embed_rows = embed_rows.reshape(2, 3 * ROWS, 128)
    bundle_rows = jnp.concatenate(
        [
            near(project_weight.astype(LOW), 0).reshape(ROWS, 3 * HALF),
            near(output_weight.astype(LOW), 1).T,
        ],
        axis=1,
    )
    bundle_rows = jnp.transpose(bundle_rows.reshape(ROWS, 3, PACKED), (1, 0, 2))
    second_rows = jnp.concatenate(
        [
            filter_rows(second_filter),
            embed_rows[0],
            embed_rows[1],
            bundle_rows.reshape(3 * ROWS, PACKED),
        ],
        axis=1,
    )
    second_one = gather_slow(second_rows, first_one)
    validity = lax.dynamic_slice_in_dim(pixel_masks, own_start, images, 0).astype(WIDE)
    validity = validity.reshape(images, 1, PIX)
    member = (jnp.arange(C)[:, None] // WIDTH == jnp.arange(C)[None, :] // WIDTH).astype(LOW)
    order = jnp.array(ORDER, jnp.int32)
    place = jnp.concatenate(
        [
            jnp.bitwise_xor(block, order) * ROWS,
            jnp.stack([chan, own_start, other_start]).astype(jnp.int32),
        ]
    )

    def time_features(steps, index, embed_width):
        half_width = embed_width // 2
        power = jnp.where(index < half_width, index, index - half_width).astype(WIDE)
        frequency = jnp.exp(-math.log(10000.0) * power / half_width)
        angles = steps[:, None] * frequency[None, :]
        return jax.nn.silu(
            jnp.where(index[None, :] < half_width, jnp.cos(angles), jnp.sin(angles))
        )

    embed_width = embed_weight.shape[1] * dp
    own_steps = lax.dynamic_slice_in_dim(timesteps, own_start, images, 0).astype(WIDE)
    flat = jnp.arange(2 * 3 * ROWS)
    third, entry_row = flat // PAIR, flat % PAIR
    embed_index = (jnp.bitwise_xor(block, order)[:, None] * PAIR + entry_row).reshape(-1)
    embed_values = time_features(after(own_steps, first_one), embed_index, embed_width)
    embed_split = jnp.stack(parts_of(embed_values), axis=2)
    embed_split = embed_split.reshape(images, PAIRS, 2, 2, 3, ROWS, 3)
    embed_split = jnp.transpose(embed_split, (0, 3, 1, 4, 2, 5, 6))
    late = (third.reshape(2, 3, ROWS) == jnp.array([1, 2])[:, None, None])
    late = late[None, :, None, :, None, :, None]
    embed_parts = jnp.concatenate(
        [jnp.where(late, 0, embed_split), jnp.where(late, embed_split, 0)], axis=6
    ).reshape(images, 2, TAPS, 6)
    embed_parts = jnp.concatenate([embed_parts[image] for image in range(images)], axis=2)
    embed_parts = jnp.pad(embed_parts, ((0, 0), (0, 0), (0, 128 - 6 * images)))
    steps_row = jnp.pad(own_steps, (0, HALF - images))
    steps_row = jnp.pad(jnp.concatenate([steps_row, steps_row])[None, :], ((0, 7), (0, 0)))

    value_scratch = pltpu.VMEM((C, PIX), WIDE)
    product_scratch = pltpu.VMEM((TAPS, PIX), WIDE)
    back_scratch = [pltpu.VMEM((TAPS, PIX), LOW), product_scratch, value_scratch]
    mask_in = (validity, per_image(1, PIX))
    params_in = (params, fixed(C, 8))
    member_in = (member, fixed(C, C))
    image_low = (shape(images, C, PIX, dtype=LOW), per_image(C, PIX))
    image_wide = (shape(images, C, PIX), per_image(C, PIX))
    image_rows = (shape(images, 8, C), per_image(8, C))
    weight_out = (shape(TAPS, TAPS, dtype=LOW), fixed(TAPS, TAPS))
    stack_out = (shape(TAPS // 2, images * PIX, dtype=LOW), per_columns(TAPS // 2, PIX))
    input_out = (shape(C // 2, images * PIX, dtype=LOW), per_columns(C // 2, PIX))
    anywhere = pl.BlockSpec(memory_space=pl.ANY)

    prepared = run(
        prepare_kernel,
        place,
        images,
        [
            (features, own_image(HALF, PIX)),
            (theirs, per_image(HALF, PIX)),
            mask_in,
            params_in,
            member_in,
        ],
        [stack_out, stack_out, image_rows],
        [value_scratch],
    )
    first_low, first_high, stats_whole = prepared
    cots = others(after(cotangent, first_one))
    first_pieces = first_pieces + gather_three(after(first_pieces, first_low))
    mine, side = after(second_one, first_low)
    second_one = halves(mine[:, :SECOND], side[:, :SECOND], 1)
    bundle_one = halves(mine[:, SECOND:], side[:, SECOND:], 1)
    second_normed, stats_first, first_weight = run(
        first_kernel,
        place,
        images,
        [
            mask_in,
            member_in,
            (first_pieces, [fixed(PIECE, TAPS)] * 8),
            (after([first_low, first_high], second_one, cots, embed_parts, steps_row), [per_columns(TAPS // 2, PIX)] * 2),
        ],
        [image_wide, image_rows, weight_out],
        [value_scratch, product_scratch],
    )
    second_pieces = gather_two(second_one)
    second_pieces = second_pieces + gather_three(after(second_pieces, second_normed))
    bundle_pieces = gather_two(bundle_one)
    their_cots = swap(after(cots, first_low), 0, 1)
    second_low, second_high, residual, stats_second = run(
        second_kernel,
        place,
        images,
        [
            (after(second_normed, bundle_one), per_image(C, PIX)),
            (stats_first, per_image(8, C)),
            (features, own_image(HALF, PIX)),
            (theirs, per_image(HALF, PIX)),
            (embed_parts, fixed(2, TAPS, 128)),
            mask_in,
            params_in,
            member_in,
            (second_pieces, [fixed(PIECE, 2 * SECOND)] * 8),
        ],
        [input_out, input_out, image_wide, image_rows],
        [
            pltpu.VMEM((TAPS, TAPS), LOW),
            pltpu.VMEM((2, 2, TAPS, 128), LOW),
            pltpu.VMEM((2, 2, 128, 128), WIDE),
            value_scratch,
            pltpu.VMEM((TAPS, PIX), LOW),
            product_scratch,
        ],
        room=60,
    )
    bundle_pieces = bundle_pieces + gather_three(after(bundle_pieces, residual))
    second_theirs = swap(second_high, 1, 0)
    mixed_rows = PAIRS // 2 * (JOINT - PIECE)
    block_keep, block_send, second_grad, *mixed, small_third = run(
        attend_kernel,
        place,
        images,
        [
            (residual, per_image(C, PIX)),
            (stats_second, per_image(8, C)),
            (cotangent, own_image(HALF, PIX)),
            (their_cots, per_image(HALF, PIX)),
            mask_in,
            params_in,
            member_in,
            (bundle_pieces, [fixed(PIECE, 2 * PACKED)] * 8),
        ],
        [
            (shape(2 * images, HALF, PIX, dtype=LOW), own_image(HALF, PIX)),
            (shape(images, HALF, PIX, dtype=LOW), per_image(HALF, PIX)),
            image_low,
            (shape(mixed_rows, TAPS), fixed(mixed_rows, TAPS)),
            (shape(mixed_rows, TAPS, dtype=LOW), fixed(mixed_rows, TAPS)),
            image_rows,
        ],
        [
            pltpu.VMEM((2, C, 2 * C), WIDE),
            pltpu.VMEM((C, PIX), LOW),
            pltpu.VMEM((C, TAPS), LOW),
            pltpu.VMEM((C, C), LOW),
            pltpu.VMEM((C, PIX), LOW),
            pltpu.VMEM((TAPS, PIX), LOW),
            pltpu.VMEM((C, PIX), LOW),
            pltpu.VMEM((C, PIX), LOW),
            pltpu.VMEM((TAPS, PIX), LOW),
            pltpu.VMEM((PIX, KEYS), LOW),
            pltpu.VMEM((PIX, KEYS), LOW),
            pltpu.VMEM((HEAD + 16, PIX), LOW),
            pltpu.VMEM((KEYS, PIX), LOW),
            pltpu.VMEM((KEYS, PIX), LOW),
            pltpu.VMEM((PIX, PIX), WIDE),
            pltpu.VMEM((PIX, PIX), LOW),
            pltpu.VMEM((PIX, PIX), LOW),
            pltpu.VMEM((C, TAPS + C), WIDE),
            value_scratch,
        ],
        room=62,
        cost=60,
    )
    block_theirs = swap(block_send, 0, 1)
    mixed = [mixed[0], swap(mixed[1], 1, 0)]
    grads_theirs = swap(second_grad, 1, 0)
    joint = filter_gradient(
        place, [second_low, second_theirs], [second_grad, grads_theirs], mixed
    )
    first_grad, small_second = run(
        second_back_kernel,
        place,
        images,
        [
            (after(second_grad, joint), per_image(C, PIX)),
            (second_pieces, [fixed(PIECE, 2 * SECOND)] * 8),
            (second_normed, per_image(C, PIX)),
            (stats_second, per_image(8, C)),
            mask_in,
            params_in,
            member_in,
        ],
        [image_low, image_rows],
        [pltpu.VMEM((TAPS, TAPS), LOW)] + back_scratch,
        room=32,
    )
    masked_out = lax.dynamic_update_slice_in_dim(
        after(block_keep, joint), block_theirs, other_start, 0
    )
    send, keep = own_filter_gradient(
        place, [first_low, first_high], after(first_grad, masked_out)
    )
    first_part = scatter_one(send, keep)
    joint = joint_two(*joint, late=send)
    input_grad, input_theirs, smalls = None, [], []
    back_grad = after(first_grad, first_part, joint)
    for image in range(images):
        last = image == images - 1
        small_in = (smalls, small_second, small_third, steps_row) if last else ()
        carried = [] if input_grad is None else [(input_grad, anywhere)]
        small_shape = shape(16 if last else 8, C)
        input_grad, input_send, small = run(
            first_back_kernel,
            place,
            1,
            carried
            + [
                (back_grad, per_image(C, PIX, first=image)),
                (first_weight, fixed(TAPS, TAPS)),
                (features, own_image(HALF, PIX, first=image)),
                (theirs, per_image(HALF, PIX, first=image)),
                (stats_whole, per_image(8, C, first=image)),
                (second_grad, per_image(C, PIX, first=image)),
                (validity, per_image(1, PIX, first=image)),
                params_in,
                member_in,
                (small_in, jax.tree.map(whole_array, small_in)),
            ],
            [
                (shape(2 * images, HALF, PIX), own_image(HALF, PIX, first=image)),
                (shape(1, HALF, PIX, dtype=LOW), per_image(HALF, PIX)),
                (small_shape, whole_array(small_shape)),
            ],
            back_scratch + [pltpu.VMEM((C, PIX), LOW)],
            {1: 0} if carried else None,
        )
        smalls.append(small)
        input_theirs.append(swap(input_send, 0, 1))
        if image == 0:
            joint = joint_three(*joint, late=small)
            back_grad = after(back_grad, joint)
    first_part = scatter_two(*first_part)
    message = after(smalls[-1], input_theirs[:-1])

    def merge(arrived):
        total = sum(message[:8] for message in arrived)
        return jnp.concatenate([total] + [message[8:] for message in arrived], axis=0)

    message = after(merge([message, swap(message, 1, 0)]), first_part)
    joint = joint_four(*joint, late=first_part)
    grad_first = share(scatter_three(*first_part), 1)
    grad_second = share(joint[0], 1)
    grad_project = share(joint[1].reshape(ROWS, 3, HALF), 0)
    grad_output = share(joint[2].T, 1)
    (input_grad,) = run(
        receive_kernel,
        place,
        images,
        [(input_grad, anywhere), (input_theirs, [fixed(1, HALF, PIX)] * images)],
        [(shape(2 * images, HALF, PIX), other_image(HALF, PIX))],
        [],
        {1: 0},
        cost=1,
    )

    message = merge([message, swap(message, 4, 0)])
    message = merge([message, swap(message, 2, 0)])
    one, two = after(message[:, :HALF], input_theirs[-1]), message[:, HALF:]
    own, away = jnp.where(left, one, two), jnp.where(left, two, one)
    message = merge([own, swap(away, 0, 1), swap(own, 8, 0), swap(away, 8, 1)])
    total, entries = message[:6], message[8:]
    if span > 1:
        total = lax.psum(total, "dp", axis_index_groups=groups)
        entries = lax.all_gather(entries, "dp", axis=0, tiled=True, axis_index_groups=groups)
    entries = entries.reshape(-1, 8, HALF)
    all_steps = entries[:, 2 * images, :images].reshape(-1)
    scale_grads = entries[:, :images].reshape(-1, HALF)
    shift_grads = entries[:, images : 2 * images].reshape(-1, HALF)
    rows = embed_weight.shape[1]
    row_index = lax.axis_index("dp") * rows + jnp.arange(rows)
    all_embed = time_features(all_steps, row_index, embed_width)
    grad_embed = jnp.einsum(
        "be,kbd->ked",
        all_embed,
        jnp.stack([scale_grads, shift_grads]),
        precision=lax.Precision.HIGHEST,
    )
    return (
        masked_out,
        input_grad,
        grad_first,
        grad_second,
        grad_project,
        grad_output,
        grad_embed,
        total[:3],
        total[3:],
    )


def solution(mesh):
    in_specs = (
        P("dp", "chan", None),
        P("dp", None),
        P("dp"),
        P(None, "dp", "chan"),
        P(None, "dp", "chan"),
        P("dp", None, "chan"),
        P("chan", "dp"),
        P(None, "dp", "chan"),
        P(None, "chan"),
        P(None, "chan"),
        P("dp", "chan", None),
    )
    out_specs = (
        P("dp", "chan", None),
        P("dp", "chan", None),
        P(None, "dp", "chan"),
        P(None, "dp", "chan"),
        P("dp", None, "chan"),
        P("chan", "dp"),
        P(None, "dp", "chan"),
        P(None, "chan"),
        P(None, "chan"),
    )
    return jax.shard_map(
        functools.partial(on_device, mesh.shape["dp"]),
        mesh=mesh,
        in_specs=in_specs,
        out_specs=out_specs,
        check_vma=False,
    )
```
